32 devices in a mesh: prow: 8 (over z, x), pcol: 2 (over y), zgrid: 2 (over core).
Axes of the slice: x: 2, y: 2, z: 4, core: 2. Of those that a mesh axis runs over, the one named last changes fastest.
Arguments:
- blocks: bfloat16 [8, 2, 2, 3, 40, 128, 128], P('prow', 'pcol', 'zgrid'), may hold values from -0.078125 to 0.078125
- sources: int32 [8, 2, 2, 3, 40], P('prow', 'pcol', 'zgrid'), may hold values from 0 to 1, as said below
- targets: int32 [8, 2, 2, 3, 40], P('prow', 'pcol', 'zgrid'), may hold values from 0 to 23, as said below
- counts: int32 [8, 2, 2, 3], P('prow', 'pcol', 'zgrid'), may hold values from 1 to 40, as said below
- given_sub: bfloat16 [8, 2, 2, 2, 128, 128], P('prow', 'pcol', 'zgrid'), may hold values from -6 to 6
- given_top: bfloat16 [8, 2, 2, 128, 128], P('prow', 'pcol'), may hold values from -6 to 6
- inverse_sub: bfloat16 [8, 2, 2, 2, 128, 128], P('prow', 'pcol', 'zgrid'), as said below
- inverse_top: bfloat16 [8, 2, 2, 128, 128], P('prow', 'pcol'), as said below
Outputs:
- solved_sub: bfloat16 [8, 2, 2, 2, 128, 128], P('prow', 'pcol', 'zgrid')
- solved_top: bfloat16 [8, 2, 2, 128, 128], P('prow', 'pcol')
The draws below stay inside these ranges and needn't reach their ends.
Inputs may be any that keep to these rules, and one draw needn't show every extreme that they name: `sources`: column of the source supernode of a slot. `targets`: a slot of source level l aims at a level t = value // 8 + 1 above l and the row value % 8. `counts`: on some device of each source level all 40 slots are live. `inverse_sub`: unit lower triangular. `inverse_top`: unit lower triangular.
All inputs are finite; a program needn't handle non-finite values.
Results may differ from the reference program's by a relative error of at most 0.023.
Values may be sent and summed in bfloat16 or wider, within the bound.
No kernel may reach another device: no remote copies, remote signals or barrier semaphores. Data moves between devices by JAX's collectives and lax.ppermute only.
A program may use at most 64 MiB of HBM per device.

```python
import math
import jax
import jax.numpy as jnp
from jax import lax

WIDTH = 128
SIDES = 128
CAP = 40
ROWS = 8
COLS = 2
LAYERS = 2


def draw_sources(key, part):
    return jax.random.randint(jax.random.fold_in(key, 101), (ROWS, COLS, LAYERS, 3, CAP), 0, COLS).astype(jnp.int32)


def draw_targets(key, part):
    first_key = jax.random.fold_in(key, 202)
    second_key = jax.random.fold_in(key, 203)
    shape_all = (ROWS, COLS, LAYERS, 3, CAP)
    lowest = jnp.arange(3, dtype=jnp.int32)[None, None, None, :, None] + 1
    level_pick = jax.random.randint(first_key, shape_all, lowest, 4)
    row_pick = jax.random.randint(second_key, shape_all, 0, ROWS)
    return ((level_pick - 1) * ROWS + row_pick).astype(jnp.int32)


def draw_counts(key, part):
    first_key = jax.random.fold_in(key, 301)
    second_key = jax.random.fold_in(key, 302)
    third_key = jax.random.fold_in(key, 303)
    devices_all = ROWS * COLS * LAYERS
    first_pick = jax.random.randint(first_key, (devices_all, 3), 1, CAP + 1)
    second_pick = jax.random.randint(second_key, (devices_all, 3), 1, CAP + 1)
    smaller = jnp.minimum(first_pick, second_pick)
    spots = jax.random.randint(third_key, (3,), 0, devices_all)
    smaller = smaller.at[spots, jnp.arange(3)].set(CAP)
    return smaller.reshape(ROWS, COLS, LAYERS, 3).astype(jnp.int32)


def unit_lower(key, shape_all):
    normal_part = jax.random.normal(key, shape_all, jnp.float32)
    lower_part = jnp.tril(normal_part, -1) * (0.5 / math.sqrt(WIDTH)) + jnp.eye(WIDTH, dtype=jnp.float32)
    return lower_part.astype(jnp.bfloat16)


def draw_inverse_sub(key, part):
    return unit_lower(jax.random.fold_in(key, 401), (ROWS, COLS, LAYERS, 2, WIDTH, WIDTH))


def draw_inverse_top(key, part):
    return unit_lower(jax.random.fold_in(key, 402), (ROWS, COLS, 2, WIDTH, WIDTH))


def level_of(own_key, shape, shards, smallest, high):
    loudness = 1.0
    for position, blocks in shards:
        heights = jax.random.uniform(jax.random.fold_in(jax.random.fold_in(own_key, 6), position), (blocks,), jnp.float32, smallest / len(shards), high / len(shards))
        loudness = loudness * jnp.repeat(jnp.exp(heights), shape[position] // blocks).reshape((-1,) + (1,) * (len(shape) - 1 - position))
    return loudness


def centred(stream_key, extent, spread, most, split=(), kind=jnp.bfloat16):
    array = spread * jax.random.normal(stream_key, extent, jnp.float32)
    if split:
        array = array * level_of(stream_key, extent, split, -0.22, 0.18)
    return jnp.clip(array, -most, most).astype(kind)


def setup_inputs(seed: int = 0) -> dict:
    key_of = jax.random.split(jax.random.key(seed), 9)
    return {
        "blocks": centred(key_of[0], (ROWS, COLS, LAYERS, 3, CAP, WIDTH, WIDTH), (WIDTH * CAP) ** -0.5, 0.078125, ((0, 8), (1, 2), (2, 2))),
        "sources": draw_sources(jax.random.fold_in(key_of[8], 71), 0),
        "targets": draw_targets(jax.random.fold_in(key_of[8], 71), 0),
        "counts": draw_counts(jax.random.fold_in(key_of[8], 71), 0),
        "given_sub": centred(key_of[4], (ROWS, COLS, LAYERS, 2, WIDTH, SIDES), 1.0, 6.0, ((0, 8), (1, 2), (2, 2))),
        "given_top": centred(key_of[5], (ROWS, COLS, 2, WIDTH, SIDES), 1.0, 6.0, ((0, 8), (1, 2))),
        "inverse_sub": draw_inverse_sub(jax.random.fold_in(key_of[8], 71), 0),
        "inverse_top": draw_inverse_top(jax.random.fold_in(key_of[8], 71), 0),
    }


def solve_block(inverse, residual):
    return jnp.einsum("...wk,...kr->...wr", inverse.astype(jnp.float32), residual.astype(jnp.float32)).astype(jnp.bfloat16)


def incoming_sums(target_level, blocks, sources, targets, counts, sub_now, top_now):
    row_count = blocks.shape[0]
    col_count = blocks.shape[1]
    layer_count = blocks.shape[2]
    slot_count = blocks.shape[4]
    width = blocks.shape[5]
    sides = sub_now.shape[-1]
    start_sum = jnp.zeros((col_count, layer_count, row_count, width, sides), jnp.float32)

    def row_step(carry, inputs):
        block_row, source_row, target_row, count_row, sub_row, top_row = inputs
        total = jnp.zeros((col_count, layer_count, row_count, width, sides), jnp.float32)
        layer_ids = jnp.arange(layer_count)[None, :, None]
        for source_level in range(target_level):
            source_part = source_row[:, :, source_level]
            target_part = target_row[:, :, source_level]
            if source_level < 2:
                chosen = sub_row[source_part, layer_ids, source_level]
            else:
                chosen = top_row[source_part]
            product = jnp.einsum("qzswk,qzskr->qzswr", block_row[:, :, source_level].astype(jnp.float32), chosen.astype(jnp.float32))
            alive_mask = (jnp.arange(slot_count)[None, None, :] < count_row[:, :, source_level][:, :, None]) & (target_part // row_count + 1 == target_level)
            one_hot = (((target_part % row_count)[..., None] == jnp.arange(row_count)) & alive_mask[..., None]).astype(jnp.float32)
            total = total + jnp.einsum("qzsp,qzswr->qzpwr", one_hot, product)
        rounded = lax.optimization_barrier(total.astype(jnp.bfloat16)).astype(jnp.float32)
        return carry + rounded, None

    result, unused = lax.scan(row_step, start_sum, (blocks, sources, targets, counts, sub_now, top_now))
    return result


def reference(blocks, sources, targets, counts, given_sub, given_top, inverse_sub, inverse_top):
    level_zero = solve_block(inverse_sub[:, :, :, 0], given_sub[:, :, :, 0])
    sub_now = jnp.stack([level_zero, jnp.zeros_like(level_zero)], axis=3)
    top_now = jnp.zeros(given_top[:, :, 0].shape, jnp.bfloat16)
    arrive_one = jnp.transpose(incoming_sums(1, blocks, sources, targets, counts, sub_now, top_now), (2, 0, 1, 3, 4))
    level_one = solve_block(inverse_sub[:, :, :, 1], (given_sub[:, :, :, 1].astype(jnp.float32) - arrive_one).astype(jnp.bfloat16))
    sub_now = jnp.stack([level_zero, level_one], axis=3)
    arrive_two = jnp.transpose(jnp.sum(incoming_sums(2, blocks, sources, targets, counts, sub_now, top_now), axis=1), (1, 0, 2, 3))
    level_two = solve_block(inverse_top[:, :, 0], (given_top[:, :, 0].astype(jnp.float32) - arrive_two).astype(jnp.bfloat16))
    arrive_three = jnp.transpose(jnp.sum(incoming_sums(3, blocks, sources, targets, counts, sub_now, level_two), axis=1), (1, 0, 2, 3))
    level_three = solve_block(inverse_top[:, :, 1], (given_top[:, :, 1].astype(jnp.float32) - arrive_three).astype(jnp.bfloat16))
    return sub_now, jnp.stack([level_two, level_three], axis=2)
```

```python
import jax
import jax.numpy as jnp
from jax import lax
from jax.sharding import PartitionSpec as P

slot_group = 8


def solve_block(inverse, residual):
    return jnp.dot(inverse, residual, preferred_element_type=jnp.float32).astype(jnp.bfloat16)


def spread_updates(totals, solved, block_set, source_ids, target_ids, live_count):
    gathered = lax.all_gather(solved[None], "pcol", axis=0, tiled=True)
    group_count = (live_count + slot_group - 1) // slot_group

    def add_group(position, running):
        first_slot = position * slot_group
        block_piece = lax.dynamic_slice_in_dim(block_set, first_slot, slot_group, 0)
        source_part = lax.dynamic_slice_in_dim(source_ids, first_slot, slot_group, 0)
        target_part = lax.dynamic_slice_in_dim(target_ids, first_slot, slot_group, 0)
        chosen = jnp.take(gathered, source_part, axis=0)
        product = jnp.einsum(
            "swk,skr->swr", block_piece, chosen, preferred_element_type=jnp.float32
        )
        alive_mask = first_slot + jnp.arange(slot_group) < live_count
        product = product * alive_mask.astype(jnp.float32)[:, None, None]
        return running.at[target_part].add(product)

    return lax.fori_loop(0, group_count, add_group, totals)


def reduce_rows(totals, level_index, row_count):
    section = lax.slice_in_dim(
        totals, level_index * row_count, (level_index + 1) * row_count, axis=0
    )
    received = lax.all_to_all(section.astype(jnp.bfloat16), "prow", 0, 0, tiled=True)
    return jnp.sum(received.astype(jnp.float32), axis=0)


def reduce_all(totals, level_index, row_count):
    section = lax.slice_in_dim(
        totals, level_index * row_count, (level_index + 1) * row_count, axis=0
    ).astype(jnp.bfloat16)
    layer_count = lax.axis_size("zgrid")
    copies = jnp.repeat(section, layer_count, axis=0)
    received = lax.all_to_all(copies, ("prow", "zgrid"), 0, 0, tiled=True)
    return jnp.sum(received.astype(jnp.float32), axis=0)


def ancestor_solve(incoming, given, inverse):
    residual = (given.astype(jnp.float32) - incoming).astype(jnp.bfloat16)
    return solve_block(inverse, residual)


def local(blocks, sources, targets, counts, given_sub, given_top, inverse_sub, inverse_top):
    block_set = blocks[0, 0, 0]
    source_ids = sources[0, 0, 0]
    target_ids = targets[0, 0, 0]
    live_counts = counts[0, 0, 0]
    right_sub = given_sub[0, 0, 0]
    right_top = given_top[0, 0]
    factor_sub = inverse_sub[0, 0, 0]
    factor_top = inverse_top[0, 0]
    row_count = lax.axis_size("prow")
    totals = jnp.zeros((3 * row_count,) + right_sub.shape[1:], jnp.float32)
    level_zero = solve_block(factor_sub[0], right_sub[0])
    totals = spread_updates(
        totals, level_zero, block_set[0], source_ids[0], target_ids[0], live_counts[0]
    )
    incoming = reduce_rows(totals, 0, row_count)
    level_one = solve_block(
        factor_sub[1], (right_sub[1].astype(jnp.float32) - incoming).astype(jnp.bfloat16)
    )
    totals = spread_updates(
        totals, level_one, block_set[1], source_ids[1], target_ids[1], live_counts[1]
    )
    level_two = ancestor_solve(reduce_all(totals, 1, row_count), right_top[0], factor_top[0])
    totals = spread_updates(
        totals, level_two, block_set[2], source_ids[2], target_ids[2], live_counts[2]
    )
    level_three = ancestor_solve(reduce_all(totals, 2, row_count), right_top[1], factor_top[1])
    solved_sub = jnp.stack([level_zero, level_one])[None, None, None]
    solved_top = jnp.stack([level_two, level_three])[None, None]
    return (solved_sub, solved_top)


def solution(mesh):
    in_specs = (
        P("prow", "pcol", "zgrid", None, None, None, None),
        P("prow", "pcol", "zgrid", None, None),
        P("prow", "pcol", "zgrid", None, None),
        P("prow", "pcol", "zgrid", None),
        P("prow", "pcol", "zgrid", None, None, None),
        P("prow", "pcol", None, None, None),
        P("prow", "pcol", "zgrid", None, None, None),
        P("prow", "pcol", None, None, None),
    )
    out_specs = (P("prow", "pcol", "zgrid", None, None, None), P("prow", "pcol", None, None, None))
    return jax.shard_map(local, mesh=mesh, in_specs=in_specs, out_specs=out_specs, check_vma=False)
```

```python
import functools

import jax
import jax.numpy as jnp
from jax import lax
from jax.experimental import pallas as pl
from jax.experimental.pallas import tpu as pltpu
from jax.sharding import PartitionSpec as P

slot_group = 8


def shifted_copies(value, layers):
    cols = lax.axis_size("pcol")
    depth = lax.axis_size("zgrid")
    found = []
    for k in range(cols):
        if k == 0 and layers == 0:
            found.append(value)
            continue
        moves = []
        for c in range(cols):
            for z in range(depth):
                target = ((c - k) % cols) * depth + (z - layers) % depth
                moves.append((c * depth + z, target))
        found.append(lax.ppermute(value, ("pcol", "zgrid"), moves))
    return found


def from_other_core(value, shift):
    depth = lax.axis_size("zgrid")
    return lax.ppermute(value, "zgrid", [(z, (z - shift) % depth) for z in range(depth)])


def update_kernel(sets, cols, row_count, lowest_kept, carries, keeps, *refs):
    refs = list(refs)
    set_count = len(sets)
    solution_sets = 1 + max(s[2] for s in sets)
    layer_sets = 1 + max(s[3] for s in sets)
    metas = [[refs.pop(0) for _ in range(4)] for _ in range(layer_sets)]
    solutions = [[refs.pop(0) for _ in range(cols)] for _ in range(solution_sets)]
    total_in = refs.pop(0) if carries else None
    send_ref = refs.pop(0) if keeps[0] else None
    kept_ref = refs.pop(0) if keeps[1] else None
    buffer, wide, product, total, semaphores = refs
    me = lax.axis_index("pcol")
    capacity = buffer.shape[1]
    width = buffer.shape[2]
    groups = capacity // slot_group

    def group_copy(k, g):
        level = sets[k][0]
        blocks = metas[sets[k][3]][3]
        return pltpu.make_async_copy(
            blocks.at[level, pl.ds(g * slot_group, slot_group)],
            buffer.at[k, pl.ds(g * slot_group, slot_group)],
            semaphores.at[k, g],
        )

    for k in range(set_count):
        live = metas[sets[k][3]][2][sets[k][0]]
        for g in range(groups):

            @pl.when(g * slot_group < live)
            def _():
                group_copy(k, g).start()

    if carries:
        total[: total_in.shape[0]] = total_in[...]
    else:
        total[...] = jnp.zeros_like(total)
    spare = total.shape[0] - 1
    for j in range(solution_sets):
        for c in range(cols):
            wide[j, :, c * width : (c + 1) * width] = solutions[j][c][...]

    for k in range(set_count):
        level, lowest, solution_index, layer_index = sets[k]
        sources, targets, counts, _ = metas[layer_index]
        live = counts[level]

        def one_group(g, unused):
            group_copy(k, g).wait()
            first = g * slot_group
            pieces = buffer[k, pl.ds(first, slot_group)].reshape(slot_group * width, width)
            product[...] = jnp.dot(
                pieces, wide[solution_index], preferred_element_type=jnp.float32
            )
            for s in range(slot_group):
                slot = first + s
                aim = targets[level, slot] - lowest_kept * row_count
                used = (slot < live) & (targets[level, slot] >= lowest * row_count)
                place = jnp.where(used, aim, spare)
                column = lax.rem(sources[level, slot] - me + cols, cols)
                total[place] += product[
                    s * width : (s + 1) * width, pl.ds(pl.multiple_of(column * width, width), width)
                ]
            return unused

        lax.fori_loop(0, (live + slot_group - 1) // slot_group, one_group, 0)

    if keeps[0]:
        send_ref[...] = total[:row_count].astype(jnp.bfloat16)
    if keeps[1]:
        first = row_count if keeps[0] else 0
        kept_ref[...] = total[first:spare]


def update(sets, layer_arrays, solution_groups, total_in, row_count, lowest_kept, sends, keeps):
    cols = len(solution_groups[0])
    width, sides = solution_groups[0][0].shape
    capacity = layer_arrays[0][3].shape[1]
    sections = 3 - lowest_kept
    operands = []
    specs = []
    for sources, targets, counts, blocks in layer_arrays:
        operands += [sources, targets, counts, blocks]
        specs += [pl.BlockSpec(memory_space=pltpu.SMEM)] * 3 + [pl.BlockSpec(memory_space=pl.ANY)]
    for group in solution_groups:
        operands += group
        specs += [pl.BlockSpec(memory_space=pltpu.VMEM)] * cols
    if total_in is not None:
        operands.append(total_in)
        specs.append(pl.BlockSpec(memory_space=pltpu.VMEM))
    outs = []
    if sends:
        outs.append(jax.ShapeDtypeStruct((row_count, width, sides), jnp.bfloat16))
    if keeps:
        outs.append(
            jax.ShapeDtypeStruct(((sections - int(sends)) * row_count, width, sides), jnp.float32)
        )
    return pl.pallas_call(
        functools.partial(
            update_kernel, sets, cols, row_count, lowest_kept, total_in is not None, (sends, keeps)
        ),
        out_shape=outs,
        in_specs=specs,
        out_specs=[pl.BlockSpec(memory_space=pltpu.VMEM)] * len(outs),
        scratch_shapes=[
            pltpu.VMEM((len(sets), capacity, width, width), jnp.bfloat16),
            pltpu.VMEM((len(solution_groups), width, cols * sides), jnp.bfloat16),
            pltpu.VMEM((slot_group * width, cols * sides), jnp.float32),
            pltpu.VMEM((sections * row_count + 1, width, sides), jnp.float32),
            pltpu.SemaphoreType.DMA((len(sets), capacity // slot_group)),
        ],
        compiler_params=pltpu.CompilerParams(vmem_limit_bytes=48 * 1024 * 1024),
    )(*operands)


def solve_block(inverse, residual):
    return jnp.dot(inverse, residual, preferred_element_type=jnp.float32).astype(jnp.bfloat16)


def reduced_solve(send, given, inverse):
    received = lax.all_to_all(send, "prow", 0, 0, tiled=True)
    incoming = jnp.sum(received.astype(jnp.float32), axis=0)
    residual = (given.astype(jnp.float32) - incoming).astype(jnp.bfloat16)
    return solve_block(inverse, residual)


def local(blocks, sources, targets, counts, given_sub, given_top, inverse_sub, inverse_top):
    own = (sources[0, 0, 0], targets[0, 0, 0], counts[0, 0, 0], blocks[0, 0, 0])
    right_sub = given_sub[0, 0, 0]
    right_top = given_top[0, 0]
    factor_sub = inverse_sub[0, 0, 0]
    factor_top = inverse_top[0, 0]
    row_count = lax.axis_size("prow")
    depth = lax.axis_size("zgrid")
    others = [tuple(from_other_core(a, m) for a in own) for m in range(1, depth)]

    level_zero = solve_block(factor_sub[0], right_sub[0])
    spread_zero = [shifted_copies(level_zero, m) for m in range(depth)]
    send, total = update(
        [(0, 0, 0, 0)], [own], spread_zero[:1], None, row_count, 0, True, True
    )
    level_one = reduced_solve(send, right_sub[1], factor_sub[1])
    (total,) = update(
        [(0, 1, m, m) for m in range(depth - 1)],
        others, spread_zero[1:], total, row_count, 1, False, True,
    )
    spread_one = [shifted_copies(level_one, m) for m in range(depth)]
    send, total = update(
        [(1, 1, m, m) for m in range(depth)],
        [own] + others, spread_one, total, row_count, 1, True, True,
    )
    level_two = reduced_solve(send, right_top[0], factor_top[0])
    spread_two = shifted_copies(level_two, 0)
    (send,) = update(
        [(2, 2, 0, m) for m in range(depth)],
        [own] + others, [spread_two], total, row_count, 2, True, False,
    )
    level_three = reduced_solve(send, right_top[1], factor_top[1])
    solved_sub = jnp.stack([level_zero, level_one])[None, None, None]
    solved_top = jnp.stack([level_two, level_three])[None, None]
    return (solved_sub, solved_top)


def solution(mesh):
    in_specs = (
        P("prow", "pcol", "zgrid", None, None, None, None),
        P("prow", "pcol", "zgrid", None, None),
        P("prow", "pcol", "zgrid", None, None),
        P("prow", "pcol", "zgrid", None),
        P("prow", "pcol", "zgrid", None, None, None),
        P("prow", "pcol", None, None, None),
        P("prow", "pcol", "zgrid", None, None, None),
        P("prow", "pcol", None, None, None),
    )
    out_specs = (P("prow", "pcol", "zgrid", None, None, None), P("prow", "pcol", None, None, None))
    return jax.shard_map(local, mesh=mesh, in_specs=in_specs, out_specs=out_specs, check_vma=False)
```

```python
import functools

import jax
import jax.numpy as jnp
from jax import lax
from jax.experimental import pallas as pl
from jax.experimental.pallas import tpu as pltpu
from jax.sharding import PartitionSpec as P

slot_group = 8
code_shift = 8


def partner(index, k, size):
    if size & (size - 1) == 0:
        return index ^ k
    return lax.rem(index + k, size) if not isinstance(index, int) else (index + k) % size


def origin(index, k, size):
    if size & (size - 1) == 0:
        return index ^ k
    return (index - k) % size


def sibling_values(value, layers):
    cols = lax.axis_size("pcol")
    depth = lax.axis_size("zgrid")
    found = []
    for k in range(cols):
        if k == 0 and layers == 0:
            found.append(value)
            continue
        moves = []
        for c in range(cols):
            for z in range(depth):
                target = ((c - k) % cols) * depth + (z - layers) % depth
                moves.append((c * depth + z, target))
        found.append(lax.ppermute(value, ("pcol", "zgrid"), moves))
    return found


def from_other_core(value, shift):
    depth = lax.axis_size("zgrid")
    return lax.ppermute(value, "zgrid", [(z, (z - shift) % depth) for z in range(depth)])


def update_kernel(config, *refs):
    sets, cols, row_count, lowest_kept, layer_count, carries, sends, keeps, staged = config
    refs = list(refs)
    solution_sets = 1 + max(s[2] for s in sets)
    codes = [refs.pop(0) for _ in range(layer_count)]
    blocks = [refs.pop(0) for _ in range(layer_count)]
    solutions = [refs.pop(0) for _ in range(solution_sets * cols)]
    total_in = refs.pop(0) if carries else None
    send_refs = [refs.pop(0) for _ in range(row_count)] if sends else []
    kept_ref = refs.pop(0) if keeps else None
    chosen, total = refs[:2]
    capacity = blocks[0].shape[1]
    groups = capacity // slot_group

    if staged:
        buffer, semaphores = refs[2:]

        def group_copy(k, g):
            part = pl.ds(g * slot_group, slot_group)
            return pltpu.make_async_copy(
                blocks[sets[k][3]].at[sets[k][0], part], buffer.at[k, part], semaphores.at[k, g]
            )

        for k in range(len(sets)):
            for g in range(groups):
                group_copy(k, g).start()

    if carries:
        total[: total_in.shape[0]] = total_in[...]
    else:
        total[...] = jnp.zeros_like(total)
    spare = total.shape[0] - 1
    for j in range(solution_sets * cols):
        chosen[j] = solutions[j][...]

    for k in range(len(sets)):
        level, lowest, solution_index, layer_index = sets[k]
        code = codes[layer_index]

        def one_group(g, unused):
            first = g * slot_group
            if staged:
                group_copy(k, g).wait()
            for s in range(slot_group):
                slot = first + s
                value = code[level, 0, slot]
                aim = lax.shift_right_logical(value, code_shift)
                place = jnp.where(aim < lowest * row_count, spare, aim - lowest_kept * row_count)
                column = solution_index * cols + (value & ((1 << code_shift) - 1))
                piece = buffer[k, slot] if staged else blocks[layer_index][level, slot]
                total[place] += jnp.dot(
                    piece, chosen[column], preferred_element_type=jnp.float32
                )
            return unused

        lax.fori_loop(0, groups, one_group, 0)

    if sends:
        me = lax.axis_index("prow")
        for k in range(row_count):
            send_refs[k][...] = total[partner(me, k, row_count)].astype(jnp.bfloat16)
    if keeps:
        first = row_count if sends else 0
        kept_ref[...] = total[first:spare]


def update(sets, layers, solution_groups, total_in, row_count, lowest_kept, sends, keeps, staged):
    cols = len(solution_groups[0])
    width, sides = solution_groups[0][0].shape
    capacity = layers[0][1].shape[1]
    sections = 3 - lowest_kept
    solutions = [part for group in solution_groups for part in group]
    operands = [a[0] for a in layers] + [a[1] for a in layers] + solutions
    block_space = pltpu.HBM if staged else pltpu.VMEM
    specs = [pl.BlockSpec(memory_space=pltpu.SMEM)] * len(layers)
    specs += [pl.BlockSpec(memory_space=block_space)] * len(layers)
    specs += [pl.BlockSpec(memory_space=pltpu.VMEM)] * len(solutions)
    if total_in is not None:
        operands.append(total_in)
        specs.append(pl.BlockSpec(memory_space=pltpu.VMEM))
    outs = []
    if sends:
        outs += [jax.ShapeDtypeStruct((width, sides), jnp.bfloat16)] * row_count
    if keeps:
        kept = (sections - int(sends)) * row_count
        outs.append(jax.ShapeDtypeStruct((kept, width, sides), jnp.float32))
    scratch = [
        pltpu.VMEM((len(solutions), width, sides), jnp.bfloat16),
        pltpu.VMEM((sections * row_count + 1, width, sides), jnp.float32),
    ]
    if staged:
        scratch += [
            pltpu.VMEM((len(sets), capacity, width, width), jnp.bfloat16),
            pltpu.SemaphoreType.DMA((len(sets), capacity // slot_group)),
        ]
    config = (
        sets, cols, row_count, lowest_kept, len(layers), total_in is not None, sends, keeps, staged,
    )
    found = pl.pallas_call(
        functools.partial(update_kernel, config),
        out_shape=outs,
        in_specs=specs,
        out_specs=[pl.BlockSpec(memory_space=pltpu.VMEM)] * len(outs),
        scratch_shapes=scratch,
        compiler_params=pltpu.CompilerParams(vmem_limit_bytes=48 * 1024 * 1024),
    )(*operands)
    return list(found[:row_count]) if sends else [], found[-1] if keeps else None


def exchange(parts):
    size = len(parts)
    found = [parts[0]]
    for k in range(1, size):
        moves = [(j, partner(j, k, size)) for j in range(size)]
        found.append(lax.ppermute(parts[k], "prow", moves))
    return found


def solve_block(inverse, residual):
    return jnp.dot(inverse, residual, preferred_element_type=jnp.float32).astype(jnp.bfloat16)


def solve_from(received, given, inverse):
    terms = [part.astype(jnp.float32) for part in received]
    while len(terms) > 1:
        terms = [sum(terms[i : i + 2]) for i in range(0, len(terms), 2)]
    residual = (given.astype(jnp.float32) - terms[0]).astype(jnp.bfloat16)
    return solve_block(inverse, residual)


def local(blocks, sources, targets, counts, given_sub, given_top, inverse_sub, inverse_top):
    row_count = lax.axis_size("prow")
    cols = lax.axis_size("pcol")
    depth = lax.axis_size("zgrid")
    levels, capacity = sources.shape[3:]
    block_set = blocks[0, 0, 0]
    right_sub = given_sub[0, 0, 0]
    right_top = given_top[0, 0]
    factor_sub = inverse_sub[0, 0, 0]
    factor_top = inverse_top[0, 0]

    alive = jnp.arange(capacity)[None, None, :] < counts.reshape(levels, 1, 1)
    column = (sources.reshape(levels, 1, capacity) - lax.axis_index("pcol")) % cols
    aim = jnp.where(alive, targets.reshape(levels, 1, capacity), levels * row_count)
    code = (aim << code_shift) + column

    others = [
        (from_other_core(code, m), from_other_core(block_set, m)) for m in range(1, depth)
    ]
    both = [(code, block_set)] + others

    level_zero = solve_block(factor_sub[0], right_sub[0])
    spread_zero = [sibling_values(level_zero, m) for m in range(depth)]
    sends, total = update(
        [(0, 0, 0, 0)], both[:1], spread_zero[:1], None, row_count, 0, True, True, True
    )
    sends, spread_rest = lax.optimization_barrier((sends, spread_zero[1:]))
    received = exchange(sends)
    _, total = update(
        [(0, 1, m, m) for m in range(depth - 1)],
        others, spread_rest, total, row_count, 1, False, True, False,
    )
    received, total = lax.optimization_barrier((received, total))
    level_one = solve_from(received, right_sub[1], factor_sub[1])
    spread_one = [sibling_values(level_one, m) for m in range(depth)]
    sends, total = update(
        [(1, 1, m, m) for m in range(depth)],
        both, spread_one, total, row_count, 1, True, True, False,
    )
    level_two = solve_from(exchange(sends), right_top[0], factor_top[0])
    spread_two = sibling_values(level_two, 0)
    sends, _ = update(
        [(2, 2, 0, m) for m in range(depth)],
        both, [spread_two], total, row_count, 2, True, False, False,
    )
    level_three = solve_from(exchange(sends), right_top[1], factor_top[1])
    solved_sub = jnp.stack([level_zero, level_one])[None, None, None]
    solved_top = jnp.stack([level_two, level_three])[None, None]
    return (solved_sub, solved_top)


def solution(mesh):
    in_specs = (
        P("prow", "pcol", "zgrid", None, None, None, None),
        P("prow", "pcol", "zgrid", None, None),
        P("prow", "pcol", "zgrid", None, None),
        P("prow", "pcol", "zgrid", None),
        P("prow", "pcol", "zgrid", None, None, None),
        P("prow", "pcol", None, None, None),
        P("prow", "pcol", "zgrid", None, None, None),
        P("prow", "pcol", None, None, None),
    )
    out_specs = (P("prow", "pcol", "zgrid", None, None, None), P("prow", "pcol", None, None, None))
    return jax.shard_map(local, mesh=mesh, in_specs=in_specs, out_specs=out_specs, check_vma=False)
```

```python
import functools

import jax
import jax.numpy as jnp
from jax import lax
from jax.experimental import pallas as pl
from jax.experimental.pallas import tpu as pltpu
from jax.sharding import PartitionSpec as P

slot_group = 8
field = 10
field_mask = (1 << field) - 1
pairs = ((0, 1), (0, 2), (0, 3), (1, 2), (1, 3), (2, 3))
params = pltpu.CompilerParams(vmem_limit_bytes=24 * 1024 * 1024)
vmem = pl.BlockSpec(memory_space=pltpu.VMEM)
smem = pl.BlockSpec(memory_space=pltpu.SMEM)


def sibling_values(value, layers):
    cols = lax.axis_size("pcol")
    depth = lax.axis_size("zgrid")
    found = []
    for k in range(cols):
        if k == 0 and layers == 0:
            found.append(value)
            continue
        moves = []
        for c in range(cols):
            for z in range(depth):
                target = ((c - k) % cols) * depth + (z - layers) % depth
                moves.append((c * depth + z, target))
        found.append(lax.ppermute(value, ("pcol", "zgrid"), moves))
    return found


def from_other_core(value):
    return lax.ppermute(value, "zgrid", [(0, 1), (1, 0)])


def plan_kernel(row_count, cols, sources, targets, counts, plan):
    me = lax.axis_index("pcol")
    spare = row_count << field
    for level in range(3):
        first_list = pairs.index((level, level + 1))
        lists = 3 - level

        def one_slot(slot, found):
            target = targets[level, 0, slot]
            higher = [(target >= (level + j) * row_count).astype(jnp.int32) for j in range(1, lists)]
            step = sum(higher) if higher else jnp.int32(0)
            row = target - (level + step) * row_count
            column = sources[level, 0, slot] - me
            column = jnp.where(column < 0, column + cols, column)
            place = found[lists - 1]
            for j in range(lists - 1):
                place = jnp.where(step == j, found[j], place)
            plan[first_list + step, place] = (slot << (2 * field)) + (row << field) + column
            return tuple(found[j] + (step == j).astype(jnp.int32) for j in range(lists))

        found = lax.fori_loop(0, counts[level], one_slot, (jnp.int32(0),) * lists)
        for j in range(lists):
            plan[len(pairs), first_list + j] = found[j]
            for extra in range(slot_group):
                plan[first_list + j, found[j] + extra] = spare


def make_plan(row_count, cols, sources, targets, counts):
    width = -(-(sources.shape[-1] + slot_group) // 128) * 128
    return pl.pallas_call(
        functools.partial(plan_kernel, row_count, cols),
        out_shape=jax.ShapeDtypeStruct((8, width), jnp.int32),
        in_specs=[smem, smem, smem],
        out_specs=smem,
        compiler_params=params,
    )(sources, targets, counts)


def lanes_below(shape, count):
    return lax.broadcasted_iota(jnp.int32, shape, len(shape) - 1) < count


def turned(value):
    return pltpu.roll(value, value.shape[-1] // 2, value.ndim - 1)


def packed(value):
    half = value.shape[0] // 2
    low = lanes_below((half, value.shape[1]), value.shape[1] // 2)
    return jnp.where(low, value[:half], turned(value[half:]))


def unpacked(value):
    return jnp.concatenate([value, turned(value)], axis=0)


def half_first(value, half_index):
    return jnp.where(half_index == 0, value, turned(value))


def update_kernel(config, *refs):
    lists, layer_count, groups_of_solutions, cols, row_count, halved, form, carries, sends = config
    refs = list(refs)
    plans = [refs.pop(0) for _ in range(layer_count)]
    blocks = [refs.pop(0) for _ in range(layer_count)]
    solutions = [[refs.pop(0) for _ in range(cols)] for _ in range(groups_of_solutions)]
    total_in = refs.pop(0) if carries else None
    out, wide, total = refs
    width = blocks[0].shape[2]
    sides = out.shape[-1]
    chunks = wide.shape[2] // sides
    half_index = lax.axis_index("zgrid")
    low = lanes_below((width, sides), sides // 2)

    for j in range(groups_of_solutions):
        parts = [ref[...].astype(jnp.float32) for ref in solutions[j]]
        if not halved:
            for k in range(cols):
                wide[j, :, k * sides : (k + 1) * sides] = solutions[j][k][...]
            continue
        if form == "whole":
            parts = [half_first(part, half_index) for part in parts]
        else:
            parts = [unpacked(part) for part in parts]
        parts.append(parts[0])
        for k in range(chunks):
            both = jnp.where(low, parts[2 * k], turned(parts[2 * k + 1]))
            wide[j, :, k * sides : (k + 1) * sides] = both.astype(jnp.bfloat16)

    if carries:
        total[:row_count] = total_in[...]
    else:
        total[...] = jnp.zeros_like(total)

    for pair, layer, j in lists:
        plan = plans[layer]
        level = pairs[pair][0]

        def one_group(g, unused):
            entries = [plan[pair, g * slot_group + s] for s in range(slot_group)]
            pieces = [
                blocks[layer][level, lax.shift_right_logical(e, 2 * field)] for e in entries
            ]
            product = jnp.dot(
                jnp.concatenate(pieces, axis=0), wide[j], preferred_element_type=jnp.float32
            )
            for s in range(slot_group):
                place = lax.shift_right_logical(entries[s], field) & field_mask
                column = entries[s] & field_mask
                chunk = lax.shift_right_logical(column, 1) if halved else column
                rows = product[s * width : (s + 1) * width]
                part = rows[:, :sides]
                for k in range(1, chunks):
                    part = jnp.where(chunk == k, rows[:, k * sides : (k + 1) * sides], part)
                if halved:
                    part = jnp.where(low == ((column & 1) == 0), part, 0.0)
                total[place] += part
            return unused

        live = plan[len(pairs), pair]
        lax.fori_loop(0, (live + slot_group - 1) // slot_group, one_group, 0)

    if not sends:
        out[...] = total[:row_count]
    elif not halved:
        out[...] = total[:row_count].astype(jnp.bfloat16)
    else:
        for row in range(row_count):
            value = total[row]
            out[row] = packed(value + turned(value)).astype(jnp.bfloat16)


def update(lists, layers, solution_groups, form, total_in, row_count, halved, sends):
    cols = len(solution_groups[0])
    width = layers[0][1].shape[2]
    sides = solution_groups[0][0].shape[-1]
    solutions = [part for group in solution_groups for part in group]
    operands = [a[0] for a in layers] + [a[1] for a in layers] + solutions
    specs = [smem] * len(layers) + [vmem] * (len(layers) + len(solutions))
    if total_in is not None:
        operands.append(total_in)
        specs.append(vmem)
    if sends:
        rows = width // 2 if halved else width
        out_shape = jax.ShapeDtypeStruct((row_count, rows, sides), jnp.bfloat16)
    else:
        out_shape = jax.ShapeDtypeStruct((row_count, width, sides), jnp.float32)
    chunks = (cols + 1) // 2 if halved else cols
    config = (
        lists, len(layers), len(solution_groups), cols, row_count, halved, form,
        total_in is not None, sends,
    )
    return pl.pallas_call(
        functools.partial(update_kernel, config),
        out_shape=out_shape,
        in_specs=specs,
        out_specs=vmem,
        scratch_shapes=[
            pltpu.VMEM((len(solution_groups), width, chunks * sides), jnp.bfloat16),
            pltpu.VMEM((row_count + 1, width, sides), jnp.float32),
        ],
        compiler_params=params,
    )(*operands)


def half_solve_kernel(level, received, given, inverse, *refs):
    earlier, out = refs if len(refs) == 2 else (None, refs[0])
    half_index = lax.axis_index("zgrid")
    incoming = received[0].astype(jnp.float32)
    for row in range(1, received.shape[0]):
        incoming = incoming + received[row].astype(jnp.float32)
    right = half_first(given[level].astype(jnp.float32), half_index)
    residual = (right - unpacked(incoming)).astype(jnp.bfloat16)
    solved = packed(jnp.dot(inverse[level], residual, preferred_element_type=jnp.float32))
    if earlier is None:
        out[...] = solved.astype(jnp.bfloat16)
    else:
        out[0] = earlier[...]
        out[1] = solved.astype(jnp.bfloat16)


def half_solve(level, received, given, inverse, earlier):
    shape = received.shape[1:]
    operands = [received, given, inverse] + ([] if earlier is None else [earlier])
    return pl.pallas_call(
        functools.partial(half_solve_kernel, level),
        out_shape=jax.ShapeDtypeStruct(shape if earlier is None else (2,) + shape, jnp.bfloat16),
        in_specs=[vmem] * len(operands),
        out_specs=vmem,
        compiler_params=params,
    )(*operands)


def join_kernel(own, other, out):
    half_index = lax.axis_index("zgrid")
    for level in range(2):
        mine = own[level].astype(jnp.float32)
        theirs = other[level].astype(jnp.float32)
        first = unpacked(jnp.where(half_index == 0, mine, theirs))
        second = unpacked(jnp.where(half_index == 0, theirs, mine))
        low = lanes_below(first.shape, first.shape[-1] // 2)
        out[0, 0, level] = jnp.where(low, first, turned(second)).astype(jnp.bfloat16)


def join_halves(own, other):
    levels, half, sides = own.shape
    return pl.pallas_call(
        join_kernel,
        out_shape=jax.ShapeDtypeStruct((1, 1, levels, 2 * half, sides), jnp.bfloat16),
        in_specs=[vmem, vmem],
        out_specs=vmem,
        compiler_params=params,
    )(own, other)


def solve_block(inverse, residual):
    return jnp.dot(inverse, residual, preferred_element_type=jnp.float32).astype(jnp.bfloat16)


def exchange(send):
    return lax.all_to_all(send, "prow", 0, 0, tiled=True)


def local(blocks, sources, targets, counts, given_sub, given_top, inverse_sub, inverse_top):
    row_count = lax.axis_size("prow")
    cols = lax.axis_size("pcol")
    levels, capacity = sources.shape[3:]
    block_set = blocks[0, 0, 0]
    right_sub = given_sub[0, 0, 0]
    factor_sub = inverse_sub[0, 0, 0]
    right_top = given_top[0, 0]
    factor_top = inverse_top[0, 0]

    level_zero = solve_block(factor_sub[0], right_sub[0])
    zero_own = sibling_values(level_zero, 0)
    zero_other = sibling_values(level_zero, 1)
    plan = make_plan(
        row_count, cols,
        sources.reshape(levels, 1, capacity), targets.reshape(levels, 1, capacity),
        counts.reshape(levels),
    )
    block_other = from_other_core(block_set)
    plan_other = from_other_core(plan)
    own = (plan, block_set)
    other = (plan_other, block_other)

    send = update([(0, 0, 0)], [own], [zero_own], "whole", None, row_count, False, True)
    send, zero_other, plan_other = lax.optimization_barrier((send, zero_other, plan_other))
    other = (plan_other, block_other)
    received = exchange(send)
    second = update(
        [(1, 0, 0), (1, 1, 1)], [own, other], [zero_own, zero_other], "whole", None,
        row_count, True, False,
    )
    received, second = lax.optimization_barrier((received, second))
    incoming = jnp.sum(received.astype(jnp.float32), axis=0)
    level_one = solve_block(
        factor_sub[1], (right_sub[1].astype(jnp.float32) - incoming).astype(jnp.bfloat16)
    )
    one_own = sibling_values(level_one, 0)
    one_other = sibling_values(level_one, 1)

    send = update(
        [(3, 0, 0), (3, 1, 1)], [own, other], [one_own, one_other], "whole", second,
        row_count, True, True,
    )
    received = exchange(send)
    third = update(
        [(2, 0, 0), (2, 1, 1), (4, 0, 2), (4, 1, 3)], [own, other],
        [zero_own, zero_other, one_own, one_other], "whole", None, row_count, True, False,
    )
    received, third = lax.optimization_barrier((received, third))
    level_two = half_solve(0, received, right_top, factor_top, None)
    two_own = sibling_values(level_two, 0)

    send = update(
        [(5, 0, 0), (5, 1, 0)], [own, other], [two_own], "packed", third, row_count, True, True
    )
    solved_halves = half_solve(1, exchange(send), right_top, factor_top, level_two)
    solved_top = join_halves(solved_halves, from_other_core(solved_halves))
    solved_sub = jnp.stack([level_zero, level_one])[None, None, None]
    return (solved_sub, solved_top)


def solution(mesh):
    in_specs = (
        P("prow", "pcol", "zgrid", None, None, None, None),
        P("prow", "pcol", "zgrid", None, None),
        P("prow", "pcol", "zgrid", None, None),
        P("prow", "pcol", "zgrid", None),
        P("prow", "pcol", "zgrid", None, None, None),
        P("prow", "pcol", None, None, None),
        P("prow", "pcol", "zgrid", None, None, None),
        P("prow", "pcol", None, None, None),
    )
    out_specs = (P("prow", "pcol", "zgrid", None, None, None), P("prow", "pcol", None, None, None))
    return jax.shard_map(local, mesh=mesh, in_specs=in_specs, out_specs=out_specs, check_vma=False)
```

```python
import functools

import jax
import jax.numpy as jnp
from jax import lax
from jax.experimental import pallas as pl
from jax.experimental.pallas import tpu as pltpu
from jax.sharding import PartitionSpec as P

slot_group = 8
field = 10
field_mask = (1 << field) - 1
pairs = ((0, 1), (0, 2), (0, 3), (1, 2), (1, 3), (2, 3))
params = pltpu.CompilerParams(vmem_limit_bytes=24 * 1024 * 1024)
vmem = pl.BlockSpec(memory_space=pltpu.VMEM)
smem = pl.BlockSpec(memory_space=pltpu.SMEM)


def sibling_values(value, layers):
    cols = lax.axis_size("pcol")
    depth = lax.axis_size("zgrid")
    found = []
    for k in range(cols):
        if k == 0 and layers == 0:
            found.append(value)
            continue
        moves = []
        for c in range(cols):
            for z in range(depth):
                target = ((c - k) % cols) * depth + (z - layers) % depth
                moves.append((c * depth + z, target))
        found.append(lax.ppermute(value, ("pcol", "zgrid"), moves))
    return found


def from_other_core(value):
    return lax.ppermute(value, "zgrid", [(0, 1), (1, 0)])


def in_hbm(value):
    return pltpu.with_memory_space_constraint(value, pltpu.HBM)


def plan_kernel(row_count, cols, sources_in, targets_in, counts_in, blocks, plan, staged, *scratch):
    sources, targets, counts, semaphores = scratch
    loads = [
        pltpu.make_async_copy(sources_in, sources, semaphores.at[0]),
        pltpu.make_async_copy(targets_in, targets, semaphores.at[1]),
        pltpu.make_async_copy(counts_in, counts, semaphores.at[2]),
        pltpu.make_async_copy(blocks, staged, semaphores.at[3]),
    ]
    for load in loads:
        load.start()
    for load in loads[:3]:
        load.wait()
    me = lax.axis_index("pcol")
    spare = row_count << field
    for level in range(3):
        first_list = pairs.index((level, level + 1))
        lists = 3 - level

        def one_slot(slot, found):
            target = targets[level, 0, slot]
            higher = [(target >= (level + j) * row_count).astype(jnp.int32) for j in range(1, lists)]
            step = sum(higher) if higher else jnp.int32(0)
            row = target - (level + step) * row_count
            column = sources[level, 0, slot] - me
            column = jnp.where(column < 0, column + cols, column)
            place = found[lists - 1]
            for j in range(lists - 1):
                place = jnp.where(step == j, found[j], place)
            plan[first_list + step, place] = (slot << (2 * field)) + (row << field) + column
            return tuple(found[j] + (step == j).astype(jnp.int32) for j in range(lists))

        found = lax.fori_loop(0, counts[level], one_slot, (jnp.int32(0),) * lists)
        for j in range(lists):
            plan[len(pairs), first_list + j] = found[j]
            for extra in range(slot_group):
                plan[first_list + j, found[j] + extra] = spare
    loads[3].wait()


def make_plan(row_count, cols, sources, targets, counts, blocks):
    width = -(-(sources.shape[-1] + slot_group) // 128) * 128
    return pl.pallas_call(
        functools.partial(plan_kernel, row_count, cols),
        out_shape=[
            jax.ShapeDtypeStruct((8, width), jnp.int32), pltpu.VMEM(blocks.shape, blocks.dtype)
        ],
        in_specs=[pl.BlockSpec(memory_space=pltpu.HBM)] * 4,
        out_specs=[smem, vmem],
        scratch_shapes=[
            pltpu.SMEM(sources.shape, jnp.int32),
            pltpu.SMEM(targets.shape, jnp.int32),
            pltpu.SMEM(counts.shape, jnp.int32),
            pltpu.SemaphoreType.DMA((4,)),
        ],
        compiler_params=params,
    )(in_hbm(sources), in_hbm(targets), in_hbm(counts), in_hbm(blocks))


def update_kernel(config, *refs):
    lists, layer_count, groups_of_solutions, cols, row_count, carries = config
    refs = list(refs)
    plans = [refs.pop(0) for _ in range(layer_count)]
    blocks = [refs.pop(0) for _ in range(layer_count)]
    solutions = [refs.pop(0) for _ in range(groups_of_solutions * cols)]
    total_in = refs.pop(0) if carries else None
    out, chosen, total = refs

    for j, solution_ref in enumerate(solutions):
        chosen[j] = solution_ref[...]
    if carries:
        total[:row_count] = total_in[...]
    else:
        total[...] = jnp.zeros_like(total)

    for pair, layer, j in lists:
        plan = plans[layer]
        level = pairs[pair][0]

        def one_group(g, unused):
            for s in range(slot_group):
                entry = plan[pair, g * slot_group + s]
                place = lax.shift_right_logical(entry, field) & field_mask
                column = j * cols + (entry & field_mask)
                total[place] += jnp.dot(
                    blocks[layer][level, lax.shift_right_logical(entry, 2 * field)],
                    chosen[column],
                    preferred_element_type=jnp.float32,
                )
            return unused

        live = plan[len(pairs), pair]
        lax.fori_loop(0, (live + slot_group - 1) // slot_group, one_group, 0)

    out[...] = total[:row_count].astype(out.dtype)


def update(lists, plans, blocks, solution_groups, total_in, row_count, sends):
    cols = len(solution_groups[0])
    width, sides = solution_groups[0][0].shape
    solutions = [part for group in solution_groups for part in group]
    operands = plans + blocks + solutions
    specs = [smem] * len(plans) + [vmem] * (len(blocks) + len(solutions))
    if total_in is not None:
        operands.append(total_in)
        specs.append(vmem)
    config = (lists, len(plans), len(solution_groups), cols, row_count, total_in is not None)
    return pl.pallas_call(
        functools.partial(update_kernel, config),
        out_shape=jax.ShapeDtypeStruct(
            (row_count, width, sides), jnp.bfloat16 if sends else jnp.float32
        ),
        in_specs=specs,
        out_specs=vmem,
        scratch_shapes=[
            pltpu.VMEM((len(solutions), width, sides), jnp.bfloat16),
            pltpu.VMEM((row_count + 1, width, sides), jnp.float32),
        ],
        compiler_params=params,
    )(*operands)


def solve_block(inverse, residual):
    return jnp.dot(inverse, residual, preferred_element_type=jnp.float32).astype(jnp.bfloat16)


def reduced_solve(received, given, inverse):
    incoming = jnp.sum(received.astype(jnp.float32), axis=0)
    residual = (given.astype(jnp.float32) - incoming).astype(jnp.bfloat16)
    return solve_block(inverse, residual)


def exchange(send):
    return lax.all_to_all(send, "prow", 0, 0, tiled=True)


def local(blocks, sources, targets, counts, given_sub, given_top, inverse_sub, inverse_top):
    row_count = lax.axis_size("prow")
    cols = lax.axis_size("pcol")
    levels, capacity = sources.shape[3:]
    block_set = blocks[0, 0, 0]
    right_sub = given_sub[0, 0, 0]
    factor_sub = inverse_sub[0, 0, 0]
    right_top = given_top[0, 0]
    factor_top = inverse_top[0, 0]

    level_zero = solve_block(factor_sub[0], right_sub[0])
    zero_own = sibling_values(level_zero, 0)
    zero_other = sibling_values(level_zero, 1)
    plan, block_own = make_plan(
        row_count, cols,
        sources.reshape(levels, 1, capacity), targets.reshape(levels, 1, capacity),
        counts.reshape(levels), block_set,
    )
    block_other = pltpu.with_memory_space_constraint(from_other_core(block_set), pltpu.VMEM)

    send = update([(0, 0, 0)], [plan], [block_own], [zero_own], None, row_count, True)
    send, zero_other, plan_sent = lax.optimization_barrier((send, zero_other, plan))
    received = exchange(send)
    plans = [plan, from_other_core(plan_sent)]
    both = [block_own, block_other]
    second = update(
        [(1, 0, 0), (1, 1, 1)], plans, both, [zero_own, zero_other], None, row_count, False
    )
    received, second = lax.optimization_barrier((received, second))
    level_one = reduced_solve(received, right_sub[1], factor_sub[1])
    one_own = sibling_values(level_one, 0)
    one_other = sibling_values(level_one, 1)

    send = update(
        [(3, 0, 0), (3, 1, 1)], plans, both, [one_own, one_other], second, row_count, True
    )
    received = exchange(send)
    third = update(
        [(2, 0, 0), (2, 1, 1), (4, 0, 2), (4, 1, 3)], plans, both,
        [zero_own, zero_other, one_own, one_other], None, row_count, False,
    )
    received, third = lax.optimization_barrier((received, third))
    level_two = reduced_solve(received, right_top[0], factor_top[0])
    two_own = sibling_values(level_two, 0)

    send = update(
        [(5, 0, 0), (5, 1, 0)], plans, both, [two_own], third, row_count, True
    )
    level_three = reduced_solve(exchange(send), right_top[1], factor_top[1])
    solved_sub = jnp.stack([level_zero, level_one])[None, None, None]
    solved_top = jnp.stack([level_two, level_three])[None, None]
    return (solved_sub, solved_top)


def solution(mesh):
    in_specs = (
        P("prow", "pcol", "zgrid", None, None, None, None),
        P("prow", "pcol", "zgrid", None, None),
        P("prow", "pcol", "zgrid", None, None),
        P("prow", "pcol", "zgrid", None),
        P("prow", "pcol", "zgrid", None, None, None),
        P("prow", "pcol", None, None, None),
        P("prow", "pcol", "zgrid", None, None, None),
        P("prow", "pcol", None, None, None),
    )
    out_specs = (P("prow", "pcol", "zgrid", None, None, None), P("prow", "pcol", None, None, None))
    return jax.shard_map(local, mesh=mesh, in_specs=in_specs, out_specs=out_specs, check_vma=False)
```

```python
import functools

import jax
import jax.numpy as jnp
from jax import lax
from jax.experimental import pallas as pl
from jax.experimental.pallas import tpu as pltpu
from jax.sharding import PartitionSpec as P

slot_group = 8
field = 10
field_mask = (1 << field) - 1
pairs = ((0, 1), (0, 2), (0, 3), (1, 2), (1, 3), (2, 3))
params = pltpu.CompilerParams(vmem_limit_bytes=24 * 1024 * 1024)
vmem = pl.BlockSpec(memory_space=pltpu.VMEM)
smem = pl.BlockSpec(memory_space=pltpu.SMEM)
hbm = pl.BlockSpec(memory_space=pltpu.HBM)


def sibling_values(value, layers):
    cols = lax.axis_size("pcol")
    depth = lax.axis_size("zgrid")
    found = []
    for k in range(cols):
        if k == 0 and layers == 0:
            found.append(value)
            continue
        moves = []
        for c in range(cols):
            for z in range(depth):
                target = ((c - k) % cols) * depth + (z - layers) % depth
                moves.append((c * depth + z, target))
        found.append(lax.ppermute(value, ("pcol", "zgrid"), moves))
    return found


def from_other_core(value):
    return lax.ppermute(value, "zgrid", [(0, 1), (1, 0)])


def in_hbm(value):
    return pltpu.with_memory_space_constraint(value, pltpu.HBM)


def plan_kernel(row_count, cols, sources_in, targets_in, counts_in, plan, *scratch):
    sources, targets, counts, semaphores = scratch
    loads = [
        pltpu.make_async_copy(sources_in, sources, semaphores.at[0]),
        pltpu.make_async_copy(targets_in, targets, semaphores.at[1]),
        pltpu.make_async_copy(counts_in, counts, semaphores.at[2]),
    ]
    for load in loads:
        load.start()
    for load in loads:
        load.wait()
    me = lax.axis_index("pcol")
    spare = row_count << field
    for level in range(3):
        first_list = pairs.index((level, level + 1))
        lists = 3 - level

        def one_slot(slot, found):
            target = targets[level, 0, slot]
            higher = [(target >= (level + j) * row_count).astype(jnp.int32) for j in range(1, lists)]
            step = sum(higher) if higher else jnp.int32(0)
            row = target - (level + step) * row_count
            column = sources[level, 0, slot] - me
            column = jnp.where(column < 0, column + cols, column)
            place = found[lists - 1]
            for j in range(lists - 1):
                place = jnp.where(step == j, found[j], place)
            plan[first_list + step, place] = (slot << (2 * field)) + (row << field) + column
            return tuple(found[j] + (step == j).astype(jnp.int32) for j in range(lists))

        found = lax.fori_loop(0, counts[level], one_slot, (jnp.int32(0),) * lists)
        for j in range(lists):
            plan[len(pairs), first_list + j] = found[j]
            for extra in range(slot_group):
                plan[first_list + j, found[j] + extra] = spare


def make_plan(row_count, cols, sources, targets, counts):
    width = -(-(sources.shape[-1] + slot_group) // 128) * 128
    return pl.pallas_call(
        functools.partial(plan_kernel, row_count, cols),
        out_shape=jax.ShapeDtypeStruct((8, width), jnp.int32),
        in_specs=[hbm] * 3,
        out_specs=smem,
        scratch_shapes=[
            pltpu.SMEM(sources.shape, jnp.int32),
            pltpu.SMEM(targets.shape, jnp.int32),
            pltpu.SMEM(counts.shape, jnp.int32),
            pltpu.SemaphoreType.DMA((3,)),
        ],
        compiler_params=params,
    )(in_hbm(sources), in_hbm(targets), in_hbm(counts))


def fetched_levels(lists):
    return list(dict.fromkeys((layer, pairs[pair][0]) for pair, layer, _ in lists))


def update_kernel(config, *refs):
    lists, layer_count, groups_of_solutions, cols, row_count, carries = config
    refs = list(refs)
    plans = [refs.pop(0) for _ in range(layer_count)]
    blocks = [refs.pop(0) for _ in range(layer_count)]
    solutions = [refs.pop(0) for _ in range(groups_of_solutions * cols)]
    total_in = refs.pop(0) if carries else None
    out, chosen, total, staged, semaphores = refs
    fetched = fetched_levels(lists)
    loads = [
        pltpu.make_async_copy(blocks[layer].at[level], staged.at[k], semaphores.at[k])
        for k, (layer, level) in enumerate(fetched)
    ]
    for load in loads:
        load.start()
    waited = set()

    for j, solution_ref in enumerate(solutions):
        chosen[j] = solution_ref[...]
    if carries:
        total[:row_count] = total_in[...]
    else:
        total[...] = jnp.zeros_like(total)

    for pair, layer, j in lists:
        plan = plans[layer]
        k = fetched.index((layer, pairs[pair][0]))
        if k not in waited:
            loads[k].wait()
            waited.add(k)

        def one_group(g, unused):
            for s in range(slot_group):
                entry = plan[pair, g * slot_group + s]
                place = lax.shift_right_logical(entry, field) & field_mask
                column = j * cols + (entry & field_mask)
                total[place] += jnp.dot(
                    staged[k, lax.shift_right_logical(entry, 2 * field)],
                    chosen[column],
                    preferred_element_type=jnp.float32,
                )
            return unused

        live = plan[len(pairs), pair]
        lax.fori_loop(0, (live + slot_group - 1) // slot_group, one_group, 0)

    out[...] = total[:row_count].astype(out.dtype)


def update(lists, plans, blocks, solution_groups, total_in, row_count, sends):
    cols = len(solution_groups[0])
    width, sides = solution_groups[0][0].shape
    solutions = [part for group in solution_groups for part in group]
    operands = plans + blocks + solutions
    specs = [smem] * len(plans) + [hbm] * len(blocks) + [vmem] * len(solutions)
    fetched = fetched_levels(lists)
    if total_in is not None:
        operands.append(total_in)
        specs.append(vmem)
    config = (lists, len(plans), len(solution_groups), cols, row_count, total_in is not None)
    return pl.pallas_call(
        functools.partial(update_kernel, config),
        out_shape=jax.ShapeDtypeStruct(
            (row_count, width, sides), jnp.bfloat16 if sends else jnp.float32
        ),
        in_specs=specs,
        out_specs=vmem,
        scratch_shapes=[
            pltpu.VMEM((len(solutions), width, sides), jnp.bfloat16),
            pltpu.VMEM((row_count + 1, width, sides), jnp.float32),
            pltpu.VMEM((len(fetched),) + blocks[0].shape[1:], jnp.bfloat16),
            pltpu.SemaphoreType.DMA((len(fetched),)),
        ],
        compiler_params=params,
    )(*operands)


def solve_block(inverse, residual):
    return jnp.dot(inverse, residual, preferred_element_type=jnp.float32).astype(jnp.bfloat16)


def reduced_solve(received, given, inverse):
    incoming = jnp.sum(received.astype(jnp.float32), axis=0)
    residual = (given.astype(jnp.float32) - incoming).astype(jnp.bfloat16)
    return solve_block(inverse, residual)


def exchange(send):
    return lax.all_to_all(send, "prow", 0, 0, tiled=True)


def local(blocks, sources, targets, counts, given_sub, given_top, inverse_sub, inverse_top):
    row_count = lax.axis_size("prow")
    cols = lax.axis_size("pcol")
    levels, capacity = sources.shape[3:]
    block_set = blocks[0, 0, 0]
    right_sub = given_sub[0, 0, 0]
    factor_sub = inverse_sub[0, 0, 0]
    right_top = given_top[0, 0]
    factor_top = inverse_top[0, 0]

    level_zero = solve_block(factor_sub[0], right_sub[0])
    zero_own = sibling_values(level_zero, 0)
    zero_other = sibling_values(level_zero, 1)
    plan = make_plan(
        row_count, cols,
        sources.reshape(levels, 1, capacity), targets.reshape(levels, 1, capacity),
        counts.reshape(levels),
    )
    block_own = in_hbm(block_set)
    block_other = in_hbm(from_other_core(block_set))

    send = update([(0, 0, 0)], [plan], [block_own], [zero_own], None, row_count, True)
    send, zero_other, plan_sent = lax.optimization_barrier((send, zero_other, plan))
    received = exchange(send)
    plans = [plan, from_other_core(plan_sent)]
    both = [block_own, block_other]
    second = update(
        [(1, 0, 0), (1, 1, 1)], plans, both, [zero_own, zero_other], None, row_count, False
    )
    received, second = lax.optimization_barrier((received, second))
    level_one = reduced_solve(received, right_sub[1], factor_sub[1])
    one_own = sibling_values(level_one, 0)
    one_other = sibling_values(level_one, 1)

    send = update(
        [(3, 0, 0), (3, 1, 1)], plans, both, [one_own, one_other], second, row_count, True
    )
    received = exchange(send)
    third = update(
        [(2, 0, 0), (2, 1, 1), (4, 0, 2), (4, 1, 3)], plans, both,
        [zero_own, zero_other, one_own, one_other], None, row_count, False,
    )
    received, third = lax.optimization_barrier((received, third))
    level_two = reduced_solve(received, right_top[0], factor_top[0])
    two_own = sibling_values(level_two, 0)

    send = update(
        [(5, 0, 0), (5, 1, 0)], plans, both, [two_own], third, row_count, True
    )
    level_three = reduced_solve(exchange(send), right_top[1], factor_top[1])
    solved_sub = jnp.stack([level_zero, level_one])[None, None, None]
    solved_top = jnp.stack([level_two, level_three])[None, None]
    return (solved_sub, solved_top)


def solution(mesh):
    in_specs = (
        P("prow", "pcol", "zgrid", None, None, None, None),
        P("prow", "pcol", "zgrid", None, None),
        P("prow", "pcol", "zgrid", None, None),
        P("prow", "pcol", "zgrid", None),
        P("prow", "pcol", "zgrid", None, None, None),
        P("prow", "pcol", None, None, None),
        P("prow", "pcol", "zgrid", None, None, None),
        P("prow", "pcol", None, None, None),
    )
    out_specs = (P("prow", "pcol", "zgrid", None, None, None), P("prow", "pcol", None, None, None))
    return jax.shard_map(local, mesh=mesh, in_specs=in_specs, out_specs=out_specs, check_vma=False)
```

```python
import functools

import jax
import jax.numpy as jnp
from jax import lax
from jax.experimental import pallas as pl
from jax.experimental.pallas import tpu as pltpu
from jax.sharding import PartitionSpec as P

slot_group = 8
field = 10
field_mask = (1 << field) - 1
pairs = ((0, 1), (0, 2), (0, 3), (1, 2), (1, 3), (2, 3))
params = pltpu.CompilerParams(vmem_limit_bytes=24 * 1024 * 1024)
vmem = pl.BlockSpec(memory_space=pltpu.VMEM)
smem = pl.BlockSpec(memory_space=pltpu.SMEM)
hbm = pl.BlockSpec(memory_space=pltpu.HBM)
anywhere = pl.BlockSpec(memory_space=pl.ANY)


def sibling_values(value, layers):
    cols = lax.axis_size("pcol")
    depth = lax.axis_size("zgrid")
    found = []
    for k in range(cols):
        if k == 0 and layers == 0:
            found.append(value)
            continue
        moves = []
        for c in range(cols):
            for z in range(depth):
                target = ((c - k) % cols) * depth + (z - layers) % depth
                moves.append((c * depth + z, target))
        found.append(lax.ppermute(value, ("pcol", "zgrid"), moves))
    return found


def from_other_core(value):
    return lax.ppermute(value, "zgrid", [(0, 1), (1, 0)])


def in_hbm(value):
    return pltpu.with_memory_space_constraint(value, pltpu.HBM)


def plan_kernel(row_count, cols, sources_in, targets_in, counts_in, blocks, plan, staged, *scratch):
    sources, targets, counts, semaphores = scratch
    loads = [
        pltpu.make_async_copy(sources_in, sources, semaphores.at[0]),
        pltpu.make_async_copy(targets_in, targets, semaphores.at[1]),
        pltpu.make_async_copy(counts_in, counts, semaphores.at[2]),
    ]
    for load in loads:
        load.start()
    stage = pltpu.make_async_copy(blocks.at[0], staged, semaphores.at[3])
    stage.start()
    for load in loads:
        load.wait()
    me = lax.axis_index("pcol")
    spare = row_count << field
    for level in range(3):
        first_list = pairs.index((level, level + 1))
        lists = 3 - level

        def one_slot(slot, found):
            target = targets[level, 0, slot]
            higher = [(target >= (level + j) * row_count).astype(jnp.int32) for j in range(1, lists)]
            step = sum(higher) if higher else jnp.int32(0)
            row = target - (level + step) * row_count
            column = sources[level, 0, slot] - me
            column = jnp.where(column < 0, column + cols, column)
            place = found[lists - 1]
            for j in range(lists - 1):
                place = jnp.where(step == j, found[j], place)
            plan[first_list + step, place] = (slot << (2 * field)) + (row << field) + column
            return tuple(found[j] + (step == j).astype(jnp.int32) for j in range(lists))

        found = lax.fori_loop(0, counts[level], one_slot, (jnp.int32(0),) * lists)
        for j in range(lists):
            plan[len(pairs), first_list + j] = found[j]
            for extra in range(slot_group):
                plan[first_list + j, found[j] + extra] = spare
    stage.wait()


def make_plan(row_count, cols, sources, targets, counts, blocks):
    width = -(-(sources.shape[-1] + slot_group) // 128) * 128
    return pl.pallas_call(
        functools.partial(plan_kernel, row_count, cols),
        out_shape=[
            jax.ShapeDtypeStruct((8, width), jnp.int32),
            pltpu.VMEM(blocks.shape[1:], blocks.dtype),
        ],
        in_specs=[hbm] * 4,
        out_specs=[smem, vmem],
        scratch_shapes=[
            pltpu.SMEM(sources.shape, jnp.int32),
            pltpu.SMEM(targets.shape, jnp.int32),
            pltpu.SMEM(counts.shape, jnp.int32),
            pltpu.SemaphoreType.DMA((4,)),
        ],
        compiler_params=params,
    )(in_hbm(sources), in_hbm(targets), in_hbm(counts), blocks)


def fetched_levels(lists, resident):
    needed = dict.fromkeys((layer, pairs[pair][0]) for pair, layer, _ in lists)
    return [key for key in needed if key != resident]


def update_kernel(config, *refs):
    lists, layer_count, groups_of_solutions, cols, row_count, resident, stages, carries = config
    refs = list(refs)
    plans_in = [refs.pop(0) for _ in range(layer_count)]
    blocks = [refs.pop(0) for _ in range(layer_count)]
    solutions = [refs.pop(0) for _ in range(groups_of_solutions * cols)]
    resident_ref = refs.pop(0) if resident else None
    total_in = refs.pop(0) if carries else None
    out = refs.pop(0)
    next_ref = refs.pop(0) if stages else None
    chosen, total, plans, plan_semaphores, semaphores = refs[:5]
    fetched = fetched_levels(lists, resident)

    plan_loads = [
        pltpu.make_async_copy(plans_in[n], plans.at[n], plan_semaphores.at[n])
        for n in range(layer_count)
    ]
    loads = {
        key: pltpu.make_async_copy(blocks[key[0]].at[key[1]], refs[5].at[k], semaphores.at[k])
        for k, key in enumerate(fetched)
    }
    for load in plan_loads + list(loads.values()):
        load.start()
    if stages:
        stage = pltpu.make_async_copy(blocks[0].at[stages], next_ref, semaphores.at[len(fetched)])
        stage.start()

    for j, solution_ref in enumerate(solutions):
        chosen[j] = solution_ref[...]
    if carries:
        total[:row_count] = total_in[...]
    else:
        total[...] = jnp.zeros_like(total)
    for load in plan_loads:
        load.wait()

    for pair, layer, j in lists:
        key = (layer, pairs[pair][0])
        if key in loads:
            loads.pop(key).wait()
        pieces = resident_ref if key == resident else refs[5].at[fetched.index(key)]

        def one_group(g, unused):
            for s in range(slot_group):
                entry = plans[layer, pair, g * slot_group + s]
                place = lax.shift_right_logical(entry, field) & field_mask
                column = j * cols + (entry & field_mask)
                total[place] += jnp.dot(
                    pieces[lax.shift_right_logical(entry, 2 * field)],
                    chosen[column],
                    preferred_element_type=jnp.float32,
                )
            return unused

        live = plans[layer, len(pairs), pair]
        lax.fori_loop(0, (live + slot_group - 1) // slot_group, one_group, 0)

    out[...] = total[:row_count].astype(out.dtype)
    if stages:
        stage.wait()


def update(
    lists, plans, blocks, solution_groups, total_in, row_count, sends, resident, resident_blocks, stages
):
    cols = len(solution_groups[0])
    width, sides = solution_groups[0][0].shape
    solutions = [part for group in solution_groups for part in group]
    operands = plans + blocks + solutions
    specs = [anywhere] * len(plans) + [hbm] * len(blocks) + [vmem] * len(solutions)
    for extra in (resident_blocks, total_in):
        if extra is not None:
            operands.append(extra)
            specs.append(vmem)
    fetched = fetched_levels(lists, resident)
    outs = [
        jax.ShapeDtypeStruct((row_count, width, sides), jnp.bfloat16 if sends else jnp.float32)
    ]
    if stages:
        outs.append(pltpu.VMEM(blocks[0].shape[1:], blocks[0].dtype))
    config = (
        lists, len(plans), len(solution_groups), cols, row_count, resident, stages,
        total_in is not None,
    )
    scratch = [
        pltpu.VMEM((len(solutions), width, sides), jnp.bfloat16),
        pltpu.VMEM((row_count + 1, width, sides), jnp.float32),
        pltpu.SMEM((len(plans),) + plans[0].shape, jnp.int32),
        pltpu.SemaphoreType.DMA((len(plans),)),
        pltpu.SemaphoreType.DMA((len(fetched) + 1,)),
    ]
    if fetched:
        scratch.append(pltpu.VMEM((len(fetched),) + blocks[0].shape[1:], jnp.bfloat16))
    found = pl.pallas_call(
        functools.partial(update_kernel, config),
        out_shape=outs,
        in_specs=specs,
        out_specs=[vmem] * len(outs),
        scratch_shapes=scratch,
        compiler_params=params,
    )(*operands)
    return found if stages else found[0]


def solve_block(inverse, residual):
    return jnp.dot(inverse, residual, preferred_element_type=jnp.float32).astype(jnp.bfloat16)


def reduced_solve(received, given, inverse):
    incoming = jnp.sum(received.astype(jnp.float32), axis=0)
    residual = (given.astype(jnp.float32) - incoming).astype(jnp.bfloat16)
    return solve_block(inverse, residual)


def exchange(send):
    return lax.all_to_all(send, "prow", 0, 0, tiled=True)


def local(blocks, sources, targets, counts, given_sub, given_top, inverse_sub, inverse_top):
    row_count = lax.axis_size("prow")
    cols = lax.axis_size("pcol")
    levels, capacity = sources.shape[3:]
    block_set = blocks[0, 0, 0]
    right_sub = given_sub[0, 0, 0]
    factor_sub = inverse_sub[0, 0, 0]
    right_top = given_top[0, 0]
    factor_top = inverse_top[0, 0]

    level_zero = solve_block(factor_sub[0], right_sub[0])
    zero_own = sibling_values(level_zero, 0)
    block_own = in_hbm(block_set)
    plan, staged = make_plan(
        row_count, cols,
        sources.reshape(levels, 1, capacity), targets.reshape(levels, 1, capacity),
        counts.reshape(levels), block_own,
    )
    both = [block_own, in_hbm(from_other_core(block_set))]

    send = update(
        [(0, 0, 0)], [plan], both[:1], [zero_own], None, row_count, True, (0, 0), staged, 0
    )
    send, zero_sent, plan_sent = lax.optimization_barrier((send, level_zero, plan))
    received = exchange(send)
    zero_other = sibling_values(zero_sent, 1)
    plans = [plan, from_other_core(plan_sent)]
    second, staged = update(
        [(1, 0, 0), (1, 1, 1)], plans, both, [zero_own, zero_other], None, row_count, False,
        None, None, 1,
    )
    received, second, staged = lax.optimization_barrier((received, second, staged))
    level_one = reduced_solve(received, right_sub[1], factor_sub[1])
    one_own = sibling_values(level_one, 0)
    one_other = sibling_values(level_one, 1)

    send = update(
        [(3, 0, 0), (3, 1, 1)], plans, both, [one_own, one_other], second, row_count, True,
        (0, 1), staged, 0,
    )
    received = exchange(send)
    third, staged = update(
        [(2, 0, 0), (2, 1, 1), (4, 0, 2), (4, 1, 3)], plans, both,
        [zero_own, zero_other, one_own, one_other], None, row_count, False, None, None, 2,
    )
    received, third, staged = lax.optimization_barrier((received, third, staged))
    level_two = reduced_solve(received, right_top[0], factor_top[0])
    two_own = sibling_values(level_two, 0)

    send = update(
        [(5, 0, 0), (5, 1, 0)], plans, both, [two_own], third, row_count, True, (0, 2), staged, 0
    )
    level_three = reduced_solve(exchange(send), right_top[1], factor_top[1])
    solved_sub = jnp.stack([level_zero, level_one])[None, None, None]
    solved_top = jnp.stack([level_two, level_three])[None, None]
    return (solved_sub, solved_top)


def solution(mesh):
    in_specs = (
        P("prow", "pcol", "zgrid", None, None, None, None),
        P("prow", "pcol", "zgrid", None, None),
        P("prow", "pcol", "zgrid", None, None),
        P("prow", "pcol", "zgrid", None),
        P("prow", "pcol", "zgrid", None, None, None),
        P("prow", "pcol", None, None, None),
        P("prow", "pcol", "zgrid", None, None, None),
        P("prow", "pcol", None, None, None),
    )
    out_specs = (P("prow", "pcol", "zgrid", None, None, None), P("prow", "pcol", None, None, None))
    return jax.shard_map(local, mesh=mesh, in_specs=in_specs, out_specs=out_specs, check_vma=False)
```

```python
import functools

import jax
import jax.numpy as jnp
from jax import lax
from jax.experimental import pallas as pl
from jax.experimental.pallas import tpu as pltpu
from jax.sharding import PartitionSpec as P

slot_group = 8
field = 10
field_mask = (1 << field) - 1
pairs = ((0, 1), (0, 2), (0, 3), (1, 2), (1, 3), (2, 3))
params = pltpu.CompilerParams(vmem_limit_bytes=24 * 1024 * 1024)
vmem = pl.BlockSpec(memory_space=pltpu.VMEM)
smem = pl.BlockSpec(memory_space=pltpu.SMEM)
hbm = pl.BlockSpec(memory_space=pltpu.HBM)
anywhere = pl.BlockSpec(memory_space=pl.ANY)


def sibling_values(value, layers):
    cols = lax.axis_size("pcol")
    depth = lax.axis_size("zgrid")
    found = []
    for k in range(cols):
        if k == 0 and layers == 0:
            found.append(value)
            continue
        moves = []
        for c in range(cols):
            for z in range(depth):
                target = ((c - k) % cols) * depth + (z - layers) % depth
                moves.append((c * depth + z, target))
        found.append(lax.ppermute(value, ("pcol", "zgrid"), moves))
    return found


def from_other_core(value):
    return lax.ppermute(value, "zgrid", [(0, 1), (1, 0)])


def in_hbm(value):
    return pltpu.with_memory_space_constraint(value, pltpu.HBM)


def plan_kernel(row_count, cols, sources_in, targets_in, counts_in, blocks, plan, staged, *scratch):
    sources, targets, counts, semaphores = scratch
    loads = [
        pltpu.make_async_copy(sources_in, sources, semaphores.at[0]),
        pltpu.make_async_copy(targets_in, targets, semaphores.at[1]),
        pltpu.make_async_copy(counts_in, counts, semaphores.at[2]),
    ]
    for load in loads:
        load.start()
    stage = pltpu.make_async_copy(blocks.at[0], staged, semaphores.at[3])
    stage.start()
    for load in loads:
        load.wait()
    me = lax.axis_index("pcol")
    my_parity = lax.axis_index("prow") & 1
    spare = (row_count // 2) << field
    list_count = 2 * len(pairs)
    for level in range(3):
        first_list = 2 * pairs.index((level, level + 1))
        steps = 3 - level
        lists = 2 * steps

        def one_slot(slot, found):
            target = targets[level, 0, slot]
            higher = [(target >= (level + j) * row_count).astype(jnp.int32) for j in range(1, steps)]
            step = sum(higher) if higher else jnp.int32(0)
            row = target - (level + step) * row_count
            kind = 2 * step + ((row & 1) ^ my_parity)
            column = sources[level, 0, slot] - me
            column = jnp.where(column < 0, column + cols, column)
            place = found[lists - 1]
            for j in range(lists - 1):
                place = jnp.where(kind == j, found[j], place)
            half_row = lax.shift_right_logical(row, 1)
            plan[first_list + kind, place] = (slot << (2 * field)) + (half_row << field) + column
            return tuple(found[j] + (kind == j).astype(jnp.int32) for j in range(lists))

        found = lax.fori_loop(0, counts[level], one_slot, (jnp.int32(0),) * lists)
        for j in range(lists):
            plan[list_count, first_list + j] = found[j]
            for extra in range(slot_group):
                plan[first_list + j, found[j] + extra] = spare
    stage.wait()


def make_plan(row_count, cols, sources, targets, counts, blocks):
    width = -(-(sources.shape[-1] + slot_group) // 128) * 128
    return pl.pallas_call(
        functools.partial(plan_kernel, row_count, cols),
        out_shape=[
            jax.ShapeDtypeStruct((16, width), jnp.int32),
            pltpu.VMEM(blocks.shape[1:], blocks.dtype),
        ],
        in_specs=[hbm] * 4,
        out_specs=[smem, vmem],
        scratch_shapes=[
            pltpu.SMEM(sources.shape, jnp.int32),
            pltpu.SMEM(targets.shape, jnp.int32),
            pltpu.SMEM(counts.shape, jnp.int32),
            pltpu.SemaphoreType.DMA((4,)),
        ],
        compiler_params=params,
    )(in_hbm(sources), in_hbm(targets), in_hbm(counts), blocks)


def fetched_levels(lists, resident):
    needed = dict.fromkeys((layer, pairs[pair][0]) for pair, layer, _ in lists)
    return [key for key in needed if key != resident]


def update_kernel(config, *refs):
    lists, parities, layer_count, groups_of_solutions, cols, half_rows, resident, stages, carries = config
    refs = list(refs)
    plans_in = [refs.pop(0) for _ in range(layer_count)]
    blocks = [refs.pop(0) for _ in range(layer_count)]
    solutions = [refs.pop(0) for _ in range(groups_of_solutions * cols)]
    resident_ref = refs.pop(0) if resident else None
    total_in = refs.pop(0) if carries else None
    out = refs.pop(0)
    next_ref = refs.pop(0) if stages else None
    chosen, total, plans, plan_semaphores, semaphores = refs[:5]
    fetched = fetched_levels(lists, resident)

    plan_loads = [
        pltpu.make_async_copy(plans_in[n], plans.at[n], plan_semaphores.at[n])
        for n in range(layer_count)
    ]
    loads = {
        key: pltpu.make_async_copy(blocks[key[0]].at[key[1]], refs[5].at[k], semaphores.at[k])
        for k, key in enumerate(fetched)
    }
    for load in plan_loads + list(loads.values()):
        load.start()
    if stages:
        stage = pltpu.make_async_copy(blocks[0].at[stages], next_ref, semaphores.at[len(fetched)])
        stage.start()

    for j, solution_ref in enumerate(solutions):
        chosen[j] = solution_ref[...]
    if carries:
        for n, parity in enumerate(parities):
            total[n, :half_rows] = total_in[parity]
    else:
        total[...] = jnp.zeros_like(total)
    for load in plan_loads:
        load.wait()

    for pair, layer, j in lists:
        key = (layer, pairs[pair][0])
        if key in loads:
            loads.pop(key).wait()
        pieces = resident_ref if key == resident else refs[5].at[fetched.index(key)]

        for n, parity in enumerate(parities):
            which = 2 * pair + parity

            def one_group(g, unused):
                for s in range(slot_group):
                    entry = plans[layer, which, g * slot_group + s]
                    place = lax.shift_right_logical(entry, field) & field_mask
                    column = j * cols + (entry & field_mask)
                    total[n, place] += jnp.dot(
                        pieces[lax.shift_right_logical(entry, 2 * field)],
                        chosen[column],
                        preferred_element_type=jnp.float32,
                    )
                return unused

            live = plans[layer, 2 * len(pairs), which]
            lax.fori_loop(0, (live + slot_group - 1) // slot_group, one_group, 0)

    for n in range(len(parities)):
        out[n] = total[n, :half_rows].astype(out.dtype)
    if stages:
        stage.wait()


def update(
    lists, parities, plans, blocks, solution_groups, total_in, half_rows, kind, resident,
    resident_blocks, stages,
):
    cols = len(solution_groups[0])
    width, sides = solution_groups[0][0].shape
    solutions = [part for group in solution_groups for part in group]
    operands = plans + blocks + solutions
    specs = [anywhere] * len(plans) + [hbm] * len(blocks) + [vmem] * len(solutions)
    for extra in (resident_blocks, total_in):
        if extra is not None:
            operands.append(extra)
            specs.append(vmem)
    fetched = fetched_levels(lists, resident)
    outs = [
        jax.ShapeDtypeStruct((len(parities), half_rows, width, sides), kind)
    ]
    if stages:
        outs.append(pltpu.VMEM(blocks[0].shape[1:], blocks[0].dtype))
    config = (
        lists, parities, len(plans), len(solution_groups), cols, half_rows, resident, stages,
        total_in is not None,
    )
    scratch = [
        pltpu.VMEM((len(solutions), width, sides), jnp.bfloat16),
        pltpu.VMEM((len(parities), half_rows + 1, width, sides), jnp.float32),
        pltpu.SMEM((len(plans),) + plans[0].shape, jnp.int32),
        pltpu.SemaphoreType.DMA((len(plans),)),
        pltpu.SemaphoreType.DMA((len(fetched) + 1,)),
    ]
    if fetched:
        scratch.append(pltpu.VMEM((len(fetched),) + blocks[0].shape[1:], jnp.bfloat16))
    found = pl.pallas_call(
        functools.partial(update_kernel, config),
        out_shape=outs,
        in_specs=specs,
        out_specs=[vmem] * len(outs),
        scratch_shapes=scratch,
        compiler_params=params,
    )(*operands)
    return found if stages else found[0]


def solve_block(inverse, residual):
    return jnp.dot(inverse, residual, preferred_element_type=jnp.float32).astype(jnp.bfloat16)


def reduced_solve(received, given, inverse):
    incoming = jnp.sum(received.astype(jnp.float32), axis=0)
    residual = (given.astype(jnp.float32) - incoming).astype(jnp.bfloat16)
    return solve_block(inverse, residual)


def to_neighbour(value):
    rows = lax.axis_size("prow")
    return lax.ppermute(value, "prow", [(row, row ^ 1) for row in range(rows)])


def pair_sum(own, received):
    return (own[0] + received[0].astype(jnp.float32)).astype(jnp.bfloat16)


def exchange(send):
    rows = lax.axis_size("prow")
    groups = [list(range(parity, rows, 2)) for parity in range(2)]
    return lax.all_to_all(send, "prow", 0, 0, tiled=True, axis_index_groups=groups)


def local(blocks, sources, targets, counts, given_sub, given_top, inverse_sub, inverse_top):
    row_count = lax.axis_size("prow")
    cols = lax.axis_size("pcol")
    levels, capacity = sources.shape[3:]
    block_set = blocks[0, 0, 0]
    right_sub = given_sub[0, 0, 0]
    factor_sub = inverse_sub[0, 0, 0]
    right_top = given_top[0, 0]
    factor_top = inverse_top[0, 0]

    level_zero = solve_block(factor_sub[0], right_sub[0])
    zero_own = sibling_values(level_zero, 0)
    block_own = in_hbm(block_set)
    plan, staged = make_plan(
        row_count, cols,
        sources.reshape(levels, 1, capacity), targets.reshape(levels, 1, capacity),
        counts.reshape(levels), block_own,
    )
    both = [block_own, in_hbm(from_other_core(block_set))]

    half_rows = row_count // 2

    def partials(lists, plans, blocks, solutions, total, resident, staged):
        send = update(
            lists, (1,), plans, blocks, solutions, total, half_rows, jnp.bfloat16, resident, staged, 0
        )
        received = to_neighbour(send)
        own = update(
            lists, (0,), plans, blocks, solutions, total, half_rows, jnp.float32, resident, staged, 0
        )
        received, own = lax.optimization_barrier((received, own))
        return pair_sum(own, received)

    send = partials([(0, 0, 0)], [plan], both[:1], [zero_own], None, (0, 0), staged)
    send, zero_sent, plan_sent = lax.optimization_barrier((send, level_zero, plan))
    received = exchange(send)
    zero_other = sibling_values(zero_sent, 1)
    plans = [plan, from_other_core(plan_sent)]
    second, staged = update(
        [(1, 0, 0), (1, 1, 1)], (0, 1), plans, both, [zero_own, zero_other], None, half_rows,
        jnp.float32, None, None, 1,
    )
    received, second, staged = lax.optimization_barrier((received, second, staged))
    level_one = reduced_solve(received, right_sub[1], factor_sub[1])
    one_own = sibling_values(level_one, 0)
    one_other = sibling_values(level_one, 1)

    send = partials(
        [(3, 0, 0), (3, 1, 1)], plans, both, [one_own, one_other], second, (0, 1), staged
    )
    send, one_own, one_other = lax.optimization_barrier((send, one_own, one_other))
    received = exchange(send)
    third, staged = update(
        [(2, 0, 0), (2, 1, 1), (4, 0, 2), (4, 1, 3)], (0, 1), plans, both,
        [zero_own, zero_other, one_own, one_other], None, half_rows, jnp.float32, None, None, 2,
    )
    received, third, staged = lax.optimization_barrier((received, third, staged))
    level_two = reduced_solve(received, right_top[0], factor_top[0])
    two_own = sibling_values(level_two, 0)

    send = partials([(5, 0, 0), (5, 1, 0)], plans, both, [two_own], third, (0, 2), staged)
    level_three = reduced_solve(exchange(send), right_top[1], factor_top[1])
    solved_sub = jnp.stack([level_zero, level_one])[None, None, None]
    solved_top = jnp.stack([level_two, level_three])[None, None]
    return (solved_sub, solved_top)


def solution(mesh):
    in_specs = (
        P("prow", "pcol", "zgrid", None, None, None, None),
        P("prow", "pcol", "zgrid", None, None),
        P("prow", "pcol", "zgrid", None, None),
        P("prow", "pcol", "zgrid", None),
        P("prow", "pcol", "zgrid", None, None, None),
        P("prow", "pcol", None, None, None),
        P("prow", "pcol", "zgrid", None, None, None),
        P("prow", "pcol", None, None, None),
    )
    out_specs = (P("prow", "pcol", "zgrid", None, None, None), P("prow", "pcol", None, None, None))
    return jax.shard_map(local, mesh=mesh, in_specs=in_specs, out_specs=out_specs, check_vma=False)
```

```python
import functools

import jax
import jax.numpy as jnp
from jax import lax
from jax.experimental import pallas as pl
from jax.experimental.pallas import tpu as pltpu
from jax.sharding import PartitionSpec as P

slot_group = 8
field = 10
field_mask = (1 << field) - 1
pairs = ((0, 1), (0, 2), (0, 3), (1, 2), (1, 3), (2, 3))
params = pltpu.CompilerParams(vmem_limit_bytes=24 * 1024 * 1024)
vmem = pl.BlockSpec(memory_space=pltpu.VMEM)
smem = pl.BlockSpec(memory_space=pltpu.SMEM)
hbm = pl.BlockSpec(memory_space=pltpu.HBM)
anywhere = pl.BlockSpec(memory_space=pl.ANY)


def sibling_values(value, layers):
    cols = lax.axis_size("pcol")
    depth = lax.axis_size("zgrid")
    found = []
    for k in range(cols):
        if k == 0 and layers == 0:
            found.append(value)
            continue
        moves = []
        for c in range(cols):
            for z in range(depth):
                target = ((c - k) % cols) * depth + (z - layers) % depth
                moves.append((c * depth + z, target))
        found.append(lax.ppermute(value, ("pcol", "zgrid"), moves))
    return found


def from_other_core(value):
    return lax.ppermute(value, "zgrid", [(0, 1), (1, 0)])


def in_hbm(value):
    return pltpu.with_memory_space_constraint(value, pltpu.HBM)


def plan_kernel(row_count, cols, sources_in, targets_in, counts_in, blocks, plan, staged, *scratch):
    sources, targets, counts, semaphores = scratch
    loads = [
        pltpu.make_async_copy(sources_in, sources, semaphores.at[0]),
        pltpu.make_async_copy(targets_in, targets, semaphores.at[1]),
        pltpu.make_async_copy(counts_in, counts, semaphores.at[2]),
    ]
    for load in loads:
        load.start()
    stage = pltpu.make_async_copy(blocks.at[0], staged, semaphores.at[3])
    stage.start()
    for load in loads:
        load.wait()
    me = lax.axis_index("pcol")
    spare = row_count << field
    for level in range(3):
        first_list = pairs.index((level, level + 1))
        lists = 3 - level

        def one_slot(slot, found):
            target = targets[level, 0, slot]
            higher = [(target >= (level + j) * row_count).astype(jnp.int32) for j in range(1, lists)]
            step = sum(higher) if higher else jnp.int32(0)
            row = target - (level + step) * row_count
            column = sources[level, 0, slot] - me
            column = jnp.where(column < 0, column + cols, column)
            place = found[lists - 1]
            for j in range(lists - 1):
                place = jnp.where(step == j, found[j], place)
            plan[first_list + step, place] = (slot << (2 * field)) + (row << field) + column
            return tuple(found[j] + (step == j).astype(jnp.int32) for j in range(lists))

        found = lax.fori_loop(0, counts[level], one_slot, (jnp.int32(0),) * lists)
        for j in range(lists):
            plan[len(pairs), first_list + j] = found[j]
            for extra in range(slot_group):
                plan[first_list + j, found[j] + extra] = spare
    stage.wait()


def make_plan(row_count, cols, sources, targets, counts, blocks):
    width = -(-(sources.shape[-1] + slot_group) // 128) * 128
    return pl.pallas_call(
        functools.partial(plan_kernel, row_count, cols),
        out_shape=[
            jax.ShapeDtypeStruct((8, width), jnp.int32),
            pltpu.VMEM(blocks.shape[1:], blocks.dtype),
        ],
        in_specs=[hbm] * 4,
        out_specs=[smem, vmem],
        scratch_shapes=[
            pltpu.SMEM(sources.shape, jnp.int32),
            pltpu.SMEM(targets.shape, jnp.int32),
            pltpu.SMEM(counts.shape, jnp.int32),
            pltpu.SemaphoreType.DMA((4,)),
        ],
        compiler_params=params,
    )(in_hbm(sources), in_hbm(targets), in_hbm(counts), blocks)


def low_lanes(value):
    return lax.broadcasted_iota(jnp.int32, value.shape, 1) < value.shape[1] // 2


def turned(value):
    return pltpu.roll(value, value.shape[1] // 2, 1)


def half_first(value):
    return jnp.where(lax.axis_index("zgrid") == 0, value, turned(value))


def packed(value):
    half = value.shape[0] // 2
    upper = value[:half]
    return jnp.where(low_lanes(upper), upper, turned(value[half:]))


def unpacked(value):
    return jnp.concatenate([value, turned(value)], axis=0)


def joined(first, second):
    first, second = unpacked(first), unpacked(second)
    return jnp.where(low_lanes(first), first, turned(second))


def fetched_levels(lists, resident):
    needed = dict.fromkeys((layer, pairs[pair][0]) for pair, layer, _ in lists)
    return [key for key in needed if key != resident]


def update_kernel(config, *refs):
    lists, layer_count, groups_of_solutions, cols, row_count, resident, stages, carries, form = config
    refs = list(refs)
    plans_in = [refs.pop(0) for _ in range(layer_count)]
    blocks = [refs.pop(0) for _ in range(layer_count)]
    solutions = [refs.pop(0) for _ in range(1 if form == "resent" else groups_of_solutions * cols)]
    resident_ref = refs.pop(0) if resident else None
    total_in = refs.pop(0) if carries else None
    out = refs.pop(0)
    next_ref = refs.pop(0) if stages else None
    chosen, total, plans, plan_semaphores, semaphores = refs[:5]
    fetched = fetched_levels(lists, resident)

    plan_loads = [
        pltpu.make_async_copy(plans_in[n], plans.at[n], plan_semaphores.at[n])
        for n in range(layer_count)
    ]
    loads = {
        key: pltpu.make_async_copy(blocks[key[0]].at[key[1]], refs[5].at[k], semaphores.at[k])
        for k, key in enumerate(fetched)
    }
    for load in plan_loads + list(loads.values()):
        load.start()
    if stages:
        stage = pltpu.make_async_copy(blocks[0].at[stages], next_ref, semaphores.at[len(fetched)])
        stage.start()

    if form == "resent":
        for j in range(cols):
            chosen[j] = unpacked(solutions[0][j].astype(jnp.float32)).astype(jnp.bfloat16)
    else:
        for j, solution_ref in enumerate(solutions):
            chosen[j] = solution_ref[...]
    if carries:
        total[:row_count] = total_in[...]
    else:
        total[...] = jnp.zeros_like(total)
    for load in plan_loads:
        load.wait()

    for pair, layer, j in lists:
        key = (layer, pairs[pair][0])
        if key in loads:
            loads.pop(key).wait()
        pieces = resident_ref if key == resident else refs[5].at[fetched.index(key)]

        def one_group(g, unused):
            for s in range(slot_group):
                entry = plans[layer, pair, g * slot_group + s]
                place = lax.shift_right_logical(entry, field) & field_mask
                column = j * cols + (entry & field_mask)
                total[place] += jnp.dot(
                    pieces[lax.shift_right_logical(entry, 2 * field)],
                    chosen[column],
                    preferred_element_type=jnp.float32,
                )
            return unused

        live = plans[layer, len(pairs), pair]
        lax.fori_loop(0, (live + slot_group - 1) // slot_group, one_group, 0)

    if form in ("plain", "summed"):
        out[...] = total[:row_count].astype(out.dtype)
    else:
        for row in range(row_count):
            value = total[row] if form == "resent" else half_first(total[row])
            if form == "turned":
                out[row] = value
            else:
                value = packed(value).astype(jnp.bfloat16)
                for k in range(out.shape[1]):
                    out[row, k] = value
    if stages:
        stage.wait()


def update(
    lists, plans, blocks, solution_groups, total_in, row_count, form, resident, resident_blocks, stages
):
    cols = lax.axis_size("pcol")
    width, sides = blocks[0].shape[-1], solution_groups[0][0].shape[-1]
    solutions = [part for group in solution_groups for part in group]
    operands = plans + blocks + solutions
    specs = [anywhere] * len(plans) + [hbm] * len(blocks) + [vmem] * len(solutions)
    for extra in (resident_blocks, total_in):
        if extra is not None:
            operands.append(extra)
            specs.append(vmem)
    fetched = fetched_levels(lists, resident)
    if form in ("sent", "resent"):
        receivers = cols if form == "sent" else lax.axis_size("zgrid")
        outs = [jax.ShapeDtypeStruct((row_count, receivers, width // 2, sides), jnp.bfloat16)]
    else:
        kind = jnp.bfloat16 if form == "plain" else jnp.float32
        outs = [jax.ShapeDtypeStruct((row_count, width, sides), kind)]
    if stages:
        outs.append(pltpu.VMEM(blocks[0].shape[1:], blocks[0].dtype))
    config = (
        lists, len(plans), len(solution_groups), cols, row_count, resident, stages,
        total_in is not None, form,
    )
    scratch = [
        pltpu.VMEM((len(solution_groups) * cols, width, sides), jnp.bfloat16),
        pltpu.VMEM((row_count + 1, width, sides), jnp.float32),
        pltpu.SMEM((len(plans),) + plans[0].shape, jnp.int32),
        pltpu.SemaphoreType.DMA((len(plans),)),
        pltpu.SemaphoreType.DMA((len(fetched) + 1,)),
    ]
    if fetched:
        scratch.append(pltpu.VMEM((len(fetched),) + blocks[0].shape[1:], jnp.bfloat16))
    found = pl.pallas_call(
        functools.partial(update_kernel, config),
        out_shape=outs,
        in_specs=specs,
        out_specs=[vmem] * len(outs),
        scratch_shapes=scratch,
        compiler_params=params,
    )(*operands)
    return found if stages else found[0]


def solve_block(inverse, residual):
    return jnp.dot(inverse, residual, preferred_element_type=jnp.float32).astype(jnp.bfloat16)


def reduced_solve(received, given, inverse):
    incoming = jnp.sum(received.astype(jnp.float32), axis=0)
    residual = (given.astype(jnp.float32) - incoming).astype(jnp.bfloat16)
    return solve_block(inverse, residual)


def exchange(send, axes):
    return lax.all_to_all(send, axes, 0, 0, tiled=True)


def row_solve_kernel(cols, received, *refs):
    givens, inverses, out = refs[:cols], refs[cols : 2 * cols], refs[-1]
    me = lax.axis_index("pcol")
    for k in range(cols):
        column = lax.rem(me + k, cols)
        incoming = received[column].astype(jnp.float32)
        for row in range(1, received.shape[0] // cols):
            incoming = incoming + received[row * cols + column].astype(jnp.float32)
        right = half_first(givens[k][0].astype(jnp.float32))
        residual = (right - unpacked(incoming)).astype(jnp.bfloat16)
        found = jnp.dot(inverses[k][0], residual, preferred_element_type=jnp.float32)
        out[k] = packed(found).astype(jnp.bfloat16)


def row_solve(received, givens, inverses):
    cols = len(givens)
    return pl.pallas_call(
        functools.partial(row_solve_kernel, cols),
        out_shape=jax.ShapeDtypeStruct((cols,) + received.shape[1:], jnp.bfloat16),
        in_specs=[vmem] * (1 + 2 * cols),
        out_specs=vmem,
        compiler_params=params,
    )(received, *givens, *inverses)


def last_solve_kernel(received, given, inverse, own, other, out):
    halves = []
    for core in range(2):
        incoming = received[core].astype(jnp.float32)
        for row in range(1, received.shape[0] // 2):
            incoming = incoming + received[2 * row + core].astype(jnp.float32)
        halves.append(incoming)
    residual = (given[1].astype(jnp.float32) - joined(*halves)).astype(jnp.bfloat16)
    found = jnp.dot(inverse[1], residual, preferred_element_type=jnp.float32)
    out[0, 0, 1] = found.astype(jnp.bfloat16)
    mine, theirs = own[0].astype(jnp.float32), other[0].astype(jnp.float32)
    first = lax.axis_index("zgrid") == 0
    whole = joined(jnp.where(first, mine, theirs), jnp.where(first, theirs, mine))
    out[0, 0, 0] = whole.astype(jnp.bfloat16)


def last_solve(received, given, inverse, own, other):
    return pl.pallas_call(
        last_solve_kernel,
        out_shape=jax.ShapeDtypeStruct((1, 1) + given.shape, jnp.bfloat16),
        in_specs=[vmem] * 5,
        out_specs=vmem,
        compiler_params=params,
    )(received, given, inverse, own, other)


def local(blocks, sources, targets, counts, given_sub, given_top, inverse_sub, inverse_top):
    row_count = lax.axis_size("prow")
    cols = lax.axis_size("pcol")
    levels, capacity = sources.shape[3:]
    block_set = blocks[0, 0, 0]
    right_sub = given_sub[0, 0, 0]
    factor_sub = inverse_sub[0, 0, 0]
    right_top = given_top[0, 0]
    factor_top = inverse_top[0, 0]

    level_zero = solve_block(factor_sub[0], right_sub[0])
    zero_own = sibling_values(level_zero, 0)
    block_own = in_hbm(block_set)
    plan, staged = make_plan(
        row_count, cols,
        sources.reshape(levels, 1, capacity), targets.reshape(levels, 1, capacity),
        counts.reshape(levels), block_own,
    )
    both = [block_own, in_hbm(from_other_core(block_set))]

    send = update(
        [(0, 0, 0)], [plan], both[:1], [zero_own], None, row_count, "plain", (0, 0), staged, 0
    )
    send, zero_sent, plan_sent = lax.optimization_barrier((send, level_zero, plan))
    received = exchange(send, "prow")
    zero_other = sibling_values(zero_sent, 1)
    plans = [plan, from_other_core(plan_sent)]
    second, staged = update(
        [(1, 0, 0), (1, 1, 1)], plans, both, [zero_own, zero_other], None, row_count, "summed",
        None, None, 1,
    )
    received, second, staged = lax.optimization_barrier((received, second, staged))
    level_one = reduced_solve(received, right_sub[1], factor_sub[1])
    one_own = sibling_values(level_one, 0)
    one_other = sibling_values(level_one, 1)

    send = update(
        [(3, 0, 0), (3, 1, 1)], plans, both, [one_own, one_other], second, row_count, "sent",
        (0, 1), staged, 0,
    )
    send, right_sent, factor_sent = lax.optimization_barrier((send, right_top, factor_top))
    received = exchange(send.reshape((-1,) + send.shape[2:]), ("prow", "pcol"))
    rights = sibling_values(right_sent, 0)
    factors = sibling_values(factor_sent, 0)
    third, staged = update(
        [(2, 0, 0), (2, 1, 1), (4, 0, 2), (4, 1, 3)], plans, both,
        [zero_own, zero_other, one_own, one_other], None, row_count, "turned", None, None, 2,
    )
    received, third, staged = lax.optimization_barrier((received, third, staged))
    level_two = row_solve(received, rights, factors)

    send = update(
        [(5, 0, 0), (5, 1, 0)], plans, both, [[level_two]], third, row_count, "resent",
        (0, 2), staged, 0,
    )
    send, two_sent = lax.optimization_barrier((send, level_two))
    received = exchange(send.reshape((-1,) + send.shape[2:]), ("prow", "zgrid"))
    two_other = from_other_core(two_sent)
    solved_top = last_solve(received, right_top, factor_top, level_two, two_other)
    solved_sub = jnp.stack([level_zero, level_one])[None, None, None]
    return (solved_sub, solved_top)


def solution(mesh):
    in_specs = (
        P("prow", "pcol", "zgrid", None, None, None, None),
        P("prow", "pcol", "zgrid", None, None),
        P("prow", "pcol", "zgrid", None, None),
        P("prow", "pcol", "zgrid", None),
        P("prow", "pcol", "zgrid", None, None, None),
        P("prow", "pcol", None, None, None),
        P("prow", "pcol", "zgrid", None, None, None),
        P("prow", "pcol", None, None, None),
    )
    out_specs = (P("prow", "pcol", "zgrid", None, None, None), P("prow", "pcol", None, None, None))
    return jax.shard_map(local, mesh=mesh, in_specs=in_specs, out_specs=out_specs, check_vma=False)
```

```python
import functools

import jax
import jax.numpy as jnp
from jax import lax
from jax.experimental import pallas as pl
from jax.experimental.pallas import tpu as pltpu
from jax.sharding import PartitionSpec as P

slot_group = 8
batch = 4
field = 10
field_mask = (1 << field) - 1
pairs = ((0, 1), (0, 2), (0, 3), (1, 2), (1, 3), (2, 3))
params = pltpu.CompilerParams(vmem_limit_bytes=24 * 1024 * 1024)
vmem = pl.BlockSpec(memory_space=pltpu.VMEM)
smem = pl.BlockSpec(memory_space=pltpu.SMEM)
hbm = pl.BlockSpec(memory_space=pltpu.HBM)
anywhere = pl.BlockSpec(memory_space=pl.ANY)


def sibling_values(value, layers):
    cols = lax.axis_size("pcol")
    depth = lax.axis_size("zgrid")
    found = []
    for k in range(cols):
        if k == 0 and layers == 0:
            found.append(value)
            continue
        moves = []
        for c in range(cols):
            for z in range(depth):
                target = ((c - k) % cols) * depth + (z - layers) % depth
                moves.append((c * depth + z, target))
        found.append(lax.ppermute(value, ("pcol", "zgrid"), moves))
    return found


def from_other_core(value):
    return lax.ppermute(value, "zgrid", [(0, 1), (1, 0)])


def in_hbm(value):
    return pltpu.with_memory_space_constraint(value, pltpu.HBM)


def plan_kernel(row_count, cols, sources_in, targets_in, counts_in, blocks, plan, staged, *scratch):
    sources, targets, counts, semaphores = scratch
    loads = [
        pltpu.make_async_copy(sources_in, sources, semaphores.at[0]),
        pltpu.make_async_copy(targets_in, targets, semaphores.at[1]),
        pltpu.make_async_copy(counts_in, counts, semaphores.at[2]),
    ]
    for load in loads:
        load.start()
    stage = pltpu.make_async_copy(blocks.at[0], staged, semaphores.at[3])
    stage.start()
    for load in loads:
        load.wait()
    me = lax.axis_index("pcol")
    spare = row_count << field
    for level in range(3):
        first_list = pairs.index((level, level + 1))
        lists = 3 - level

        def one_slot(slot, found):
            target = targets[level, 0, slot]
            higher = [(target >= (level + j) * row_count).astype(jnp.int32) for j in range(1, lists)]
            step = sum(higher) if higher else jnp.int32(0)
            row = target - (level + step) * row_count
            column = sources[level, 0, slot] - me
            column = jnp.where(column < 0, column + cols, column)
            place = found[lists - 1]
            for j in range(lists - 1):
                place = jnp.where(step == j, found[j], place)
            plan[first_list + step, place] = (slot << (2 * field)) + (row << field) + column
            return tuple(found[j] + (step == j).astype(jnp.int32) for j in range(lists))

        found = lax.fori_loop(0, counts[level], one_slot, (jnp.int32(0),) * lists)
        for j in range(lists):
            plan[len(pairs), first_list + j] = found[j]
            for extra in range(slot_group):
                plan[first_list + j, found[j] + extra] = spare
    stage.wait()


def make_plan(row_count, cols, sources, targets, counts, blocks):
    width = -(-(sources.shape[-1] + slot_group) // 128) * 128
    return pl.pallas_call(
        functools.partial(plan_kernel, row_count, cols),
        out_shape=[
            jax.ShapeDtypeStruct((8, width), jnp.int32),
            pltpu.VMEM(blocks.shape[1:], blocks.dtype),
        ],
        in_specs=[hbm] * 4,
        out_specs=[smem, vmem],
        scratch_shapes=[
            pltpu.SMEM(sources.shape, jnp.int32),
            pltpu.SMEM(targets.shape, jnp.int32),
            pltpu.SMEM(counts.shape, jnp.int32),
            pltpu.SemaphoreType.DMA((4,)),
        ],
        compiler_params=params,
    )(in_hbm(sources), in_hbm(targets), in_hbm(counts), blocks)


def exchange_order(row_count):
    return [(row + row_count // 2) % row_count for row in range(row_count)]


def fetched_levels(lists, resident):
    needed = dict.fromkeys((layer, pairs[pair][0]) for pair, layer, _ in lists)
    return [key for key in needed if key != resident]


def update_kernel(config, *refs):
    lists, layer_count, groups_of_solutions, cols, row_count, resident, stages, carries = config
    refs = list(refs)
    plans_in = [refs.pop(0) for _ in range(layer_count)]
    blocks = [refs.pop(0) for _ in range(layer_count)]
    solutions = [refs.pop(0) for _ in range(groups_of_solutions * cols)]
    resident_ref = refs.pop(0) if resident else None
    total_in = refs.pop(0) if carries else None
    out = refs.pop(0)
    next_ref = refs.pop(0) if stages else None
    chosen, total, plans, plan_semaphores, semaphores = refs[:5]
    fetched = fetched_levels(lists, resident)

    plan_loads = [
        pltpu.make_async_copy(plans_in[n], plans.at[n], plan_semaphores.at[n])
        for n in range(layer_count)
    ]
    loads = {
        key: pltpu.make_async_copy(blocks[key[0]].at[key[1]], refs[5].at[k], semaphores.at[k])
        for k, key in enumerate(fetched)
    }
    for load in plan_loads + list(loads.values()):
        load.start()
    if stages:
        stage = pltpu.make_async_copy(blocks[0].at[stages], next_ref, semaphores.at[len(fetched)])
        stage.start()

    for j, solution_ref in enumerate(solutions):
        chosen[j] = solution_ref[...]
    if carries:
        total[:row_count] = total_in[...]
    else:
        total[...] = jnp.zeros_like(total)
    for load in plan_loads:
        load.wait()

    for pair, layer, j in lists:
        key = (layer, pairs[pair][0])
        if key in loads:
            loads.pop(key).wait()
        pieces = resident_ref if key == resident else refs[5].at[fetched.index(key)]

        def one_group(g, unused):
            for first in range(0, slot_group, batch):
                entries = [plans[layer, pair, g * slot_group + first + s] for s in range(batch)]
                products = [
                    jnp.dot(
                        pieces[lax.shift_right_logical(entry, 2 * field)],
                        chosen[j * cols + (entry & field_mask)],
                        preferred_element_type=jnp.float32,
                    )
                    for entry in entries
                ]
                for entry, product in zip(entries, products):
                    total[lax.shift_right_logical(entry, field) & field_mask] += product
            return unused

        live = plans[layer, len(pairs), pair]
        lax.fori_loop(0, (live + slot_group - 1) // slot_group, one_group, 0)

    if out.dtype == jnp.bfloat16:
        for k, row in enumerate(exchange_order(row_count)):
            out[k] = total[row].astype(jnp.bfloat16)
    else:
        out[...] = total[:row_count]
    if stages:
        stage.wait()


def update(
    lists, plans, blocks, solution_groups, total_in, row_count, sends, resident, resident_blocks, stages
):
    cols = len(solution_groups[0])
    width, sides = solution_groups[0][0].shape
    solutions = [part for group in solution_groups for part in group]
    operands = plans + blocks + solutions
    specs = [anywhere] * len(plans) + [hbm] * len(blocks) + [vmem] * len(solutions)
    for extra in (resident_blocks, total_in):
        if extra is not None:
            operands.append(extra)
            specs.append(vmem)
    fetched = fetched_levels(lists, resident)
    outs = [
        jax.ShapeDtypeStruct((row_count, width, sides), jnp.bfloat16 if sends else jnp.float32)
    ]
    if stages:
        outs.append(pltpu.VMEM(blocks[0].shape[1:], blocks[0].dtype))
    config = (
        lists, len(plans), len(solution_groups), cols, row_count, resident, stages,
        total_in is not None,
    )
    scratch = [
        pltpu.VMEM((len(solutions), width, sides), jnp.bfloat16),
        pltpu.VMEM((row_count + 1, width, sides), jnp.float32),
        pltpu.SMEM((len(plans),) + plans[0].shape, jnp.int32),
        pltpu.SemaphoreType.DMA((len(plans),)),
        pltpu.SemaphoreType.DMA((len(fetched) + 1,)),
    ]
    if fetched:
        scratch.append(pltpu.VMEM((len(fetched),) + blocks[0].shape[1:], jnp.bfloat16))
    found = pl.pallas_call(
        functools.partial(update_kernel, config),
        out_shape=outs,
        in_specs=specs,
        out_specs=[vmem] * len(outs),
        scratch_shapes=scratch,
        compiler_params=params,
    )(*operands)
    return found if stages else found[0]


def solve_block(inverse, residual):
    return jnp.dot(inverse, residual, preferred_element_type=jnp.float32).astype(jnp.bfloat16)


def reduced_solve(received, given, inverse):
    incoming = jnp.sum(received.astype(jnp.float32), axis=0)
    residual = (given.astype(jnp.float32) - incoming).astype(jnp.bfloat16)
    return solve_block(inverse, residual)


def exchange(send):
    order = exchange_order(lax.axis_size("prow"))
    return lax.all_to_all(send, "prow", 0, 0, tiled=True, axis_index_groups=[order])


def local(blocks, sources, targets, counts, given_sub, given_top, inverse_sub, inverse_top):
    row_count = lax.axis_size("prow")
    cols = lax.axis_size("pcol")
    levels, capacity = sources.shape[3:]
    block_set = blocks[0, 0, 0]
    right_sub = given_sub[0, 0, 0]
    factor_sub = inverse_sub[0, 0, 0]
    right_top = given_top[0, 0]
    factor_top = inverse_top[0, 0]

    level_zero = solve_block(factor_sub[0], right_sub[0])
    zero_own = sibling_values(level_zero, 0)
    block_own = in_hbm(block_set)
    plan, staged = make_plan(
        row_count, cols,
        sources.reshape(levels, 1, capacity), targets.reshape(levels, 1, capacity),
        counts.reshape(levels), block_own,
    )
    both = [block_own, in_hbm(from_other_core(block_set))]

    send = update(
        [(0, 0, 0)], [plan], both[:1], [zero_own], None, row_count, True, (0, 0), staged, 0
    )
    send, zero_sent, plan_sent = lax.optimization_barrier((send, level_zero, plan))
    received = exchange(send)
    zero_other = sibling_values(zero_sent, 1)
    plans = [plan, from_other_core(plan_sent)]
    second, staged = update(
        [(1, 0, 0), (1, 1, 1)], plans, both, [zero_own, zero_other], None, row_count, False,
        None, None, 1,
    )
    received, second, staged = lax.optimization_barrier((received, second, staged))
    level_one = reduced_solve(received, right_sub[1], factor_sub[1])
    one_own = sibling_values(level_one, 0)
    one_other = sibling_values(level_one, 1)

    send = update(
        [(3, 0, 0), (3, 1, 1)], plans, both, [one_own, one_other], second, row_count, True,
        (0, 1), staged, 0,
    )
    received = exchange(send)
    third, staged = update(
        [(2, 0, 0), (2, 1, 1), (4, 0, 2), (4, 1, 3)], plans, both,
        [zero_own, zero_other, one_own, one_other], None, row_count, False, None, None, 2,
    )
    received, third, staged = lax.optimization_barrier((received, third, staged))
    level_two = reduced_solve(received, right_top[0], factor_top[0])
    two_own = sibling_values(level_two, 0)

    send = update(
        [(5, 0, 0), (5, 1, 0)], plans, both, [two_own], third, row_count, True, (0, 2), staged, 0
    )
    level_three = reduced_solve(exchange(send), right_top[1], factor_top[1])
    solved_sub = jnp.stack([level_zero, level_one])[None, None, None]
    solved_top = jnp.stack([level_two, level_three])[None, None]
    return (solved_sub, solved_top)


def solution(mesh):
    in_specs = (
        P("prow", "pcol", "zgrid", None, None, None, None),
        P("prow", "pcol", "zgrid", None, None),
        P("prow", "pcol", "zgrid", None, None),
        P("prow", "pcol", "zgrid", None),
        P("prow", "pcol", "zgrid", None, None, None),
        P("prow", "pcol", None, None, None),
        P("prow", "pcol", "zgrid", None, None, None),
        P("prow", "pcol", None, None, None),
    )
    out_specs = (P("prow", "pcol", "zgrid", None, None, None), P("prow", "pcol", None, None, None))
    return jax.shard_map(local, mesh=mesh, in_specs=in_specs, out_specs=out_specs, check_vma=False)
```

```python
import functools

import jax
import jax.numpy as jnp
from jax import lax
from jax.experimental import pallas as pl
from jax.experimental.pallas import tpu as pltpu
from jax.sharding import PartitionSpec as P

slot_group = 8
batch = 4
field = 10
field_mask = (1 << field) - 1
pairs = ((0, 1), (0, 2), (0, 3), (1, 2), (1, 3), (2, 3))
params = pltpu.CompilerParams(vmem_limit_bytes=24 * 1024 * 1024)
vmem = pl.BlockSpec(memory_space=pltpu.VMEM)
smem = pl.BlockSpec(memory_space=pltpu.SMEM)
hbm = pl.BlockSpec(memory_space=pltpu.HBM)
anywhere = pl.BlockSpec(memory_space=pl.ANY)


def sibling_values(value, layers):
    cols = lax.axis_size("pcol")
    depth = lax.axis_size("zgrid")
    found = []
    for k in range(cols):
        if k == 0 and layers == 0:
            found.append(value)
            continue
        moves = []
        for c in range(cols):
            for z in range(depth):
                target = ((c - k) % cols) * depth + (z - layers) % depth
                moves.append((c * depth + z, target))
        found.append(lax.ppermute(value, ("pcol", "zgrid"), moves))
    return found


def from_other_core(value):
    return lax.ppermute(value, "zgrid", [(0, 1), (1, 0)])


def in_hbm(value):
    return pltpu.with_memory_space_constraint(value, pltpu.HBM)


def plan_kernel(row_count, cols, sources_in, targets_in, counts_in, blocks, plan, staged, *scratch):
    sources, targets, counts, semaphores = scratch
    loads = [
        pltpu.make_async_copy(sources_in, sources, semaphores.at[0]),
        pltpu.make_async_copy(targets_in, targets, semaphores.at[1]),
        pltpu.make_async_copy(counts_in, counts, semaphores.at[2]),
    ]
    for load in loads:
        load.start()
    stage = pltpu.make_async_copy(blocks.at[0], staged, semaphores.at[3])
    stage.start()
    me = lax.axis_index("pcol")
    lists = len(pairs) * cols
    for which in range(lists):
        plan[lists, which] = 0
    for load in loads:
        load.wait()
    for level in range(3):

        def one_slot(slot, unused):
            target = targets[level, 0, slot]
            pair = jnp.int32(pairs.index((level, level + 1)))
            row = target - level * row_count
            for higher in range(level + 1, 3):
                above = (target >= higher * row_count).astype(jnp.int32)
                pair = pair + above
                row = row - above * row_count
            column = sources[level, 0, slot] - me
            column = jnp.where(column < 0, column + cols, column)
            which = pair * cols + column
            place = plan[lists, which]
            plan[which, place] = (slot << field) + row
            plan[lists, which] = place + 1
            return unused

        lax.fori_loop(0, counts[level], one_slot, 0)
    for which in range(lists):
        found = plan[lists, which]
        for extra in range(slot_group):
            plan[which, found + extra] = row_count
    stage.wait()


def make_plan(row_count, cols, sources, targets, counts, blocks):
    width = -(-(sources.shape[-1] + slot_group) // 128) * 128
    rows = -(-(len(pairs) * cols + 1) // 8) * 8
    return pl.pallas_call(
        functools.partial(plan_kernel, row_count, cols),
        out_shape=[
            jax.ShapeDtypeStruct((rows, width), jnp.int32),
            pltpu.VMEM(blocks.shape[1:], blocks.dtype),
        ],
        in_specs=[hbm] * 4,
        out_specs=[smem, vmem],
        scratch_shapes=[
            pltpu.SMEM(sources.shape, jnp.int32),
            pltpu.SMEM(targets.shape, jnp.int32),
            pltpu.SMEM(counts.shape, jnp.int32),
            pltpu.SemaphoreType.DMA((4,)),
        ],
        compiler_params=params,
    )(in_hbm(sources), in_hbm(targets), in_hbm(counts), blocks)


def exchange_order(row_count):
    return [(row + row_count // 2) % row_count for row in range(row_count)]


def needed_levels(lists):
    return list(dict.fromkeys((layer, pairs[pair][0]) for pair, _, layer, _ in lists))


def update_kernel(config, *refs):
    lists, layer_count, solution_count, cols, row_count, resident, stages, carries = config
    refs = list(refs)
    plans_in = [refs.pop(0) for _ in range(layer_count)]
    blocks = [refs.pop(0) for _ in range(layer_count)]
    solutions = [refs.pop(0) for _ in range(solution_count)]
    places = {key: refs.pop(0) for key in resident}
    total_in = refs.pop(0) if carries else None
    out = refs.pop(0)
    next_ref = refs.pop(0) if stages else None
    total, plans, plan_semaphores, semaphores = refs[:4]

    plan_loads = [
        pltpu.make_async_copy(plans_in[n], plans.at[n], plan_semaphores.at[n])
        for n in range(layer_count)
    ]
    loads = {}
    if stages:
        places[stages] = next_ref
        loads[stages] = pltpu.make_async_copy(
            blocks[stages[0]].at[stages[1]], next_ref, semaphores.at[0]
        )
    for key in needed_levels(lists):
        if key not in places:
            places[key] = refs[4].at[len(loads) - (1 if stages else 0)]
            loads[key] = pltpu.make_async_copy(
                blocks[key[0]].at[key[1]], places[key], semaphores.at[len(loads)]
            )
    for load in plan_loads + list(loads.values()):
        load.start()

    if carries:
        total[:row_count] = total_in[...]
    else:
        total[...] = jnp.zeros_like(total)
    for load in plan_loads:
        load.wait()

    for pair, further, layer, j in lists:
        key = (layer, pairs[pair][0])
        if key in loads:
            loads.pop(key).wait()
        pieces = places[key]
        width = pieces.shape[1]
        which = pair * cols + further

        def one_group(g, unused):
            for first in range(0, slot_group, batch):
                entries = [plans[layer, which, g * slot_group + first + s] for s in range(batch)]
                left = [pieces[lax.shift_right_logical(entry, field)] for entry in entries]
                product = jnp.dot(
                    jnp.concatenate(left, axis=0),
                    solutions[j][...],
                    preferred_element_type=jnp.float32,
                )
                for s, entry in enumerate(entries):
                    total[entry & field_mask] += product[s * width : (s + 1) * width]
            return unused

        live = plans[layer, len(pairs) * cols, which]
        lax.fori_loop(0, (live + slot_group - 1) // slot_group, one_group, 0)

    if out.dtype == jnp.bfloat16:
        for k, row in enumerate(exchange_order(row_count)):
            out[k] = total[row].astype(jnp.bfloat16)
    else:
        out[...] = total[:row_count]
    for load in loads.values():
        load.wait()


def update(lists, plans, blocks, solutions, total_in, row_count, sends, resident, stages):
    cols = lax.axis_size("pcol")
    width, sides = solutions[0].shape
    operands = plans + blocks + solutions + list(resident.values())
    specs = [anywhere] * len(plans) + [hbm] * len(blocks)
    specs += [vmem] * (len(solutions) + len(resident))
    if total_in is not None:
        operands.append(total_in)
        specs.append(vmem)
    kind = jnp.bfloat16 if sends else jnp.float32
    outs = [jax.ShapeDtypeStruct((row_count, width, sides), kind)]
    if stages:
        outs.append(pltpu.VMEM(blocks[0].shape[1:], blocks[0].dtype))
    fetched = [key for key in needed_levels(lists) if key not in resident and key != stages]
    config = (
        lists, len(plans), len(solutions), cols, row_count, tuple(resident), stages,
        total_in is not None,
    )
    scratch = [
        pltpu.VMEM((row_count + 1, width, sides), jnp.float32),
        pltpu.SMEM((len(plans),) + plans[0].shape, jnp.int32),
        pltpu.SemaphoreType.DMA((len(plans),)),
        pltpu.SemaphoreType.DMA((len(fetched) + 1,)),
    ]
    if fetched:
        scratch.append(pltpu.VMEM((len(fetched),) + blocks[0].shape[1:], jnp.bfloat16))
    found = pl.pallas_call(
        functools.partial(update_kernel, config),
        out_shape=outs,
        in_specs=specs,
        out_specs=[vmem] * len(outs),
        scratch_shapes=scratch,
        compiler_params=params,
    )(*operands)
    return found if stages else found[0]


def solve_block(inverse, residual):
    return jnp.dot(inverse, residual, preferred_element_type=jnp.float32).astype(jnp.bfloat16)


def reduced_solve(received, given, inverse):
    incoming = jnp.sum(received.astype(jnp.float32), axis=0)
    residual = (given.astype(jnp.float32) - incoming).astype(jnp.bfloat16)
    return solve_block(inverse, residual)


def exchange(send):
    order = exchange_order(lax.axis_size("prow"))
    return lax.all_to_all(send, "prow", 0, 0, tiled=True, axis_index_groups=[order])


def local(blocks, sources, targets, counts, given_sub, given_top, inverse_sub, inverse_top):
    row_count = lax.axis_size("prow")
    cols = lax.axis_size("pcol")
    levels, capacity = sources.shape[3:]
    block_set = blocks[0, 0, 0]
    right_sub = given_sub[0, 0, 0]
    factor_sub = inverse_sub[0, 0, 0]
    right_top = given_top[0, 0]
    factor_top = inverse_top[0, 0]

    level_zero = solve_block(factor_sub[0], right_sub[0])
    zero_own = sibling_values(level_zero, 0)
    block_own = in_hbm(block_set)
    plan, staged = make_plan(
        row_count, cols,
        sources.reshape(levels, 1, capacity), targets.reshape(levels, 1, capacity),
        counts.reshape(levels), block_own,
    )
    both = [block_own, in_hbm(from_other_core(block_set))]

    every = range(cols)

    def lists_of(pair, layer, first, columns=every):
        return [(pair, k, layer, first + k) for k in columns]

    send = update(
        lists_of(0, 0, 0), [plan], both[:1], zero_own, None, row_count, True, {(0, 0): staged}, None
    )
    send, zero_sent, plan_sent = lax.optimization_barrier((send, level_zero, plan))
    received = exchange(send)
    zero_other = sibling_values(zero_sent, 1)
    plans = [plan, from_other_core(plan_sent)]
    second, staged = update(
        lists_of(1, 0, 0) + lists_of(1, 1, cols), plans, both, zero_own + zero_other, None,
        row_count, False, {}, (0, 1),
    )
    received, second, staged = lax.optimization_barrier((received, second, staged))
    level_one = reduced_solve(received, right_sub[1], factor_sub[1])
    one_own = sibling_values(level_one, 0)
    one_other = sibling_values(level_one, 1)

    resident = {(0, 1): staged}
    second, resident[(1, 1)] = update(
        lists_of(3, 0, 0, [0]), plans, both, [level_one], second, row_count, False, resident, (1, 1)
    )
    send = update(
        lists_of(3, 0, 0, every[1:]) + lists_of(3, 1, cols), plans, both, one_own + one_other, second,
        row_count, True, resident, None,
    )
    send, one_own, one_other = lax.optimization_barrier((send, one_own, one_other))
    received = exchange(send)
    third, staged = update(
        lists_of(2, 0, 0) + lists_of(2, 1, cols) + lists_of(4, 0, 2 * cols) + lists_of(4, 1, 3 * cols),
        plans, both, zero_own + zero_other + one_own + one_other, None, row_count, False, {}, (0, 2),
    )
    received, third, staged = lax.optimization_barrier((received, third, staged))
    level_two = reduced_solve(received, right_top[0], factor_top[0])
    two_own = sibling_values(level_two, 0)

    resident = {(0, 2): staged}
    third, resident[(1, 2)] = update(
        lists_of(5, 0, 0, [0]) + lists_of(5, 1, 0, [0]), plans, both, [level_two], third, row_count,
        False, resident, (1, 2),
    )
    send = update(
        lists_of(5, 0, 0, every[1:]) + lists_of(5, 1, 0, every[1:]), plans, both, two_own, third,
        row_count, True, resident, None,
    )
    level_three = reduced_solve(exchange(send), right_top[1], factor_top[1])
    solved_sub = jnp.stack([level_zero, level_one])[None, None, None]
    solved_top = jnp.stack([level_two, level_three])[None, None]
    return (solved_sub, solved_top)


def solution(mesh):
    in_specs = (
        P("prow", "pcol", "zgrid", None, None, None, None),
        P("prow", "pcol", "zgrid", None, None),
        P("prow", "pcol", "zgrid", None, None),
        P("prow", "pcol", "zgrid", None),
        P("prow", "pcol", "zgrid", None, None, None),
        P("prow", "pcol", None, None, None),
        P("prow", "pcol", "zgrid", None, None, None),
        P("prow", "pcol", None, None, None),
    )
    out_specs = (P("prow", "pcol", "zgrid", None, None, None), P("prow", "pcol", None, None, None))
    return jax.shard_map(local, mesh=mesh, in_specs=in_specs, out_specs=out_specs, check_vma=False)
```

```python
import functools

import jax
import jax.numpy as jnp
from jax import lax
from jax.experimental import pallas as pl
from jax.experimental.pallas import tpu as pltpu
from jax.sharding import PartitionSpec as P

slot_group = 8
batch = 4
field = 10
field_mask = (1 << field) - 1
pairs = ((0, 1), (0, 2), (0, 3), (1, 2), (1, 3), (2, 3), (2, 3))
count_row = len(pairs)
params = pltpu.CompilerParams(vmem_limit_bytes=24 * 1024 * 1024)
vmem = pl.BlockSpec(memory_space=pltpu.VMEM)
smem = pl.BlockSpec(memory_space=pltpu.SMEM)
hbm = pl.BlockSpec(memory_space=pltpu.HBM)
anywhere = pl.BlockSpec(memory_space=pl.ANY)


def sibling_values(value, layers):
    cols = lax.axis_size("pcol")
    depth = lax.axis_size("zgrid")
    found = []
    for k in range(cols):
        if k == 0 and layers == 0:
            found.append(value)
            continue
        moves = []
        for c in range(cols):
            for z in range(depth):
                target = ((c - k) % cols) * depth + (z - layers) % depth
                moves.append((c * depth + z, target))
        found.append(lax.ppermute(value, ("pcol", "zgrid"), moves))
    return found


def from_other_core(value):
    return lax.ppermute(value, "zgrid", [(0, 1), (1, 0)])


def in_hbm(value):
    return pltpu.with_memory_space_constraint(value, pltpu.HBM)


def plan_kernel(row_count, cols, sources_in, targets_in, counts_in, blocks, plan, staged, *scratch):
    sources, targets, counts, semaphores = scratch
    loads = [
        pltpu.make_async_copy(sources_in, sources, semaphores.at[0]),
        pltpu.make_async_copy(targets_in, targets, semaphores.at[1]),
        pltpu.make_async_copy(counts_in, counts, semaphores.at[2]),
    ]
    for load in loads:
        load.start()
    stage = pltpu.make_async_copy(blocks.at[0], staged, semaphores.at[3])
    stage.start()
    for load in loads:
        load.wait()
    me = lax.axis_index("pcol")
    spare = row_count << field
    for level in range(3):
        first_list = pairs.index((level, level + 1))
        steps = 3 - level
        lists = max(steps, 2)

        def one_slot(slot, found):
            target = targets[level, 0, slot]
            higher = [(target >= (level + j) * row_count).astype(jnp.int32) for j in range(1, steps)]
            step = sum(higher) if higher else jnp.int32(0)
            row = target - (level + step) * row_count
            column = sources[level, 0, slot] - me
            column = jnp.where(column < 0, column + cols, column)
            kind = step if steps > 1 else (column > 0).astype(jnp.int32)
            place = found[lists - 1]
            for j in range(lists - 1):
                place = jnp.where(kind == j, found[j], place)
            plan[first_list + kind, place] = (slot << (2 * field)) + (row << field) + column
            return tuple(found[j] + (kind == j).astype(jnp.int32) for j in range(lists))

        found = lax.fori_loop(0, counts[level], one_slot, (jnp.int32(0),) * lists)
        for j in range(lists):
            plan[count_row, first_list + j] = found[j]
            for extra in range(slot_group):
                plan[first_list + j, found[j] + extra] = spare
    stage.wait()


def make_plan(row_count, cols, sources, targets, counts, blocks):
    width = -(-(sources.shape[-1] + slot_group) // 128) * 128
    return pl.pallas_call(
        functools.partial(plan_kernel, row_count, cols),
        out_shape=[
            jax.ShapeDtypeStruct((8, width), jnp.int32),
            pltpu.VMEM(blocks.shape[1:], blocks.dtype),
        ],
        in_specs=[hbm] * 4,
        out_specs=[smem, vmem],
        scratch_shapes=[
            pltpu.SMEM(sources.shape, jnp.int32),
            pltpu.SMEM(targets.shape, jnp.int32),
            pltpu.SMEM(counts.shape, jnp.int32),
            pltpu.SemaphoreType.DMA((4,)),
        ],
        compiler_params=params,
    )(in_hbm(sources), in_hbm(targets), in_hbm(counts), blocks)


def exchange_order(row_count):
    return [(row + row_count // 2) % row_count for row in range(row_count)]


def fetched_levels(lists, resident):
    needed = dict.fromkeys((layer, pairs[pair][0]) for pair, layer, _ in lists)
    return [key for key in needed if key not in resident]


def update_kernel(config, *refs):
    lists, layer_count, groups_of_solutions, cols, row_count, resident, stages, carries = config
    refs = list(refs)
    plans_in = [refs.pop(0) for _ in range(layer_count)]
    blocks = [refs.pop(0) for _ in range(layer_count)]
    solutions = [refs.pop(0) for _ in range(groups_of_solutions * cols)]
    places = {key: refs.pop(0) for key in resident}
    total_in = refs.pop(0) if carries else None
    out = refs.pop(0)
    next_ref = refs.pop(0) if stages else None
    chosen, total, plans, plan_semaphores, semaphores = refs[:5]
    fetched = fetched_levels(lists, resident + ((stages,) if stages else ()))

    plan_loads = [
        pltpu.make_async_copy(plans_in[n], plans.at[n], plan_semaphores.at[n])
        for n in range(layer_count)
    ]
    loads = {
        key: pltpu.make_async_copy(blocks[key[0]].at[key[1]], refs[5].at[k], semaphores.at[k])
        for k, key in enumerate(fetched)
    }
    for load in plan_loads + list(loads.values()):
        load.start()
    places.update({key: refs[5].at[k] for k, key in enumerate(fetched)})
    if stages:
        places[stages] = next_ref
        loads[stages] = pltpu.make_async_copy(
            blocks[stages[0]].at[stages[1]], next_ref, semaphores.at[len(fetched)]
        )
        loads[stages].start()

    for j, solution_ref in enumerate(solutions):
        chosen[j] = solution_ref[...]
    if carries:
        total[:row_count] = total_in[...]
    else:
        total[...] = jnp.zeros_like(total)
    for load in plan_loads:
        load.wait()

    for pair, layer, j in lists:
        key = (layer, pairs[pair][0])
        if key in loads:
            loads.pop(key).wait()
        pieces = places[key]

        def one_group(g, unused):
            for first in range(0, slot_group, batch):
                entries = [plans[layer, pair, g * slot_group + first + s] for s in range(batch)]
                products = [
                    jnp.dot(
                        pieces[lax.shift_right_logical(entry, 2 * field)],
                        chosen[j * cols + (entry & field_mask)],
                        preferred_element_type=jnp.float32,
                    )
                    for entry in entries
                ]
                for entry, product in zip(entries, products):
                    total[lax.shift_right_logical(entry, field) & field_mask] += product
            return unused

        live = plans[layer, count_row, pair]
        lax.fori_loop(0, (live + slot_group - 1) // slot_group, one_group, 0)

    if out.dtype == jnp.bfloat16:
        for k, row in enumerate(exchange_order(row_count)):
            out[k] = total[row].astype(jnp.bfloat16)
    else:
        out[...] = total[:row_count]
    for load in loads.values():
        load.wait()


def update(
    lists, plans, blocks, solution_groups, total_in, row_count, sends, resident, stages
):
    cols = len(solution_groups[0])
    width, sides = solution_groups[0][0].shape
    solutions = [part for group in solution_groups for part in group]
    operands = plans + blocks + solutions
    specs = [anywhere] * len(plans) + [hbm] * len(blocks) + [vmem] * len(solutions)
    for extra in list(resident.values()) + [total_in]:
        if extra is not None:
            operands.append(extra)
            specs.append(vmem)
    fetched = fetched_levels(lists, tuple(resident) + ((stages,) if stages else ()))
    shape = (row_count, width, sides)
    outs = [pltpu.VMEM(shape, jnp.bfloat16) if sends else jax.ShapeDtypeStruct(shape, jnp.float32)]
    if stages:
        outs.append(pltpu.VMEM(blocks[0].shape[1:], blocks[0].dtype))
    config = (
        lists, len(plans), len(solution_groups), cols, row_count, tuple(resident), stages,
        total_in is not None,
    )
    scratch = [
        pltpu.VMEM((len(solutions), width, sides), jnp.bfloat16),
        pltpu.VMEM((row_count + 1, width, sides), jnp.float32),
        pltpu.SMEM((len(plans),) + plans[0].shape, jnp.int32),
        pltpu.SemaphoreType.DMA((len(plans),)),
        pltpu.SemaphoreType.DMA((len(fetched) + 1,)),
    ]
    if fetched:
        scratch.append(pltpu.VMEM((len(fetched),) + blocks[0].shape[1:], jnp.bfloat16))
    found = pl.pallas_call(
        functools.partial(update_kernel, config),
        out_shape=outs,
        in_specs=specs,
        out_specs=[vmem] * len(outs),
        scratch_shapes=scratch,
        compiler_params=params,
    )(*operands)
    return found if stages else found[0]


def solve_block(inverse, residual):
    return jnp.dot(inverse, residual, preferred_element_type=jnp.float32).astype(jnp.bfloat16)


def reduced_solve(received, given, inverse):
    incoming = jnp.sum(received.astype(jnp.float32), axis=0)
    residual = (given.astype(jnp.float32) - incoming).astype(jnp.bfloat16)
    return solve_block(inverse, residual)


def exchange(send):
    order = exchange_order(lax.axis_size("prow"))
    return lax.all_to_all(send, "prow", 0, 0, tiled=True, axis_index_groups=[order])


def local(blocks, sources, targets, counts, given_sub, given_top, inverse_sub, inverse_top):
    row_count = lax.axis_size("prow")
    cols = lax.axis_size("pcol")
    levels, capacity = sources.shape[3:]
    block_set = blocks[0, 0, 0]
    right_sub = given_sub[0, 0, 0]
    factor_sub = inverse_sub[0, 0, 0]
    right_top = given_top[0, 0]
    factor_top = inverse_top[0, 0]

    level_zero = solve_block(factor_sub[0], right_sub[0])
    zero_own = sibling_values(level_zero, 0)
    block_own = in_hbm(block_set)
    block_sent, level_zero = lax.optimization_barrier((block_set, level_zero))
    plan, staged = make_plan(
        row_count, cols,
        sources.reshape(levels, 1, capacity), targets.reshape(levels, 1, capacity),
        counts.reshape(levels), block_own,
    )
    both = [block_own, in_hbm(from_other_core(block_sent))]

    send = update(
        [(0, 0, 0)], [plan], both[:1], [zero_own], None, row_count, True, {(0, 0): staged}, None
    )
    send, zero_sent, plan_sent = lax.optimization_barrier((send, level_zero, plan))
    received = exchange(send)
    zero_other = sibling_values(zero_sent, 1)
    plans = [plan, from_other_core(plan_sent)]
    second, staged = update(
        [(1, 0, 0), (1, 1, 1)], plans, both, [zero_own, zero_other], None, row_count, False,
        {}, (0, 1),
    )
    received, second, staged = lax.optimization_barrier((received, second, staged))
    level_one = reduced_solve(received, right_sub[1], factor_sub[1])
    one_own = sibling_values(level_one, 0)
    one_other = sibling_values(level_one, 1)

    send = update(
        [(3, 0, 0), (3, 1, 1)], plans, both, [one_own, one_other], second, row_count, True,
        {(0, 1): staged}, None,
    )
    received = exchange(send)
    third, staged = update(
        [(2, 0, 0), (2, 1, 1), (4, 0, 2), (4, 1, 3)], plans, both,
        [zero_own, zero_other, one_own, one_other], None, row_count, False, {}, (0, 2),
    )
    received, third, staged = lax.optimization_barrier((received, third, staged))
    level_two = reduced_solve(received, right_top[0], factor_top[0])
    two_own = sibling_values(level_two, 0)

    resident = {(0, 2): staged}
    third, resident[(1, 2)] = update(
        [(5, 0, 0), (5, 1, 0)], plans, both, [[level_two] * cols], third, row_count, False, resident,
        (1, 2),
    )
    send = update(
        [(6, 0, 0), (6, 1, 0)], plans, both, [two_own], third, row_count, True, resident, None
    )
    send, level_zero, level_one = lax.optimization_barrier((send, level_zero, level_one))
    level_three = reduced_solve(exchange(send), right_top[1], factor_top[1])
    solved_sub = jnp.stack([level_zero, level_one])[None, None, None]
    solved_top = jnp.stack([level_two, level_three])[None, None]
    return (solved_sub, solved_top)


def solution(mesh):
    in_specs = (
        P("prow", "pcol", "zgrid", None, None, None, None),
        P("prow", "pcol", "zgrid", None, None),
        P("prow", "pcol", "zgrid", None, None),
        P("prow", "pcol", "zgrid", None),
        P("prow", "pcol", "zgrid", None, None, None),
        P("prow", "pcol", None, None, None),
        P("prow", "pcol", "zgrid", None, None, None),
        P("prow", "pcol", None, None, None),
    )
    out_specs = (P("prow", "pcol", "zgrid", None, None, None), P("prow", "pcol", None, None, None))
    return jax.shard_map(local, mesh=mesh, in_specs=in_specs, out_specs=out_specs, check_vma=False)
```

```python
import functools

import jax
import jax.numpy as jnp
from jax import lax
from jax.experimental import pallas as pl
from jax.experimental.pallas import tpu as pltpu
from jax.sharding import PartitionSpec as P

slot_group = 8
batch = 4
field = 10
field_mask = (1 << field) - 1
pairs = ((0, 1), (0, 2), (0, 3), (1, 2), (1, 3), (2, 3), (2, 3))
count_row = len(pairs)
params = pltpu.CompilerParams(vmem_limit_bytes=24 * 1024 * 1024)
vmem = pl.BlockSpec(memory_space=pltpu.VMEM)
smem = pl.BlockSpec(memory_space=pltpu.SMEM)
hbm = pl.BlockSpec(memory_space=pltpu.HBM)
anywhere = pl.BlockSpec(memory_space=pl.ANY)


def sibling_values(value, layers):
    cols = lax.axis_size("pcol")
    depth = lax.axis_size("zgrid")
    found = []
    for k in range(cols):
        if k == 0 and layers == 0:
            found.append(value)
            continue
        moves = []
        for c in range(cols):
            for z in range(depth):
                target = ((c - k) % cols) * depth + (z - layers) % depth
                moves.append((c * depth + z, target))
        found.append(lax.ppermute(value, ("pcol", "zgrid"), moves))
    return found


def from_other_core(value):
    return lax.ppermute(value, "zgrid", [(0, 1), (1, 0)])


def in_hbm(value):
    return pltpu.with_memory_space_constraint(value, pltpu.HBM)


def plan_kernel(row_count, cols, sources_in, targets_in, counts_in, blocks, plan, kept, staged, *scratch):
    sources, targets, counts, semaphores = scratch
    loads = [
        pltpu.make_async_copy(sources_in, sources, semaphores.at[0]),
        pltpu.make_async_copy(targets_in, targets, semaphores.at[1]),
        pltpu.make_async_copy(counts_in, counts, semaphores.at[2]),
    ]
    for load in loads:
        load.start()
    stage = pltpu.make_async_copy(blocks.at[0], staged, semaphores.at[3])
    stage.start()
    for load in loads:
        load.wait()
    me = lax.axis_index("pcol")
    spare = row_count << field
    for level in range(3):
        first_list = pairs.index((level, level + 1))
        steps = 3 - level
        lists = max(steps, 2)

        def one_slot(slot, found):
            target = targets[level, 0, slot]
            higher = [(target >= (level + j) * row_count).astype(jnp.int32) for j in range(1, steps)]
            step = sum(higher) if higher else jnp.int32(0)
            row = target - (level + step) * row_count
            column = sources[level, 0, slot] - me
            column = jnp.where(column < 0, column + cols, column)
            kind = step if steps > 1 else (column > 0).astype(jnp.int32)
            place = found[lists - 1]
            for j in range(lists - 1):
                place = jnp.where(kind == j, found[j], place)
            entry = (slot << (2 * field)) + (row << field) + column
            plan[first_list + kind, place] = entry
            kept[first_list + kind, place] = entry
            return tuple(found[j] + (kind == j).astype(jnp.int32) for j in range(lists))

        found = lax.fori_loop(0, counts[level], one_slot, (jnp.int32(0),) * lists)
        for j in range(lists):
            plan[count_row, first_list + j] = found[j]
            kept[count_row, first_list + j] = found[j]
            for extra in range(slot_group):
                plan[first_list + j, found[j] + extra] = spare
                kept[first_list + j, found[j] + extra] = spare
    stage.wait()


def make_plan(row_count, cols, sources, targets, counts, blocks):
    width = -(-(sources.shape[-1] + slot_group) // 128) * 128
    return pl.pallas_call(
        functools.partial(plan_kernel, row_count, cols),
        out_shape=[
            jax.ShapeDtypeStruct((8, width), jnp.int32),
            pltpu.SMEM((8, width), jnp.int32),
            pltpu.VMEM(blocks.shape[1:], blocks.dtype),
        ],
        in_specs=[hbm] * 4,
        out_specs=[smem, smem, vmem],
        scratch_shapes=[
            pltpu.SMEM(sources.shape, jnp.int32),
            pltpu.SMEM(targets.shape, jnp.int32),
            pltpu.SMEM(counts.shape, jnp.int32),
            pltpu.SemaphoreType.DMA((4,)),
        ],
        compiler_params=params,
    )(in_hbm(sources), in_hbm(targets), in_hbm(counts), blocks)


def exchange_order(row_count):
    return [(row + row_count // 2) % row_count for row in range(row_count)]


def fetched_levels(lists, resident):
    needed = dict.fromkeys((layer, pairs[pair][0]) for pair, layer, _ in lists)
    return [key for key in needed if key not in resident]


def update_kernel(config, *refs):
    lists, layer_count, groups_of_solutions, cols, row_count, resident, stages, carries, keeps_plan = config
    refs = list(refs)
    plans_in = [refs.pop(0) for _ in range(layer_count)]
    blocks = [refs.pop(0) for _ in range(layer_count)]
    solutions = [refs.pop(0) for _ in range(groups_of_solutions * cols)]
    places = {key: refs.pop(0) for key in resident}
    total_in = refs.pop(0) if carries else None
    out = refs.pop(0)
    next_ref = refs.pop(0) if stages else None
    plans = list(plans_in)
    if keeps_plan:
        plans[1] = refs.pop(0)
    chosen, total, plan_semaphore, semaphores = refs[:4]
    fetched = fetched_levels(lists, resident + ((stages,) if stages else ()))

    plan_loads = []
    if keeps_plan:
        plan_loads.append(pltpu.make_async_copy(plans_in[1], plans[1], plan_semaphore))
    loads = {
        key: pltpu.make_async_copy(blocks[key[0]].at[key[1]], refs[4].at[k], semaphores.at[k])
        for k, key in enumerate(fetched)
    }
    for load in plan_loads + list(loads.values()):
        load.start()
    places.update({key: refs[4].at[k] for k, key in enumerate(fetched)})
    if stages:
        places[stages] = next_ref
        loads[stages] = pltpu.make_async_copy(
            blocks[stages[0]].at[stages[1]], next_ref, semaphores.at[len(fetched)]
        )
        loads[stages].start()

    for j, solution_ref in enumerate(solutions):
        chosen[j] = solution_ref[...]
    if carries:
        total[:row_count] = total_in[...]
    else:
        total[...] = jnp.zeros_like(total)
    for load in plan_loads:
        load.wait()

    for pair, layer, j in lists:
        key = (layer, pairs[pair][0])
        if key in loads:
            loads.pop(key).wait()
        pieces = places[key]

        def one_group(g, unused):
            for first in range(0, slot_group, batch):
                entries = [plans[layer][pair, g * slot_group + first + s] for s in range(batch)]
                products = [
                    jnp.dot(
                        pieces[lax.shift_right_logical(entry, 2 * field)],
                        chosen[j * cols + (entry & field_mask)],
                        preferred_element_type=jnp.float32,
                    )
                    for entry in entries
                ]
                for entry, product in zip(entries, products):
                    total[lax.shift_right_logical(entry, field) & field_mask] += product
            return unused

        live = plans[layer][count_row, pair]
        lax.fori_loop(0, (live + slot_group - 1) // slot_group, one_group, 0)

    if out.dtype == jnp.bfloat16:
        for k, row in enumerate(exchange_order(row_count)):
            out[k] = total[row].astype(jnp.bfloat16)
    else:
        out[...] = total[:row_count]
    for load in loads.values():
        load.wait()


def update(
    lists, plans, blocks, solution_groups, total_in, row_count, sends, resident, stages, keeps_plan=False
):
    cols = len(solution_groups[0])
    width, sides = solution_groups[0][0].shape
    solutions = [part for group in solution_groups for part in group]
    operands = plans + blocks + solutions
    specs = [smem] * len(plans) + [hbm] * len(blocks) + [vmem] * len(solutions)
    for extra in list(resident.values()) + [total_in]:
        if extra is not None:
            operands.append(extra)
            specs.append(vmem)
    fetched = fetched_levels(lists, tuple(resident) + ((stages,) if stages else ()))
    shape = (row_count, width, sides)
    outs = [pltpu.VMEM(shape, jnp.bfloat16) if sends else jax.ShapeDtypeStruct(shape, jnp.float32)]
    if stages:
        outs.append(pltpu.VMEM(blocks[0].shape[1:], blocks[0].dtype))
    places = [vmem] * len(outs)
    if keeps_plan:
        specs[1] = anywhere
        outs.append(pltpu.SMEM(plans[1].shape, jnp.int32))
        places.append(smem)
    config = (
        lists, len(plans), len(solution_groups), cols, row_count, tuple(resident), stages,
        total_in is not None, keeps_plan,
    )
    scratch = [
        pltpu.VMEM((len(solutions), width, sides), jnp.bfloat16),
        pltpu.VMEM((row_count + 1, width, sides), jnp.float32),
        pltpu.SemaphoreType.DMA,
        pltpu.SemaphoreType.DMA((len(fetched) + 1,)),
    ]
    if fetched:
        scratch.append(pltpu.VMEM((len(fetched),) + blocks[0].shape[1:], jnp.bfloat16))
    found = pl.pallas_call(
        functools.partial(update_kernel, config),
        out_shape=outs,
        in_specs=specs,
        out_specs=places,
        scratch_shapes=scratch,
        compiler_params=params,
    )(*operands)
    return found if len(outs) > 1 else found[0]


def solve_block(inverse, residual):
    return jnp.dot(inverse, residual, preferred_element_type=jnp.float32).astype(jnp.bfloat16)


def reduced_solve(received, given, inverse):
    incoming = jnp.sum(received.astype(jnp.float32), axis=0)
    residual = (given.astype(jnp.float32) - incoming).astype(jnp.bfloat16)
    return solve_block(inverse, residual)


def exchange(send):
    order = exchange_order(lax.axis_size("prow"))
    return lax.all_to_all(send, "prow", 0, 0, tiled=True, axis_index_groups=[order])


def local(blocks, sources, targets, counts, given_sub, given_top, inverse_sub, inverse_top):
    row_count = lax.axis_size("prow")
    cols = lax.axis_size("pcol")
    levels, capacity = sources.shape[3:]
    block_set = blocks[0, 0, 0]
    right_sub = given_sub[0, 0, 0]
    factor_sub = inverse_sub[0, 0, 0]
    right_top = given_top[0, 0]
    factor_top = inverse_top[0, 0]

    level_zero = solve_block(factor_sub[0], right_sub[0])
    zero_own = sibling_values(level_zero, 0)
    block_own = in_hbm(block_set)
    block_sent, level_zero = lax.optimization_barrier((block_set, level_zero))
    plan, own_plan, staged = make_plan(
        row_count, cols,
        sources.reshape(levels, 1, capacity), targets.reshape(levels, 1, capacity),
        counts.reshape(levels), block_own,
    )
    both = [block_own, in_hbm(from_other_core(block_sent))]

    send = update(
        [(0, 0, 0)], [own_plan], both[:1], [zero_own], None, row_count, True, {(0, 0): staged}, None
    )
    send, zero_sent, plan_sent = lax.optimization_barrier((send, level_zero, plan))
    received = exchange(send)
    zero_other = sibling_values(zero_sent, 1)
    plans = [own_plan, from_other_core(plan_sent)]
    second, staged, plans[1] = update(
        [(1, 0, 0), (1, 1, 1)], plans, both, [zero_own, zero_other], None, row_count, False,
        {}, (0, 1), True,
    )
    received, second, staged = lax.optimization_barrier((received, second, staged))
    level_one = reduced_solve(received, right_sub[1], factor_sub[1])
    one_own = sibling_values(level_one, 0)
    one_other = sibling_values(level_one, 1)

    send = update(
        [(3, 0, 0), (3, 1, 1)], plans, both, [one_own, one_other], second, row_count, True,
        {(0, 1): staged}, None,
    )
    received = exchange(send)
    third, staged = update(
        [(2, 0, 0), (2, 1, 1), (4, 0, 2), (4, 1, 3)], plans, both,
        [zero_own, zero_other, one_own, one_other], None, row_count, False, {}, (0, 2),
    )
    received, third, staged = lax.optimization_barrier((received, third, staged))
    level_two = reduced_solve(received, right_top[0], factor_top[0])
    two_own = sibling_values(level_two, 0)

    resident = {(0, 2): staged}
    third, resident[(1, 2)] = update(
        [(5, 0, 0), (5, 1, 0)], plans, both, [[level_two] * cols], third, row_count, False, resident,
        (1, 2),
    )
    send = update(
        [(6, 0, 0), (6, 1, 0)], plans, both, [two_own], third, row_count, True, resident, None
    )
    send, level_zero, level_one = lax.optimization_barrier((send, level_zero, level_one))
    level_three = reduced_solve(exchange(send), right_top[1], factor_top[1])
    solved_sub = jnp.stack([level_zero, level_one])[None, None, None]
    solved_top = jnp.stack([level_two, level_three])[None, None]
    return (solved_sub, solved_top)


def solution(mesh):
    in_specs = (
        P("prow", "pcol", "zgrid", None, None, None, None),
        P("prow", "pcol", "zgrid", None, None),
        P("prow", "pcol", "zgrid", None, None),
        P("prow", "pcol", "zgrid", None),
        P("prow", "pcol", "zgrid", None, None, None),
        P("prow", "pcol", None, None, None),
        P("prow", "pcol", "zgrid", None, None, None),
        P("prow", "pcol", None, None, None),
    )
    out_specs = (P("prow", "pcol", "zgrid", None, None, None), P("prow", "pcol", None, None, None))
    return jax.shard_map(local, mesh=mesh, in_specs=in_specs, out_specs=out_specs, check_vma=False)
```

```python
import functools

import jax
import jax.numpy as jnp
from jax import lax
from jax.experimental import pallas as pl
from jax.experimental.pallas import tpu as pltpu
from jax.sharding import PartitionSpec as P

slot_group = 8
batch = 4
field = 10
field_mask = (1 << field) - 1
pairs = ((0, 1), (0, 2), (0, 3), (1, 2), (1, 2), (1, 3), (2, 3), (2, 3))
params = pltpu.CompilerParams(vmem_limit_bytes=24 * 1024 * 1024)
vmem = pl.BlockSpec(memory_space=pltpu.VMEM)
smem = pl.BlockSpec(memory_space=pltpu.SMEM)
hbm = pl.BlockSpec(memory_space=pltpu.HBM)
anywhere = pl.BlockSpec(memory_space=pl.ANY)


def sibling_values(value, layers):
    cols = lax.axis_size("pcol")
    depth = lax.axis_size("zgrid")
    found = []
    for k in reversed(range(cols)):
        if k == 0 and layers == 0:
            found.append(value)
            continue
        moves = []
        for c in range(cols):
            for z in range(depth):
                target = ((c - k) % cols) * depth + (z - layers) % depth
                moves.append((c * depth + z, target))
        found.append(lax.ppermute(value, ("pcol", "zgrid"), moves))
    return found[::-1]


def from_other_core(value):
    return lax.ppermute(value, "zgrid", [(0, 1), (1, 0)])


def in_hbm(value):
    return pltpu.with_memory_space_constraint(value, pltpu.HBM)


def plan_kernel(row_count, cols, sources_in, targets_in, counts_in, blocks, plan, kept, staged, *scratch):
    sources, targets, counts, semaphores = scratch
    loads = [
        pltpu.make_async_copy(sources_in, sources, semaphores.at[0]),
        pltpu.make_async_copy(targets_in, targets, semaphores.at[1]),
        pltpu.make_async_copy(counts_in, counts, semaphores.at[2]),
    ]
    for load in loads:
        load.start()
    stage = pltpu.make_async_copy(blocks.at[0], staged, semaphores.at[3])
    stage.start()
    for load in loads:
        load.wait()
    me = lax.axis_index("pcol")
    spare = row_count << field
    width = plan.shape[1]
    for level in range(3):
        first_list = pairs.index((level, level + 1))
        steps = 3 - level
        lists = sum(pair[0] == level for pair in pairs)

        def one_slot(slot, found):
            target = targets[level, 0, slot]
            higher = [(target >= (level + j) * row_count).astype(jnp.int32) for j in range(1, steps)]
            step = sum(higher, jnp.int32(0))
            row = target - (level + step) * row_count
            column = sources[level, 0, slot] - me
            column = jnp.where(column < 0, column + cols, column)
            kind = step
            if lists > steps:
                kind = step + ((step > 0) | (column > 0)).astype(jnp.int32)
            place = found[lists - 1]
            for j in range(lists - 1):
                place = jnp.where(kind == j, found[j], place)
            entry = (slot << (2 * field)) + (row << field) + column
            plan[first_list + kind, place] = entry
            kept[first_list + kind, place] = entry
            return tuple(found[j] + (kind == j).astype(jnp.int32) for j in range(lists))

        found = lax.fori_loop(0, counts[level], one_slot, (jnp.int32(0),) * lists)
        for j in range(lists):
            plan[first_list + j, width - 1] = found[j]
            kept[first_list + j, width - 1] = found[j]
            for extra in range(slot_group):
                plan[first_list + j, found[j] + extra] = spare
                kept[first_list + j, found[j] + extra] = spare
    stage.wait()


def make_plan(row_count, cols, sources, targets, counts, blocks):
    width = -(-(sources.shape[-1] + slot_group + 1) // 128) * 128
    return pl.pallas_call(
        functools.partial(plan_kernel, row_count, cols),
        out_shape=[
            jax.ShapeDtypeStruct((len(pairs), width), jnp.int32),
            pltpu.SMEM((len(pairs), width), jnp.int32),
            pltpu.VMEM(blocks.shape[1:], blocks.dtype),
        ],
        in_specs=[hbm] * 4,
        out_specs=[smem, smem, vmem],
        scratch_shapes=[
            pltpu.SMEM(sources.shape, jnp.int32),
            pltpu.SMEM(targets.shape, jnp.int32),
            pltpu.SMEM(counts.shape, jnp.int32),
            pltpu.SemaphoreType.DMA((4,)),
        ],
        compiler_params=params,
    )(in_hbm(sources), in_hbm(targets), in_hbm(counts), blocks)


def exchange_order(row_count):
    return [(row + row_count // 2) % row_count for row in range(row_count)]


def fetched_levels(lists, resident):
    needed = dict.fromkeys((layer, pairs[pair][0]) for pair, layer, _ in lists)
    return [key for key in needed if key not in resident]


def update_kernel(config, *refs):
    lists, layer_count, groups_of_solutions, cols, row_count, resident, stages, carries, keeps_plan = config
    refs = list(refs)
    plans_in = [refs.pop(0) for _ in range(layer_count)]
    blocks = [refs.pop(0) for _ in range(layer_count)]
    solutions = [refs.pop(0) for _ in range(groups_of_solutions * cols)]
    places = {key: refs.pop(0) for key in resident}
    total_in = refs.pop(0) if carries else None
    out = refs.pop(0)
    next_ref = refs.pop(0) if stages else None
    plans = list(plans_in)
    if keeps_plan:
        plans[1] = refs.pop(0)
    chosen, total, plan_semaphore, semaphores = refs[:4]
    fetched = fetched_levels(lists, resident + ((stages,) if stages else ()))

    plan_loads = []
    if keeps_plan:
        plan_loads.append(pltpu.make_async_copy(plans_in[1], plans[1], plan_semaphore))
    loads = {
        key: pltpu.make_async_copy(blocks[key[0]].at[key[1]], refs[4].at[k], semaphores.at[k])
        for k, key in enumerate(fetched)
    }
    for load in plan_loads + list(loads.values()):
        load.start()
    places.update({key: refs[4].at[k] for k, key in enumerate(fetched)})
    if stages:
        places[stages] = next_ref
        loads[stages] = pltpu.make_async_copy(
            blocks[stages[0]].at[stages[1]], next_ref, semaphores.at[len(fetched)]
        )
        loads[stages].start()

    for j, solution_ref in enumerate(solutions):
        chosen[j] = solution_ref[...]
    if carries:
        total[:row_count] = total_in[...]
    else:
        total[...] = jnp.zeros_like(total)
    for load in plan_loads:
        load.wait()

    for pair, layer, j in lists:
        key = (layer, pairs[pair][0])
        if key in loads:
            loads.pop(key).wait()
        pieces = places[key]

        def one_group(g, unused):
            for first in range(0, slot_group, batch):
                entries = [plans[layer][pair, g * slot_group + first + s] for s in range(batch)]
                products = [
                    jnp.dot(
                        pieces[lax.shift_right_logical(entry, 2 * field)],
                        chosen[j * cols + (entry & field_mask)],
                        preferred_element_type=jnp.float32,
                    )
                    for entry in entries
                ]
                for entry, product in zip(entries, products):
                    total[lax.shift_right_logical(entry, field) & field_mask] += product
            return unused

        live = plans[layer][pair, plans[layer].shape[1] - 1]
        lax.fori_loop(0, (live + slot_group - 1) // slot_group, one_group, 0)

    if out.dtype == jnp.bfloat16:
        for k, row in enumerate(exchange_order(row_count)):
            out[k] = total[row].astype(jnp.bfloat16)
    else:
        out[...] = total[:row_count]
    for load in loads.values():
        load.wait()


def update(
    lists, plans, blocks, solution_groups, total_in, row_count, sends, resident, stages, keeps_plan=False
):
    cols = len(solution_groups[0])
    width, sides = solution_groups[0][0].shape
    solutions = [part for group in solution_groups for part in group]
    operands = plans + blocks + solutions
    specs = [smem] * len(plans) + [hbm] * len(blocks) + [vmem] * len(solutions)
    for extra in list(resident.values()) + [total_in]:
        if extra is not None:
            operands.append(extra)
            specs.append(vmem)
    fetched = fetched_levels(lists, tuple(resident) + ((stages,) if stages else ()))
    shape = (row_count, width, sides)
    outs = [pltpu.VMEM(shape, jnp.bfloat16) if sends else jax.ShapeDtypeStruct(shape, jnp.float32)]
    if stages:
        outs.append(pltpu.VMEM(blocks[0].shape[1:], blocks[0].dtype))
    places = [vmem] * len(outs)
    if keeps_plan:
        specs[1] = anywhere
        outs.append(pltpu.SMEM(plans[1].shape, jnp.int32))
        places.append(smem)
    config = (
        lists, len(plans), len(solution_groups), cols, row_count, tuple(resident), stages,
        total_in is not None, keeps_plan,
    )
    scratch = [
        pltpu.VMEM((len(solutions), width, sides), jnp.bfloat16),
        pltpu.VMEM((row_count + 1, width, sides), jnp.float32),
        pltpu.SemaphoreType.DMA,
        pltpu.SemaphoreType.DMA((len(fetched) + 1,)),
    ]
    if fetched:
        scratch.append(pltpu.VMEM((len(fetched),) + blocks[0].shape[1:], jnp.bfloat16))
    found = pl.pallas_call(
        functools.partial(update_kernel, config),
        out_shape=outs,
        in_specs=specs,
        out_specs=places,
        scratch_shapes=scratch,
        compiler_params=params,
    )(*operands)
    return found if len(outs) > 1 else found[0]


def solve_block(inverse, residual):
    return jnp.dot(inverse, residual, preferred_element_type=jnp.float32).astype(jnp.bfloat16)


def reduced_solve(received, given, inverse):
    incoming = jnp.sum(received.astype(jnp.float32), axis=0)
    residual = (given.astype(jnp.float32) - incoming).astype(jnp.bfloat16)
    return solve_block(inverse, residual)


def exchange(send):
    order = exchange_order(lax.axis_size("prow"))
    return lax.all_to_all(send, "prow", 0, 0, tiled=True, axis_index_groups=[order])


def local(blocks, sources, targets, counts, given_sub, given_top, inverse_sub, inverse_top):
    row_count = lax.axis_size("prow")
    cols = lax.axis_size("pcol")
    levels, capacity = sources.shape[3:]
    block_set = blocks[0, 0, 0]
    right_sub = given_sub[0, 0, 0]
    factor_sub = inverse_sub[0, 0, 0]
    right_top = given_top[0, 0]
    factor_top = inverse_top[0, 0]

    level_zero = solve_block(factor_sub[0], right_sub[0])
    zero_own = sibling_values(level_zero, 0)
    block_own = in_hbm(block_set)
    block_sent, level_zero = lax.optimization_barrier((block_set, level_zero))
    plan, own_plan, staged = make_plan(
        row_count, cols,
        sources.reshape(levels, 1, capacity), targets.reshape(levels, 1, capacity),
        counts.reshape(levels), block_own,
    )
    both = [block_own, in_hbm(from_other_core(block_sent))]

    send = update(
        [(0, 0, 0)], [own_plan], both[:1], [zero_own], None, row_count, True, {(0, 0): staged}, None
    )
    send, zero_sent, plan_sent = lax.optimization_barrier((send, level_zero, plan))
    received = exchange(send)
    zero_other = sibling_values(zero_sent, 1)
    plans = [own_plan, from_other_core(plan_sent)]
    second, staged, plans[1] = update(
        [(1, 0, 0), (1, 1, 1)], plans, both, [zero_own, zero_other], None, row_count, False,
        {}, (0, 1), True,
    )
    received, second, staged = lax.optimization_barrier((received, second, staged))
    level_one = reduced_solve(received, right_sub[1], factor_sub[1])
    one_own = sibling_values(level_one, 0)
    one_other = sibling_values(level_one, 1)

    resident = {(0, 1): staged}
    second, resident[(1, 1)] = update(
        [(3, 0, 0)], plans, both, [[level_one] * cols], second, row_count, False, resident, (1, 1)
    )
    send = update(
        [(4, 0, 0), (3, 1, 1), (4, 1, 1)], plans, both, [one_own, one_other], second, row_count,
        True, resident, None,
    )
    send, one_own, one_other = lax.optimization_barrier((send, one_own, one_other))
    received = exchange(send)
    third, staged = update(
        [(2, 0, 0), (2, 1, 1), (5, 0, 2), (5, 1, 3)], plans, both,
        [zero_own, zero_other, one_own, one_other], None, row_count, False, {}, (0, 2),
    )
    received, third, staged = lax.optimization_barrier((received, third, staged))
    level_two = reduced_solve(received, right_top[0], factor_top[0])
    two_own = sibling_values(level_two, 0)

    resident = {(0, 2): staged}
    third, resident[(1, 2)] = update(
        [(6, 0, 0), (6, 1, 0)], plans, both, [[level_two] * cols], third, row_count, False, resident,
        (1, 2),
    )
    send = update(
        [(7, 0, 0), (7, 1, 0)], plans, both, [two_own], third, row_count, True, resident, None
    )
    send, level_zero, level_one = lax.optimization_barrier((send, level_zero, level_one))
    level_three = reduced_solve(exchange(send), right_top[1], factor_top[1])
    solved_sub = jnp.stack([level_zero, level_one])[None, None, None]
    solved_top = jnp.stack([level_two, level_three])[None, None]
    return (solved_sub, solved_top)


def solution(mesh):
    in_specs = (
        P("prow", "pcol", "zgrid", None, None, None, None),
        P("prow", "pcol", "zgrid", None, None),
        P("prow", "pcol", "zgrid", None, None),
        P("prow", "pcol", "zgrid", None),
        P("prow", "pcol", "zgrid", None, None, None),
        P("prow", "pcol", None, None, None),
        P("prow", "pcol", "zgrid", None, None, None),
        P("prow", "pcol", None, None, None),
    )
    out_specs = (P("prow", "pcol", "zgrid", None, None, None), P("prow", "pcol", None, None, None))
    return jax.shard_map(local, mesh=mesh, in_specs=in_specs, out_specs=out_specs, check_vma=False)
```

```python
import functools

import jax
import jax.numpy as jnp
from jax import lax
from jax.experimental import pallas as pl
from jax.experimental.pallas import tpu as pltpu
from jax.sharding import PartitionSpec as P

slot_group = 8
batch = 4
field = 10
field_mask = (1 << field) - 1
pairs = ((0, 1), (0, 2), (0, 3), (1, 2), (1, 2), (1, 3), (2, 3), (2, 3))
params = pltpu.CompilerParams(vmem_limit_bytes=24 * 1024 * 1024)
vmem = pl.BlockSpec(memory_space=pltpu.VMEM)
smem = pl.BlockSpec(memory_space=pltpu.SMEM)
hbm = pl.BlockSpec(memory_space=pltpu.HBM)
anywhere = pl.BlockSpec(memory_space=pl.ANY)


def sibling_values(value, layers):
    cols = lax.axis_size("pcol")
    depth = lax.axis_size("zgrid")
    found = []
    for k in reversed(range(cols)):
        if k == 0 and layers == 0:
            found.append(value)
            continue
        moves = []
        for c in range(cols):
            for z in range(depth):
                target = ((c - k) % cols) * depth + (z - layers) % depth
                moves.append((c * depth + z, target))
        found.append(lax.ppermute(value, ("pcol", "zgrid"), moves))
    return found[::-1]


def from_other_core(value):
    return lax.ppermute(value, "zgrid", [(0, 1), (1, 0)])


def in_hbm(value):
    return pltpu.with_memory_space_constraint(value, pltpu.HBM)


def plan_kernel(row_count, cols, sources_in, targets_in, counts_in, blocks, plan, kept, staged, *scratch):
    sources, targets, counts, semaphores = scratch
    loads = [
        pltpu.make_async_copy(sources_in, sources, semaphores.at[0]),
        pltpu.make_async_copy(targets_in, targets, semaphores.at[1]),
        pltpu.make_async_copy(counts_in, counts, semaphores.at[2]),
    ]
    for load in loads:
        load.start()
    stage = pltpu.make_async_copy(blocks.at[0], staged, semaphores.at[3])
    stage.start()
    for load in loads:
        load.wait()
    me = lax.axis_index("pcol")
    spare = row_count << field
    width = plan.shape[1]
    for level in range(3):
        first_list = pairs.index((level, level + 1))
        steps = 3 - level
        lists = sum(pair[0] == level for pair in pairs)

        def one_slot(slot, found):
            target = targets[level, 0, slot]
            higher = [(target >= (level + j) * row_count).astype(jnp.int32) for j in range(1, steps)]
            step = sum(higher, jnp.int32(0))
            row = target - (level + step) * row_count
            column = sources[level, 0, slot] - me
            column = jnp.where(column < 0, column + cols, column)
            kind = step
            if lists > steps:
                kind = step + ((step > 0) | (column > 0)).astype(jnp.int32)
            place = found[lists - 1]
            for j in range(lists - 1):
                place = jnp.where(kind == j, found[j], place)
            entry = (slot << (2 * field)) + (row << field) + column
            plan[first_list + kind, place] = entry
            kept[first_list + kind, place] = entry
            return tuple(found[j] + (kind == j).astype(jnp.int32) for j in range(lists))

        found = lax.fori_loop(0, counts[level], one_slot, (jnp.int32(0),) * lists)
        for j in range(lists):
            plan[first_list + j, width - 1] = found[j]
            kept[first_list + j, width - 1] = found[j]
            for extra in range(slot_group):
                plan[first_list + j, found[j] + extra] = spare
                kept[first_list + j, found[j] + extra] = spare
    stage.wait()


def make_plan(row_count, cols, sources, targets, counts, blocks):
    width = -(-(sources.shape[-1] + slot_group + 1) // 128) * 128
    return pl.pallas_call(
        functools.partial(plan_kernel, row_count, cols),
        out_shape=[
            jax.ShapeDtypeStruct((len(pairs), width), jnp.int32),
            pltpu.SMEM((len(pairs), width), jnp.int32),
            pltpu.VMEM(blocks.shape[1:], blocks.dtype),
        ],
        in_specs=[hbm] * 4,
        out_specs=[smem, smem, vmem],
        scratch_shapes=[
            pltpu.SMEM(sources.shape, jnp.int32),
            pltpu.SMEM(targets.shape, jnp.int32),
            pltpu.SMEM(counts.shape, jnp.int32),
            pltpu.SemaphoreType.DMA((4,)),
        ],
        compiler_params=params,
    )(in_hbm(sources), in_hbm(targets), in_hbm(counts), blocks)


def low_lanes(value):
    return lax.broadcasted_iota(jnp.int32, value.shape, 1) < value.shape[1] // 2


def turned(value):
    return pltpu.roll(value, value.shape[1] // 2, 1)


def half_first(value):
    return jnp.where(lax.axis_index("zgrid") == 0, value, turned(value))


def packed(value):
    half = value.shape[0] // 2
    upper = value[:half]
    return jnp.where(low_lanes(upper), upper, turned(value[half:]))


def unpacked(value):
    return jnp.concatenate([value, turned(value)], axis=0)


def exchange_order(row_count):
    return [(row + row_count // 2) % row_count for row in range(row_count)]


def fetched_levels(lists, resident):
    needed = dict.fromkeys((layer, pairs[pair][0]) for pair, layer, _ in lists)
    return [key for key in needed if key not in resident]


def update_kernel(config, *refs):
    lists, layer_count, groups_of_solutions, cols, row_count, resident, stages, carries, keeps_plan, form = config
    refs = list(refs)
    plans_in = [refs.pop(0) for _ in range(layer_count)]
    blocks = [refs.pop(0) for _ in range(layer_count)]
    solutions = [refs.pop(0) for _ in range(groups_of_solutions * cols)]
    places = {key: refs.pop(0) for key in resident}
    total_in = refs.pop(0) if carries else None
    out = refs.pop(0)
    next_ref = refs.pop(0) if stages else None
    plans = list(plans_in)
    if keeps_plan:
        plans[1] = refs.pop(0)
    chosen, total, plan_semaphore, semaphores = refs[:4]
    fetched = fetched_levels(lists, resident + ((stages,) if stages else ()))

    plan_loads = []
    if keeps_plan:
        plan_loads.append(pltpu.make_async_copy(plans_in[1], plans[1], plan_semaphore))
    loads = {
        key: pltpu.make_async_copy(blocks[key[0]].at[key[1]], refs[4].at[k], semaphores.at[k])
        for k, key in enumerate(fetched)
    }
    for load in plan_loads + list(loads.values()):
        load.start()
    places.update({key: refs[4].at[k] for k, key in enumerate(fetched)})
    if stages:
        places[stages] = next_ref
        loads[stages] = pltpu.make_async_copy(
            blocks[stages[0]].at[stages[1]], next_ref, semaphores.at[len(fetched)]
        )
        loads[stages].start()

    for j, solution_ref in enumerate(solutions):
        if solution_ref.shape == chosen.shape[1:]:
            chosen[j] = solution_ref[...]
        else:
            chosen[j] = unpacked(solution_ref[...].astype(jnp.float32)).astype(jnp.bfloat16)
    if carries:
        total[:row_count] = total_in[...]
    else:
        total[...] = jnp.zeros_like(total)
    for load in plan_loads:
        load.wait()

    for pair, layer, j in lists:
        key = (layer, pairs[pair][0])
        if key in loads:
            loads.pop(key).wait()
        pieces = places[key]

        def one_group(g, unused):
            for first in range(0, slot_group, batch):
                entries = [plans[layer][pair, g * slot_group + first + s] for s in range(batch)]
                products = [
                    jnp.dot(
                        pieces[lax.shift_right_logical(entry, 2 * field)],
                        chosen[j * cols + (entry & field_mask)],
                        preferred_element_type=jnp.float32,
                    )
                    for entry in entries
                ]
                for entry, product in zip(entries, products):
                    total[lax.shift_right_logical(entry, field) & field_mask] += product
            return unused

        live = plans[layer][pair, plans[layer].shape[1] - 1]
        lax.fori_loop(0, (live + slot_group - 1) // slot_group, one_group, 0)

    if form == "summed":
        out[...] = total[:row_count]
    elif form == "turned":
        for row in range(row_count):
            out[row] = half_first(total[row])
    else:
        for k, row in enumerate(exchange_order(row_count)):
            value = half_first(total[row]) if form == "half" else total[row]
            out[k] = (value if form == "whole" else packed(value)).astype(jnp.bfloat16)
    for load in loads.values():
        load.wait()


def update(
    lists, plans, blocks, solution_groups, total_in, row_count, form, resident, stages, keeps_plan=False
):
    cols = len(solution_groups[0])
    width, sides = blocks[0].shape[-1], solution_groups[0][0].shape[-1]
    solutions = [part for group in solution_groups for part in group]
    operands = plans + blocks + solutions
    specs = [smem] * len(plans) + [hbm] * len(blocks) + [vmem] * len(solutions)
    for extra in list(resident.values()) + [total_in]:
        if extra is not None:
            operands.append(extra)
            specs.append(vmem)
    fetched = fetched_levels(lists, tuple(resident) + ((stages,) if stages else ()))
    shape = (row_count, width, sides)
    if form in ("half", "rest"):
        shape = (row_count, width // 2, sides)
    if form in ("summed", "turned"):
        outs = [jax.ShapeDtypeStruct(shape, jnp.float32)]
    else:
        outs = [pltpu.VMEM(shape, jnp.bfloat16)]
    if stages:
        outs.append(pltpu.VMEM(blocks[0].shape[1:], blocks[0].dtype))
    places = [vmem] * len(outs)
    if keeps_plan:
        specs[1] = anywhere
        outs.append(pltpu.SMEM(plans[1].shape, jnp.int32))
        places.append(smem)
    config = (
        lists, len(plans), len(solution_groups), cols, row_count, tuple(resident), stages,
        total_in is not None, keeps_plan, form,
    )
    scratch = [
        pltpu.VMEM((len(solutions), width, sides), jnp.bfloat16),
        pltpu.VMEM((row_count + 1, width, sides), jnp.float32),
        pltpu.SemaphoreType.DMA,
        pltpu.SemaphoreType.DMA((len(fetched) + 1,)),
    ]
    if fetched:
        scratch.append(pltpu.VMEM((len(fetched),) + blocks[0].shape[1:], jnp.bfloat16))
    found = pl.pallas_call(
        functools.partial(update_kernel, config),
        out_shape=outs,
        in_specs=specs,
        out_specs=places,
        scratch_shapes=scratch,
        compiler_params=params,
    )(*operands)
    return found if len(outs) > 1 else found[0]


def half_solve_kernel(level, received, given, inverse, *refs):
    incoming = received[0].astype(jnp.float32)
    for row in range(1, received.shape[0]):
        incoming = incoming + received[row].astype(jnp.float32)
    right = half_first(given[level].astype(jnp.float32))
    residual = (right - unpacked(incoming)).astype(jnp.bfloat16)
    found = jnp.dot(inverse[level], residual, preferred_element_type=jnp.float32)
    found = packed(found).astype(jnp.bfloat16)
    if len(refs) == 1:
        refs[0][...] = found
    else:
        earlier, out = refs
        out[0] = earlier[...]
        out[1] = found


def half_solve(level, received, given, inverse, earlier):
    shape = received.shape[1:]
    operands = [received, given, inverse] + ([] if earlier is None else [earlier])
    return pl.pallas_call(
        functools.partial(half_solve_kernel, level),
        out_shape=jax.ShapeDtypeStruct(shape if earlier is None else (2,) + shape, jnp.bfloat16),
        in_specs=[vmem] * len(operands),
        out_specs=vmem,
        compiler_params=params,
    )(*operands)


def join_kernel(own, other, out):
    first_core = lax.axis_index("zgrid") == 0
    for level in range(own.shape[0]):
        mine, theirs = own[level].astype(jnp.float32), other[level].astype(jnp.float32)
        first = unpacked(jnp.where(first_core, mine, theirs))
        second = unpacked(jnp.where(first_core, theirs, mine))
        out[0, 0, level] = jnp.where(low_lanes(first), first, turned(second)).astype(jnp.bfloat16)


def join_halves(own, other):
    levels, half, sides = own.shape
    return pl.pallas_call(
        join_kernel,
        out_shape=jax.ShapeDtypeStruct((1, 1, levels, 2 * half, sides), jnp.bfloat16),
        in_specs=[vmem, vmem],
        out_specs=vmem,
        compiler_params=params,
    )(own, other)


def solve_block(inverse, residual):
    return jnp.dot(inverse, residual, preferred_element_type=jnp.float32).astype(jnp.bfloat16)


def reduced_solve(received, given, inverse):
    incoming = jnp.sum(received.astype(jnp.float32), axis=0)
    residual = (given.astype(jnp.float32) - incoming).astype(jnp.bfloat16)
    return solve_block(inverse, residual)


def exchange(send):
    order = exchange_order(lax.axis_size("prow"))
    return lax.all_to_all(send, "prow", 0, 0, tiled=True, axis_index_groups=[order])


def local(blocks, sources, targets, counts, given_sub, given_top, inverse_sub, inverse_top):
    row_count = lax.axis_size("prow")
    cols = lax.axis_size("pcol")
    levels, capacity = sources.shape[3:]
    block_set = blocks[0, 0, 0]
    right_sub = given_sub[0, 0, 0]
    factor_sub = inverse_sub[0, 0, 0]
    right_top = given_top[0, 0]
    factor_top = inverse_top[0, 0]

    level_zero = solve_block(factor_sub[0], right_sub[0])
    zero_own = sibling_values(level_zero, 0)
    block_own = in_hbm(block_set)
    block_sent, level_zero = lax.optimization_barrier((block_set, level_zero))
    plan, own_plan, staged = make_plan(
        row_count, cols,
        sources.reshape(levels, 1, capacity), targets.reshape(levels, 1, capacity),
        counts.reshape(levels), block_own,
    )
    both = [block_own, in_hbm(from_other_core(block_sent))]

    send = update(
        [(0, 0, 0)], [own_plan], both[:1], [zero_own], None, row_count, "whole", {(0, 0): staged}, None
    )
    send, zero_sent, plan_sent = lax.optimization_barrier((send, level_zero, plan))
    received = exchange(send)
    zero_other = sibling_values(zero_sent, 1)
    plans = [own_plan, from_other_core(plan_sent)]
    second, staged, plans[1] = update(
        [(1, 0, 0), (1, 1, 1)], plans, both, [zero_own, zero_other], None, row_count, "summed",
        {}, (0, 1), True,
    )
    received, second, staged = lax.optimization_barrier((received, second, staged))
    level_one = reduced_solve(received, right_sub[1], factor_sub[1])
    one_own = sibling_values(level_one, 0)
    one_other = sibling_values(level_one, 1)

    resident = {(0, 1): staged}
    second, resident[(1, 1)] = update(
        [(3, 0, 0)], plans, both, [[level_one] * cols], second, row_count, "summed", resident, (1, 1)
    )
    send = update(
        [(4, 0, 0), (3, 1, 1), (4, 1, 1)], plans, both, [one_own, one_other], second, row_count,
        "half", resident, None,
    )
    send, one_own, one_other = lax.optimization_barrier((send, one_own, one_other))
    received = exchange(send)
    third, staged = update(
        [(2, 0, 0), (2, 1, 1), (5, 0, 2), (5, 1, 3)], plans, both,
        [zero_own, zero_other, one_own, one_other], None, row_count, "turned", {}, (0, 2),
    )
    received, third, staged = lax.optimization_barrier((received, third, staged))
    level_two = half_solve(0, received, right_top, factor_top, None)
    two_own = sibling_values(level_two, 0)

    resident = {(0, 2): staged}
    third, resident[(1, 2)] = update(
        [(6, 0, 0), (6, 1, 0)], plans, both, [[level_two] * cols], third, row_count, "summed",
        resident, (1, 2),
    )
    send = update(
        [(7, 0, 0), (7, 1, 0)], plans, both, [two_own], third, row_count, "rest", resident, None
    )
    send, level_zero, level_one = lax.optimization_barrier((send, level_zero, level_one))
    halves = half_solve(1, exchange(send), right_top, factor_top, level_two)
    solved_top = join_halves(halves, from_other_core(halves))
    solved_sub = jnp.stack([level_zero, level_one])[None, None, None]
    return (solved_sub, solved_top)


def solution(mesh):
    in_specs = (
        P("prow", "pcol", "zgrid", None, None, None, None),
        P("prow", "pcol", "zgrid", None, None),
        P("prow", "pcol", "zgrid", None, None),
        P("prow", "pcol", "zgrid", None),
        P("prow", "pcol", "zgrid", None, None, None),
        P("prow", "pcol", None, None, None),
        P("prow", "pcol", "zgrid", None, None, None),
        P("prow", "pcol", None, None, None),
    )
    out_specs = (P("prow", "pcol", "zgrid", None, None, None), P("prow", "pcol", None, None, None))
    return jax.shard_map(local, mesh=mesh, in_specs=in_specs, out_specs=out_specs, check_vma=False)
```

```python
import functools

import jax
import jax.numpy as jnp
from jax import lax
from jax.experimental import pallas as pl
from jax.experimental.pallas import tpu as pltpu
from jax.sharding import PartitionSpec as P

slot_group = 8
batch = 4
field = 10
field_mask = (1 << field) - 1
pairs = ((0, 1), (0, 2), (0, 3), (1, 2), (1, 2), (1, 3), (2, 3), (2, 3))
params = pltpu.CompilerParams(vmem_limit_bytes=24 * 1024 * 1024)
vmem = pl.BlockSpec(memory_space=pltpu.VMEM)
smem = pl.BlockSpec(memory_space=pltpu.SMEM)
hbm = pl.BlockSpec(memory_space=pltpu.HBM)
anywhere = pl.BlockSpec(memory_space=pl.ANY)


def sibling_values(value, layers):
    cols = lax.axis_size("pcol")
    depth = lax.axis_size("zgrid")
    found = []
    for k in reversed(range(cols)):
        if k == 0 and layers == 0:
            found.append(value)
            continue
        moves = []
        for c in range(cols):
            for z in range(depth):
                target = ((c - k) % cols) * depth + (z - layers) % depth
                moves.append((c * depth + z, target))
        found.append(lax.ppermute(value, ("pcol", "zgrid"), moves))
    return found[::-1]


def from_other_core(value):
    return lax.ppermute(value, "zgrid", [(0, 1), (1, 0)])


def in_hbm(value):
    return pltpu.with_memory_space_constraint(value, pltpu.HBM)


def plan_kernel(row_count, cols, sources_in, targets_in, counts_in, blocks, plan, kept, staged, *scratch):
    sources, targets, counts, semaphores = scratch
    loads = [
        pltpu.make_async_copy(sources_in, sources, semaphores.at[0]),
        pltpu.make_async_copy(targets_in, targets, semaphores.at[1]),
        pltpu.make_async_copy(counts_in, counts, semaphores.at[2]),
    ]
    for load in loads:
        load.start()
    stage = pltpu.make_async_copy(blocks.at[0], staged, semaphores.at[3])
    stage.start()
    for load in loads:
        load.wait()
    me = lax.axis_index("pcol")
    spare = row_count << field
    width = plan.shape[1]
    for level in range(3):
        first_list = pairs.index((level, level + 1))
        steps = 3 - level
        lists = sum(pair[0] == level for pair in pairs)

        def one_slot(slot, found):
            target = targets[level, 0, slot]
            higher = [(target >= (level + j) * row_count).astype(jnp.int32) for j in range(1, steps)]
            step = sum(higher, jnp.int32(0))
            row = target - (level + step) * row_count
            column = sources[level, 0, slot] - me
            column = jnp.where(column < 0, column + cols, column)
            kind = step
            if lists > steps:
                kind = step + ((step > 0) | (column > 0)).astype(jnp.int32)
            place = found[lists - 1]
            for j in range(lists - 1):
                place = jnp.where(kind == j, found[j], place)
            entry = (slot << (2 * field)) + (row << field) + column
            plan[first_list + kind, place] = entry
            kept[first_list + kind, place] = entry
            return tuple(found[j] + (kind == j).astype(jnp.int32) for j in range(lists))

        found = lax.fori_loop(0, counts[level], one_slot, (jnp.int32(0),) * lists)
        for j in range(lists):
            plan[first_list + j, width - 1] = found[j]
            kept[first_list + j, width - 1] = found[j]
            for extra in range(slot_group):
                plan[first_list + j, found[j] + extra] = spare
                kept[first_list + j, found[j] + extra] = spare
    stage.wait()


def make_plan(row_count, cols, sources, targets, counts, blocks):
    width = -(-(sources.shape[-1] + slot_group + 1) // 128) * 128
    return pl.pallas_call(
        functools.partial(plan_kernel, row_count, cols),
        out_shape=[
            jax.ShapeDtypeStruct((len(pairs), width), jnp.int32),
            pltpu.SMEM((len(pairs), width), jnp.int32),
            pltpu.VMEM(blocks.shape[1:], blocks.dtype),
        ],
        in_specs=[hbm] * 4,
        out_specs=[smem, smem, vmem],
        scratch_shapes=[
            pltpu.SMEM(sources.shape, jnp.int32),
            pltpu.SMEM(targets.shape, jnp.int32),
            pltpu.SMEM(counts.shape, jnp.int32),
            pltpu.SemaphoreType.DMA((4,)),
        ],
        compiler_params=params,
    )(in_hbm(sources), in_hbm(targets), in_hbm(counts), blocks)


def low_lanes(value):
    return lax.broadcasted_iota(jnp.int32, value.shape, 1) < value.shape[1] // 2


def turned(value):
    return pltpu.roll(value, value.shape[1] // 2, 1)


def half_first(value):
    return jnp.where(lax.axis_index("zgrid") == 0, value, turned(value))


def packed(value):
    half = value.shape[0] // 2
    upper = value[:half]
    return jnp.where(low_lanes(upper), upper, turned(value[half:]))


def unpacked(value):
    return jnp.concatenate([value, turned(value)], axis=0)


def exchange_order(row_count):
    return [(row + row_count // 2) % row_count for row in range(row_count)]


def fetched_levels(lists, resident):
    needed = dict.fromkeys((layer, pairs[pair][0]) for pair, layer, _ in lists)
    return [key for key in needed if key not in resident]


def update_kernel(config, *refs):
    lists, layer_count, groups_of_solutions, cols, row_count, resident, stages, carries, keeps_plan, form = config
    refs = list(refs)
    plans_in = [refs.pop(0) for _ in range(layer_count)]
    blocks = [refs.pop(0) for _ in range(layer_count)]
    solutions = [refs.pop(0) for _ in range(groups_of_solutions * cols)]
    places = {key: refs.pop(0) for key in resident}
    total_in = refs.pop(0) if carries else None
    out = refs.pop(0)
    next_ref = refs.pop(0) if stages else None
    plans = list(plans_in)
    if keeps_plan:
        plans[1] = refs.pop(0)
    chosen, total, plan_semaphore, semaphores = refs[:4]
    fetched = fetched_levels(lists, resident + ((stages,) if stages else ()))

    plan_loads = []
    if keeps_plan:
        plan_loads.append(pltpu.make_async_copy(plans_in[1], plans[1], plan_semaphore))
    loads = {
        key: pltpu.make_async_copy(blocks[key[0]].at[key[1]], refs[4].at[k], semaphores.at[k])
        for k, key in enumerate(fetched)
    }
    for load in plan_loads + list(loads.values()):
        load.start()
    places.update({key: refs[4].at[k] for k, key in enumerate(fetched)})
    if stages:
        places[stages] = next_ref
        loads[stages] = pltpu.make_async_copy(
            blocks[stages[0]].at[stages[1]], next_ref, semaphores.at[len(fetched)]
        )
        loads[stages].start()

    for j, solution_ref in enumerate(solutions):
        if form == "whole":
            chosen[j] = solution_ref[...]
        elif solution_ref.shape == chosen.shape[1:]:
            chosen[j] = half_first(solution_ref[...].astype(jnp.float32)).astype(jnp.bfloat16)
        else:
            chosen[j] = unpacked(solution_ref[...].astype(jnp.float32)).astype(jnp.bfloat16)
    if carries:
        total[:row_count] = total_in[...]
    else:
        total[...] = jnp.zeros_like(total)
    for load in plan_loads:
        load.wait()

    for pair, layer, j in lists:
        key = (layer, pairs[pair][0])
        if key in loads:
            loads.pop(key).wait()
        pieces = places[key]

        def one_group(g, unused):
            for first in range(0, slot_group, batch):
                entries = [plans[layer][pair, g * slot_group + first + s] for s in range(batch)]
                products = [
                    jnp.dot(
                        pieces[lax.shift_right_logical(entry, 2 * field)],
                        chosen[j * cols + (entry & field_mask)],
                        preferred_element_type=jnp.float32,
                    )
                    for entry in entries
                ]
                for entry, product in zip(entries, products):
                    total[lax.shift_right_logical(entry, field) & field_mask] += product
            return unused

        live = plans[layer][pair, plans[layer].shape[1] - 1]
        lax.fori_loop(0, (live + slot_group - 1) // slot_group, one_group, 0)

    if form == "summed":
        out[...] = total[:row_count]
    else:
        for k, row in enumerate(exchange_order(row_count)):
            value = total[row] if form == "whole" else packed(total[row])
            out[k] = value.astype(jnp.bfloat16)
    for load in loads.values():
        load.wait()


def update(
    lists, plans, blocks, solution_groups, total_in, row_count, form, resident, stages, keeps_plan=False
):
    cols = len(solution_groups[0])
    width, sides = blocks[0].shape[-1], solution_groups[0][0].shape[-1]
    solutions = [part for group in solution_groups for part in group]
    operands = plans + blocks + solutions
    specs = [smem] * len(plans) + [hbm] * len(blocks) + [vmem] * len(solutions)
    for extra in list(resident.values()) + [total_in]:
        if extra is not None:
            operands.append(extra)
            specs.append(vmem)
    fetched = fetched_levels(lists, tuple(resident) + ((stages,) if stages else ()))
    shape = (row_count, width, sides)
    if form == "half":
        shape = (row_count, width // 2, sides)
    if form == "summed":
        outs = [jax.ShapeDtypeStruct(shape, jnp.float32)]
    else:
        outs = [pltpu.VMEM(shape, jnp.bfloat16)]
    if stages:
        outs.append(pltpu.VMEM(blocks[0].shape[1:], blocks[0].dtype))
    places = [vmem] * len(outs)
    if keeps_plan:
        specs[1] = anywhere
        outs.append(pltpu.SMEM(plans[1].shape, jnp.int32))
        places.append(smem)
    config = (
        lists, len(plans), len(solution_groups), cols, row_count, tuple(resident), stages,
        total_in is not None, keeps_plan, form,
    )
    scratch = [
        pltpu.VMEM((len(solutions), width, sides), jnp.bfloat16),
        pltpu.VMEM((row_count + 1, width, sides), jnp.float32),
        pltpu.SemaphoreType.DMA,
        pltpu.SemaphoreType.DMA((len(fetched) + 1,)),
    ]
    if fetched:
        scratch.append(pltpu.VMEM((len(fetched),) + blocks[0].shape[1:], jnp.bfloat16))
    found = pl.pallas_call(
        functools.partial(update_kernel, config),
        out_shape=outs,
        in_specs=specs,
        out_specs=places,
        scratch_shapes=scratch,
        compiler_params=params,
    )(*operands)
    return found if len(outs) > 1 else found[0]


def sub_solve_kernel(received, given, inverse, out, kept, sent):
    incoming = received[0].astype(jnp.float32)
    for row in range(1, received.shape[0]):
        incoming = incoming + received[row].astype(jnp.float32)
    residual = (given[1].astype(jnp.float32) - incoming).astype(jnp.bfloat16)
    found = jnp.dot(inverse[1], residual, preferred_element_type=jnp.float32)
    out[...] = found.astype(jnp.bfloat16)
    mine = half_first(found)
    kept[...] = packed(mine).astype(jnp.bfloat16)
    sent[...] = packed(turned(mine)).astype(jnp.bfloat16)


def sub_solve(received, given, inverse):
    _, width, sides = received.shape
    half = jax.ShapeDtypeStruct((width // 2, sides), jnp.bfloat16)
    return pl.pallas_call(
        sub_solve_kernel,
        out_shape=[jax.ShapeDtypeStruct((width, sides), jnp.bfloat16), half, half],
        in_specs=[vmem] * 3,
        out_specs=[vmem] * 3,
        compiler_params=params,
    )(received, given, inverse)


def half_solve_kernel(level, received, given, inverse, *refs):
    incoming = received[0].astype(jnp.float32)
    for row in range(1, received.shape[0]):
        incoming = incoming + received[row].astype(jnp.float32)
    right = half_first(given[level].astype(jnp.float32))
    residual = (right - unpacked(incoming)).astype(jnp.bfloat16)
    found = jnp.dot(inverse[level], residual, preferred_element_type=jnp.float32)
    found = packed(found).astype(jnp.bfloat16)
    if len(refs) == 1:
        refs[0][...] = found
    else:
        earlier, out = refs
        out[0] = earlier[...]
        out[1] = found


def half_solve(level, received, given, inverse, earlier):
    shape = received.shape[1:]
    operands = [received, given, inverse] + ([] if earlier is None else [earlier])
    return pl.pallas_call(
        functools.partial(half_solve_kernel, level),
        out_shape=jax.ShapeDtypeStruct(shape if earlier is None else (2,) + shape, jnp.bfloat16),
        in_specs=[vmem] * len(operands),
        out_specs=vmem,
        compiler_params=params,
    )(*operands)


def join_kernel(own, other, out):
    first_core = lax.axis_index("zgrid") == 0
    for level in range(own.shape[0]):
        mine, theirs = own[level].astype(jnp.float32), other[level].astype(jnp.float32)
        first = unpacked(jnp.where(first_core, mine, theirs))
        second = unpacked(jnp.where(first_core, theirs, mine))
        out[0, 0, level] = jnp.where(low_lanes(first), first, turned(second)).astype(jnp.bfloat16)


def join_halves(own, other):
    levels, half, sides = own.shape
    return pl.pallas_call(
        join_kernel,
        out_shape=jax.ShapeDtypeStruct((1, 1, levels, 2 * half, sides), jnp.bfloat16),
        in_specs=[vmem, vmem],
        out_specs=vmem,
        compiler_params=params,
    )(own, other)


def solve_block(inverse, residual):
    return jnp.dot(inverse, residual, preferred_element_type=jnp.float32).astype(jnp.bfloat16)


def exchange(send):
    order = exchange_order(lax.axis_size("prow"))
    return lax.all_to_all(send, "prow", 0, 0, tiled=True, axis_index_groups=[order])


def local(blocks, sources, targets, counts, given_sub, given_top, inverse_sub, inverse_top):
    row_count = lax.axis_size("prow")
    cols = lax.axis_size("pcol")
    levels, capacity = sources.shape[3:]
    block_set = blocks[0, 0, 0]
    right_sub = given_sub[0, 0, 0]
    factor_sub = inverse_sub[0, 0, 0]
    right_top = given_top[0, 0]
    factor_top = inverse_top[0, 0]

    level_zero = solve_block(factor_sub[0], right_sub[0])
    zero_own = sibling_values(level_zero, 0)
    block_own = in_hbm(block_set)
    block_sent, level_zero = lax.optimization_barrier((block_set, level_zero))
    plan, own_plan, staged = make_plan(
        row_count, cols,
        sources.reshape(levels, 1, capacity), targets.reshape(levels, 1, capacity),
        counts.reshape(levels), block_own,
    )
    both = [block_own, in_hbm(from_other_core(block_sent))]

    send = update(
        [(0, 0, 0)], [own_plan], both[:1], [zero_own], None, row_count, "whole", {(0, 0): staged}, None
    )
    send, zero_sent, plan_sent = lax.optimization_barrier((send, level_zero, plan))
    received = exchange(send)
    zero_other = sibling_values(zero_sent, 1)
    plans = [own_plan, from_other_core(plan_sent)]
    second, staged, plans[1] = update(
        [(1, 0, 0), (1, 1, 1)], plans, both, [zero_own, zero_other], None, row_count, "summed",
        {}, (0, 1), True,
    )
    received, second, staged = lax.optimization_barrier((received, second, staged))
    level_one, one_kept, one_sent = sub_solve(received, right_sub, factor_sub)
    one_own = sibling_values(one_kept, 0)
    one_other = sibling_values(one_sent, 1)

    resident = {(0, 1): staged}
    second, resident[(1, 1)] = update(
        [(3, 0, 0)], plans, both, [[one_kept] * cols], second, row_count, "summed", resident, (1, 1)
    )
    send = update(
        [(4, 0, 0), (3, 1, 1), (4, 1, 1)], plans, both, [one_own, one_other], second, row_count,
        "half", resident, None,
    )
    send, one_own, one_other = lax.optimization_barrier((send, one_own, one_other))
    received = exchange(send)
    third, staged = update(
        [(2, 0, 0), (2, 1, 1), (5, 0, 2), (5, 1, 3)], plans, both,
        [zero_own, zero_other, one_own, one_other], None, row_count, "summed", {}, (0, 2),
    )
    received, third, staged = lax.optimization_barrier((received, third, staged))
    level_two = half_solve(0, received, right_top, factor_top, None)
    two_own = sibling_values(level_two, 0)

    resident = {(0, 2): staged}
    third, resident[(1, 2)] = update(
        [(6, 0, 0), (6, 1, 0)], plans, both, [[level_two] * cols], third, row_count, "summed",
        resident, (1, 2),
    )
    send = update(
        [(7, 0, 0), (7, 1, 0)], plans, both, [two_own], third, row_count, "half", resident, None
    )
    send, level_zero, level_one = lax.optimization_barrier((send, level_zero, level_one))
    halves = half_solve(1, exchange(send), right_top, factor_top, level_two)
    solved_top = join_halves(halves, from_other_core(halves))
    solved_sub = jnp.stack([level_zero, level_one])[None, None, None]
    return (solved_sub, solved_top)


def solution(mesh):
    in_specs = (
        P("prow", "pcol", "zgrid", None, None, None, None),
        P("prow", "pcol", "zgrid", None, None),
        P("prow", "pcol", "zgrid", None, None),
        P("prow", "pcol", "zgrid", None),
        P("prow", "pcol", "zgrid", None, None, None),
        P("prow", "pcol", None, None, None),
        P("prow", "pcol", "zgrid", None, None, None),
        P("prow", "pcol", None, None, None),
    )
    out_specs = (P("prow", "pcol", "zgrid", None, None, None), P("prow", "pcol", None, None, None))
    return jax.shard_map(local, mesh=mesh, in_specs=in_specs, out_specs=out_specs, check_vma=False)
```

```python
import functools

import jax
import jax.numpy as jnp
from jax import lax
from jax.experimental import pallas as pl
from jax.experimental.pallas import tpu as pltpu
from jax.sharding import PartitionSpec as P

slot_group = 8
batch = 4
field = 10
field_mask = (1 << field) - 1
pairs = ((0, 1), (0, 2), (0, 3), (1, 2), (1, 2), (1, 3), (2, 3), (2, 3))
params = pltpu.CompilerParams(vmem_limit_bytes=24 * 1024 * 1024)
vmem = pl.BlockSpec(memory_space=pltpu.VMEM)
smem = pl.BlockSpec(memory_space=pltpu.SMEM)
hbm = pl.BlockSpec(memory_space=pltpu.HBM)
anywhere = pl.BlockSpec(memory_space=pl.ANY)


def sibling_values(value, layers):
    cols = lax.axis_size("pcol")
    depth = lax.axis_size("zgrid")
    found = []
    for k in reversed(range(cols)):
        if k == 0 and layers == 0:
            found.append(value)
            continue
        moves = []
        for c in range(cols):
            for z in range(depth):
                target = ((c - k) % cols) * depth + (z - layers) % depth
                moves.append((c * depth + z, target))
        found.append(lax.ppermute(value, ("pcol", "zgrid"), moves))
    return found[::-1]


def from_other_core(value):
    return lax.ppermute(value, "zgrid", [(0, 1), (1, 0)])


def in_hbm(value):
    return pltpu.with_memory_space_constraint(value, pltpu.HBM)


def plan_kernel(row_count, cols, sources_in, targets_in, counts_in, blocks, plan, kept, staged, *scratch):
    sources, targets, counts, semaphores = scratch
    loads = [
        pltpu.make_async_copy(sources_in, sources, semaphores.at[0]),
        pltpu.make_async_copy(targets_in, targets, semaphores.at[1]),
        pltpu.make_async_copy(counts_in, counts, semaphores.at[2]),
    ]
    for load in loads:
        load.start()
    stage = pltpu.make_async_copy(blocks.at[0], staged, semaphores.at[3])
    stage.start()
    for load in loads:
        load.wait()
    me = lax.axis_index("pcol")
    spare = row_count << field
    width = plan.shape[1]
    for level in range(3):
        first_list = pairs.index((level, level + 1))
        steps = 3 - level
        lists = sum(pair[0] == level for pair in pairs)

        def one_slot(slot, found):
            target = targets[level, 0, slot]
            higher = [(target >= (level + j) * row_count).astype(jnp.int32) for j in range(1, steps)]
            step = sum(higher, jnp.int32(0))
            row = target - (level + step) * row_count
            column = sources[level, 0, slot] - me
            column = jnp.where(column < 0, column + cols, column)
            kind = step
            if lists > steps:
                kind = step + ((step > 0) | (column > 0)).astype(jnp.int32)
            place = found[lists - 1]
            for j in range(lists - 1):
                place = jnp.where(kind == j, found[j], place)
            entry = (slot << (2 * field)) + (row << field) + column
            plan[first_list + kind, place] = entry
            kept[first_list + kind, place] = entry
            return tuple(found[j] + (kind == j).astype(jnp.int32) for j in range(lists))

        found = lax.fori_loop(0, counts[level], one_slot, (jnp.int32(0),) * lists)
        for j in range(lists):
            plan[first_list + j, width - 1] = found[j]
            kept[first_list + j, width - 1] = found[j]
            for extra in range(slot_group):
                plan[first_list + j, found[j] + extra] = spare
                kept[first_list + j, found[j] + extra] = spare
    stage.wait()


def make_plan(row_count, cols, sources, targets, counts, blocks):
    width = -(-(sources.shape[-1] + slot_group + 1) // 128) * 128
    return pl.pallas_call(
        functools.partial(plan_kernel, row_count, cols),
        out_shape=[
            jax.ShapeDtypeStruct((len(pairs), width), jnp.int32),
            pltpu.SMEM((len(pairs), width), jnp.int32),
            pltpu.VMEM(blocks.shape[1:], blocks.dtype),
        ],
        in_specs=[hbm] * 4,
        out_specs=[smem, smem, vmem],
        scratch_shapes=[
            pltpu.SMEM(sources.shape, jnp.int32),
            pltpu.SMEM(targets.shape, jnp.int32),
            pltpu.SMEM(counts.shape, jnp.int32),
            pltpu.SemaphoreType.DMA((4,)),
        ],
        compiler_params=params,
    )(in_hbm(sources), in_hbm(targets), in_hbm(counts), blocks)


def low_lanes(value):
    return lax.broadcasted_iota(jnp.int32, value.shape, 1) < value.shape[1] // 2


def turned(value):
    return pltpu.roll(value, value.shape[1] // 2, 1)


def half_first(value):
    return jnp.where(lax.axis_index("zgrid") == 0, value, turned(value))


def packed(value):
    half = value.shape[0] // 2
    upper = value[:half]
    return jnp.where(low_lanes(upper), upper, turned(value[half:]))


def unpacked(value):
    return jnp.concatenate([value, turned(value)], axis=0)


def exchange_order(row_count):
    return [(row + row_count // 2) % row_count for row in range(row_count)]


def fetched_levels(lists, resident):
    needed = dict.fromkeys((layer, pairs[pair][0]) for pair, layer, _ in lists)
    return [key for key in needed if key not in resident]


def update_kernel(config, *refs):
    lists, layer_count, groups_of_solutions, cols, row_count, resident, stages, carries, keeps_plan, form = config
    refs = list(refs)
    plans_in = [refs.pop(0) for _ in range(layer_count)]
    blocks = [refs.pop(0) for _ in range(layer_count)]
    solutions = [refs.pop(0) for _ in range(groups_of_solutions * cols)]
    places = {key: refs.pop(0) for key in resident}
    total_in = refs.pop(0) if carries else None
    out = refs.pop(0)
    next_ref = refs.pop(0) if stages else None
    plans = list(plans_in)
    if keeps_plan:
        plans[1] = refs.pop(0)
    chosen, total, plan_semaphore, semaphores = refs[:4]
    fetched = fetched_levels(lists, resident + ((stages,) if stages else ()))

    plan_loads = []
    if keeps_plan:
        plan_loads.append(pltpu.make_async_copy(plans_in[1], plans[1], plan_semaphore))
    loads = {
        key: pltpu.make_async_copy(blocks[key[0]].at[key[1]], refs[4].at[k], semaphores.at[k])
        for k, key in enumerate(fetched)
    }
    for load in plan_loads + list(loads.values()):
        load.start()
    places.update({key: refs[4].at[k] for k, key in enumerate(fetched)})
    if stages:
        places[stages] = next_ref
        loads[stages] = pltpu.make_async_copy(
            blocks[stages[0]].at[stages[1]], next_ref, semaphores.at[len(fetched)]
        )
        loads[stages].start()

    for j, solution_ref in enumerate(solutions):
        if len(solution_ref.shape) == 3:
            depth = lax.axis_size("zgrid")
            column = lax.rem(lax.axis_index("pcol") + j % cols, cols)
            layer = lax.rem(lax.axis_index("zgrid") + (j // cols) % depth, depth)
            value = solution_ref[column * depth + layer].astype(jnp.float32)
            chosen[j] = unpacked(value).astype(jnp.bfloat16)
        elif form == "whole":
            chosen[j] = solution_ref[...]
        elif solution_ref.shape == chosen.shape[1:]:
            chosen[j] = half_first(solution_ref[...].astype(jnp.float32)).astype(jnp.bfloat16)
        else:
            chosen[j] = unpacked(solution_ref[...].astype(jnp.float32)).astype(jnp.bfloat16)
    if carries:
        total[:row_count] = total_in[...]
    else:
        total[...] = jnp.zeros_like(total)
    for load in plan_loads:
        load.wait()

    for pair, layer, j in lists:
        key = (layer, pairs[pair][0])
        if key in loads:
            loads.pop(key).wait()
        pieces = places[key]

        def one_group(g, unused):
            for first in range(0, slot_group, batch):
                entries = [plans[layer][pair, g * slot_group + first + s] for s in range(batch)]
                products = [
                    jnp.dot(
                        pieces[lax.shift_right_logical(entry, 2 * field)],
                        chosen[j * cols + (entry & field_mask)],
                        preferred_element_type=jnp.float32,
                    )
                    for entry in entries
                ]
                for entry, product in zip(entries, products):
                    total[lax.shift_right_logical(entry, field) & field_mask] += product
            return unused

        live = plans[layer][pair, plans[layer].shape[1] - 1]
        lax.fori_loop(0, (live + slot_group - 1) // slot_group, one_group, 0)

    if form == "summed":
        out[...] = total[:row_count]
    else:
        for k, row in enumerate(exchange_order(row_count)):
            value = total[row] if form == "whole" else packed(total[row])
            out[k] = value.astype(jnp.bfloat16)
    for load in loads.values():
        load.wait()


def update(
    lists, plans, blocks, solution_groups, total_in, row_count, form, resident, stages, keeps_plan=False
):
    cols = len(solution_groups[0])
    width, sides = blocks[0].shape[-1], solution_groups[0][0].shape[-1]
    solutions = [part for group in solution_groups for part in group]
    operands = plans + blocks + solutions
    specs = [smem] * len(plans) + [hbm] * len(blocks) + [vmem] * len(solutions)
    for extra in list(resident.values()) + [total_in]:
        if extra is not None:
            operands.append(extra)
            specs.append(vmem)
    fetched = fetched_levels(lists, tuple(resident) + ((stages,) if stages else ()))
    shape = (row_count, width, sides)
    if form == "half":
        shape = (row_count, width // 2, sides)
    if form == "summed":
        outs = [jax.ShapeDtypeStruct(shape, jnp.float32)]
    else:
        outs = [pltpu.VMEM(shape, jnp.bfloat16)]
    if stages:
        outs.append(pltpu.VMEM(blocks[0].shape[1:], blocks[0].dtype))
    places = [vmem] * len(outs)
    if keeps_plan:
        specs[1] = anywhere
        outs.append(pltpu.SMEM(plans[1].shape, jnp.int32))
        places.append(smem)
    config = (
        lists, len(plans), len(solution_groups), cols, row_count, tuple(resident), stages,
        total_in is not None, keeps_plan, form,
    )
    scratch = [
        pltpu.VMEM((len(solutions), width, sides), jnp.bfloat16),
        pltpu.VMEM((row_count + 1, width, sides), jnp.float32),
        pltpu.SemaphoreType.DMA,
        pltpu.SemaphoreType.DMA((len(fetched) + 1,)),
    ]
    if fetched:
        scratch.append(pltpu.VMEM((len(fetched),) + blocks[0].shape[1:], jnp.bfloat16))
    found = pl.pallas_call(
        functools.partial(update_kernel, config),
        out_shape=outs,
        in_specs=specs,
        out_specs=places,
        scratch_shapes=scratch,
        compiler_params=params,
    )(*operands)
    return found if len(outs) > 1 else found[0]


def sub_solve_kernel(received, given, inverse, out, kept, sent):
    incoming = received[0].astype(jnp.float32)
    for row in range(1, received.shape[0]):
        incoming = incoming + received[row].astype(jnp.float32)
    residual = (given[1].astype(jnp.float32) - incoming).astype(jnp.bfloat16)
    found = jnp.dot(inverse[1], residual, preferred_element_type=jnp.float32)
    out[...] = found.astype(jnp.bfloat16)
    mine = half_first(found)
    kept[...] = packed(mine).astype(jnp.bfloat16)
    halves = [packed(found).astype(jnp.bfloat16), packed(turned(found)).astype(jnp.bfloat16)]
    for device in range(sent.shape[0]):
        sent[device] = halves[device % 2]


def sub_solve(received, given, inverse):
    _, width, sides = received.shape
    devices = lax.axis_size("pcol") * lax.axis_size("zgrid")
    return pl.pallas_call(
        sub_solve_kernel,
        out_shape=[
            jax.ShapeDtypeStruct((width, sides), jnp.bfloat16),
            jax.ShapeDtypeStruct((width // 2, sides), jnp.bfloat16),
            jax.ShapeDtypeStruct((devices, width // 2, sides), jnp.bfloat16),
        ],
        in_specs=[vmem] * 3,
        out_specs=[vmem] * 3,
        compiler_params=params,
    )(received, given, inverse)


def half_solve_kernel(level, received, given, inverse, *refs):
    incoming = received[0].astype(jnp.float32)
    for row in range(1, received.shape[0]):
        incoming = incoming + received[row].astype(jnp.float32)
    right = half_first(given[level].astype(jnp.float32))
    residual = (right - unpacked(incoming)).astype(jnp.bfloat16)
    found = jnp.dot(inverse[level], residual, preferred_element_type=jnp.float32)
    found = packed(found).astype(jnp.bfloat16)
    if len(refs) == 1:
        refs[0][...] = found
    else:
        earlier, out = refs
        out[0] = earlier[...]
        out[1] = found


def half_solve(level, received, given, inverse, earlier):
    shape = received.shape[1:]
    operands = [received, given, inverse] + ([] if earlier is None else [earlier])
    return pl.pallas_call(
        functools.partial(half_solve_kernel, level),
        out_shape=jax.ShapeDtypeStruct(shape if earlier is None else (2,) + shape, jnp.bfloat16),
        in_specs=[vmem] * len(operands),
        out_specs=vmem,
        compiler_params=params,
    )(*operands)


def join_kernel(own, other, out):
    first_core = lax.axis_index("zgrid") == 0
    for level in range(own.shape[0]):
        mine, theirs = own[level].astype(jnp.float32), other[level].astype(jnp.float32)
        first = unpacked(jnp.where(first_core, mine, theirs))
        second = unpacked(jnp.where(first_core, theirs, mine))
        out[0, 0, level] = jnp.where(low_lanes(first), first, turned(second)).astype(jnp.bfloat16)


def join_halves(own, other):
    levels, half, sides = own.shape
    return pl.pallas_call(
        join_kernel,
        out_shape=jax.ShapeDtypeStruct((1, 1, levels, 2 * half, sides), jnp.bfloat16),
        in_specs=[vmem, vmem],
        out_specs=vmem,
        compiler_params=params,
    )(own, other)


def solve_block(inverse, residual):
    return jnp.dot(inverse, residual, preferred_element_type=jnp.float32).astype(jnp.bfloat16)


def exchange(send):
    order = exchange_order(lax.axis_size("prow"))
    return lax.all_to_all(send, "prow", 0, 0, tiled=True, axis_index_groups=[order])


def local(blocks, sources, targets, counts, given_sub, given_top, inverse_sub, inverse_top):
    row_count = lax.axis_size("prow")
    cols = lax.axis_size("pcol")
    levels, capacity = sources.shape[3:]
    block_set = blocks[0, 0, 0]
    right_sub = given_sub[0, 0, 0]
    factor_sub = inverse_sub[0, 0, 0]
    right_top = given_top[0, 0]
    factor_top = inverse_top[0, 0]

    level_zero = solve_block(factor_sub[0], right_sub[0])
    zero_own = sibling_values(level_zero, 0)
    block_own = in_hbm(block_set)
    block_sent, level_zero = lax.optimization_barrier((block_set, level_zero))
    plan, own_plan, staged = make_plan(
        row_count, cols,
        sources.reshape(levels, 1, capacity), targets.reshape(levels, 1, capacity),
        counts.reshape(levels), block_own,
    )
    both = [block_own, in_hbm(from_other_core(block_sent))]

    send = update(
        [(0, 0, 0)], [own_plan], both[:1], [zero_own], None, row_count, "whole", {(0, 0): staged}, None
    )
    send, zero_sent, plan_sent = lax.optimization_barrier((send, level_zero, plan))
    received = exchange(send)
    zero_other = sibling_values(zero_sent, 1)
    plans = [own_plan, from_other_core(plan_sent)]
    second, staged, plans[1] = update(
        [(1, 0, 0), (1, 1, 1)], plans, both, [zero_own, zero_other], None, row_count, "summed",
        {}, (0, 1), True,
    )
    received, second, staged = lax.optimization_barrier((received, second, staged))
    level_one, one_kept, one_sent = sub_solve(received, right_sub, factor_sub)
    one_row = lax.all_to_all(one_sent, ("pcol", "zgrid"), 0, 0, tiled=True)

    resident = {(0, 1): staged}
    second, resident[(1, 1)] = update(
        [(3, 0, 0)], plans, both, [[one_kept] * cols], second, row_count, "summed", resident, (1, 1)
    )
    send = update(
        [(4, 0, 0), (3, 1, 1), (4, 1, 1)], plans, both, [[one_row] * cols] * 2, second,
        row_count, "half", resident, None,
    )
    send, one_row = lax.optimization_barrier((send, one_row))
    received = exchange(send)
    third, staged = update(
        [(2, 0, 0), (2, 1, 1), (5, 0, 2), (5, 1, 3)], plans, both,
        [zero_own, zero_other] + [[one_row] * cols] * 2, None, row_count, "summed", {}, (0, 2),
    )
    received, third, staged = lax.optimization_barrier((received, third, staged))
    level_two = half_solve(0, received, right_top, factor_top, None)
    two_own = sibling_values(level_two, 0)

    resident = {(0, 2): staged}
    third, resident[(1, 2)] = update(
        [(6, 0, 0), (6, 1, 0)], plans, both, [[level_two] * cols], third, row_count, "summed",
        resident, (1, 2),
    )
    send = update(
        [(7, 0, 0), (7, 1, 0)], plans, both, [two_own], third, row_count, "half", resident, None
    )
    send, level_zero, level_one = lax.optimization_barrier((send, level_zero, level_one))
    halves = half_solve(1, exchange(send), right_top, factor_top, level_two)
    solved_top = join_halves(halves, from_other_core(halves))
    solved_sub = jnp.stack([level_zero, level_one])[None, None, None]
    return (solved_sub, solved_top)


def solution(mesh):
    in_specs = (
        P("prow", "pcol", "zgrid", None, None, None, None),
        P("prow", "pcol", "zgrid", None, None),
        P("prow", "pcol", "zgrid", None, None),
        P("prow", "pcol", "zgrid", None),
        P("prow", "pcol", "zgrid", None, None, None),
        P("prow", "pcol", None, None, None),
        P("prow", "pcol", "zgrid", None, None, None),
        P("prow", "pcol", None, None, None),
    )
    out_specs = (P("prow", "pcol", "zgrid", None, None, None), P("prow", "pcol", None, None, None))
    return jax.shard_map(local, mesh=mesh, in_specs=in_specs, out_specs=out_specs, check_vma=False)
```

```python
import functools

import jax
import jax.numpy as jnp
from jax import lax
from jax.experimental import pallas as pl
from jax.experimental.pallas import tpu as pltpu
from jax.sharding import PartitionSpec as P

slot_group = 8
batch = 4
field = 10
field_mask = (1 << field) - 1
pairs = ((0, 1), (0, 2), (0, 3), (1, 2), (1, 2), (1, 3), (2, 3), (2, 3))
params = pltpu.CompilerParams(vmem_limit_bytes=24 * 1024 * 1024)
vmem = pl.BlockSpec(memory_space=pltpu.VMEM)
smem = pl.BlockSpec(memory_space=pltpu.SMEM)
hbm = pl.BlockSpec(memory_space=pltpu.HBM)
anywhere = pl.BlockSpec(memory_space=pl.ANY)


def sibling_values(value, layers):
    cols = lax.axis_size("pcol")
    depth = lax.axis_size("zgrid")
    found = []
    for k in reversed(range(cols)):
        if k == 0 and layers == 0:
            found.append(value)
            continue
        moves = []
        for c in range(cols):
            for z in range(depth):
                target = ((c - k) % cols) * depth + (z - layers) % depth
                moves.append((c * depth + z, target))
        found.append(lax.ppermute(value, ("pcol", "zgrid"), moves))
    return found[::-1]


def from_other_core(value):
    return lax.ppermute(value, "zgrid", [(0, 1), (1, 0)])


def in_hbm(value):
    return pltpu.with_memory_space_constraint(value, pltpu.HBM)


def plan_kernel(row_count, cols, sources_in, targets_in, counts_in, blocks, plan, kept, staged, *scratch):
    sources, targets, counts, semaphores = scratch
    loads = [
        pltpu.make_async_copy(sources_in, sources, semaphores.at[0]),
        pltpu.make_async_copy(targets_in, targets, semaphores.at[1]),
        pltpu.make_async_copy(counts_in, counts, semaphores.at[2]),
    ]
    for load in loads:
        load.start()
    stage = pltpu.make_async_copy(blocks.at[0], staged, semaphores.at[3])
    stage.start()
    for load in loads:
        load.wait()
    me = lax.axis_index("pcol")
    spare = row_count << field
    width = plan.shape[1]
    for level in range(3):
        first_list = pairs.index((level, level + 1))
        steps = 3 - level
        lists = sum(pair[0] == level for pair in pairs)

        def one_slot(slot, found):
            target = targets[level, 0, slot]
            higher = [(target >= (level + j) * row_count).astype(jnp.int32) for j in range(1, steps)]
            step = sum(higher, jnp.int32(0))
            row = target - (level + step) * row_count
            column = sources[level, 0, slot] - me
            column = jnp.where(column < 0, column + cols, column)
            kind = step
            if lists > steps:
                kind = step + ((step > 0) | (column > 0)).astype(jnp.int32)
            place = found[lists - 1]
            for j in range(lists - 1):
                place = jnp.where(kind == j, found[j], place)
            entry = (slot << (2 * field)) + (row << field) + column
            plan[first_list + kind, place] = entry
            kept[first_list + kind, place] = entry
            return tuple(found[j] + (kind == j).astype(jnp.int32) for j in range(lists))

        found = lax.fori_loop(0, counts[level], one_slot, (jnp.int32(0),) * lists)
        for j in range(lists):
            plan[first_list + j, width - 1] = found[j]
            kept[first_list + j, width - 1] = found[j]
            for extra in range(slot_group):
                plan[first_list + j, found[j] + extra] = spare
                kept[first_list + j, found[j] + extra] = spare
    stage.wait()


def make_plan(row_count, cols, sources, targets, counts, blocks):
    width = -(-(sources.shape[-1] + slot_group + 1) // 128) * 128
    return pl.pallas_call(
        functools.partial(plan_kernel, row_count, cols),
        out_shape=[
            jax.ShapeDtypeStruct((len(pairs), width), jnp.int32),
            pltpu.SMEM((len(pairs), width), jnp.int32),
            pltpu.VMEM(blocks.shape[1:], blocks.dtype),
        ],
        in_specs=[hbm] * 4,
        out_specs=[smem, smem, vmem],
        scratch_shapes=[
            pltpu.SMEM(sources.shape, jnp.int32),
            pltpu.SMEM(targets.shape, jnp.int32),
            pltpu.SMEM(counts.shape, jnp.int32),
            pltpu.SemaphoreType.DMA((4,)),
        ],
        compiler_params=params,
    )(in_hbm(sources), in_hbm(targets), in_hbm(counts), blocks)


def low_lanes(value):
    return lax.broadcasted_iota(jnp.int32, value.shape, 1) < value.shape[1] // 2


def turned(value):
    return pltpu.roll(value, value.shape[1] // 2, 1)


def half_first(value):
    return jnp.where(lax.axis_index("zgrid") == 0, value, turned(value))


def packed(value):
    half = value.shape[0] // 2
    upper = value[:half]
    return jnp.where(low_lanes(upper), upper, turned(value[half:]))


def unpacked(value):
    return jnp.concatenate([value, turned(value)], axis=0)


def exchange_order(row_count):
    return [(row + row_count // 2) % row_count for row in range(row_count)]


def fetched_levels(lists, resident):
    needed = dict.fromkeys((layer, pairs[pair][0]) for pair, layer, _ in lists)
    return [key for key in needed if key not in resident]


def update_kernel(config, *refs):
    lists, layer_count, groups_of_solutions, cols, row_count, resident, stages, carries, keeps_plan, form = config
    refs = list(refs)
    plans_in = [refs.pop(0) for _ in range(layer_count)]
    blocks = [refs.pop(0) for _ in range(layer_count)]
    solutions = [refs.pop(0) for _ in range(groups_of_solutions * cols)]
    places = {key: refs.pop(0) for key in resident}
    total_in = refs.pop(0) if carries else None
    out = refs.pop(0)
    next_ref = refs.pop(0) if stages else None
    plans = list(plans_in)
    if keeps_plan:
        plans[1] = refs.pop(0)
    chosen, total, plan_semaphore, semaphores = refs[:4]
    fetched = fetched_levels(lists, resident + ((stages,) if stages else ()))

    plan_loads = []
    if keeps_plan:
        plan_loads.append(pltpu.make_async_copy(plans_in[1], plans[1], plan_semaphore))
    loads = {
        key: pltpu.make_async_copy(blocks[key[0]].at[key[1]], refs[4].at[k], semaphores.at[k])
        for k, key in enumerate(fetched)
    }
    for load in plan_loads + list(loads.values()):
        load.start()
    places.update({key: refs[4].at[k] for k, key in enumerate(fetched)})
    if stages:
        places[stages] = next_ref
        loads[stages] = pltpu.make_async_copy(
            blocks[stages[0]].at[stages[1]], next_ref, semaphores.at[len(fetched)]
        )
        loads[stages].start()

    for j, solution_ref in enumerate(solutions):
        if form == "whole":
            chosen[j] = solution_ref[...]
        elif solution_ref.shape == chosen.shape[1:]:
            chosen[j] = half_first(solution_ref[...].astype(jnp.float32)).astype(jnp.bfloat16)
        else:
            chosen[j] = unpacked(solution_ref[...].astype(jnp.float32)).astype(jnp.bfloat16)
    if carries:
        total[:row_count] = total_in[...]
    else:
        total[...] = jnp.zeros_like(total)
    for load in plan_loads:
        load.wait()

    for pair, layer, j in lists:
        key = (layer, pairs[pair][0])
        if key in loads:
            loads.pop(key).wait()
        pieces = places[key]

        def one_group(g, unused):
            for first in range(0, slot_group, batch):
                entries = [plans[layer][pair, g * slot_group + first + s] for s in range(batch)]
                products = [
                    jnp.dot(
                        pieces[lax.shift_right_logical(entry, 2 * field)],
                        chosen[j * cols + (entry & field_mask)],
                        preferred_element_type=jnp.float32,
                    )
                    for entry in entries
                ]
                for entry, product in zip(entries, products):
                    total[lax.shift_right_logical(entry, field) & field_mask] += product
            return unused

        live = plans[layer][pair, plans[layer].shape[1] - 1]
        lax.fori_loop(0, (live + slot_group - 1) // slot_group, one_group, 0)

    if form == "summed":
        out[...] = total[:row_count]
    else:
        for k, row in enumerate(exchange_order(row_count)):
            value = total[row] if form == "whole" else packed(total[row])
            out[k] = value.astype(jnp.bfloat16)
    for load in loads.values():
        load.wait()


def update(
    lists, plans, blocks, solution_groups, total_in, row_count, form, resident, stages, keeps_plan=False
):
    cols = len(solution_groups[0])
    width, sides = blocks[0].shape[-1], solution_groups[0][0].shape[-1]
    solutions = [part for group in solution_groups for part in group]
    operands = plans + blocks + solutions
    specs = [smem] * len(plans) + [hbm] * len(blocks) + [vmem] * len(solutions)
    for extra in list(resident.values()) + [total_in]:
        if extra is not None:
            operands.append(extra)
            specs.append(vmem)
    fetched = fetched_levels(lists, tuple(resident) + ((stages,) if stages else ()))
    shape = (row_count, width, sides)
    if form == "half":
        shape = (row_count, width // 2, sides)
    if form == "summed":
        outs = [jax.ShapeDtypeStruct(shape, jnp.float32)]
    else:
        outs = [pltpu.VMEM(shape, jnp.bfloat16)]
    if stages:
        outs.append(pltpu.VMEM(blocks[0].shape[1:], blocks[0].dtype))
    places = [vmem] * len(outs)
    if keeps_plan:
        specs[1] = anywhere
        outs.append(pltpu.SMEM(plans[1].shape, jnp.int32))
        places.append(smem)
    config = (
        lists, len(plans), len(solution_groups), cols, row_count, tuple(resident), stages,
        total_in is not None, keeps_plan, form,
    )
    scratch = [
        pltpu.VMEM((len(solutions), width, sides), jnp.bfloat16),
        pltpu.VMEM((row_count + 1, width, sides), jnp.float32),
        pltpu.SemaphoreType.DMA,
        pltpu.SemaphoreType.DMA((len(fetched) + 1,)),
    ]
    if fetched:
        scratch.append(pltpu.VMEM((len(fetched),) + blocks[0].shape[1:], jnp.bfloat16))
    found = pl.pallas_call(
        functools.partial(update_kernel, config),
        out_shape=outs,
        in_specs=specs,
        out_specs=places,
        scratch_shapes=scratch,
        compiler_params=params,
    )(*operands)
    return found if len(outs) > 1 else found[0]


def first_solve_kernel(given, inverse, out, right, factor, semaphores):
    loads = [
        pltpu.make_async_copy(given.at[0], right, semaphores.at[0]),
        pltpu.make_async_copy(inverse.at[0], factor, semaphores.at[1]),
    ]
    for load in loads:
        load.start()
    for load in loads:
        load.wait()
    out[...] = solve_block(factor[...], right[...])


def first_solve(given, inverse):
    shape = given.shape[1:]
    return pl.pallas_call(
        first_solve_kernel,
        out_shape=jax.ShapeDtypeStruct(shape, jnp.bfloat16),
        in_specs=[hbm] * 2,
        out_specs=vmem,
        scratch_shapes=[
            pltpu.VMEM(shape, jnp.bfloat16),
            pltpu.VMEM(inverse.shape[1:], jnp.bfloat16),
            pltpu.SemaphoreType.DMA((2,)),
        ],
        compiler_params=params,
    )(in_hbm(given), in_hbm(inverse))


def sub_solve_kernel(received, given, inverse, out, kept, sent):
    incoming = received[0].astype(jnp.float32)
    for row in range(1, received.shape[0]):
        incoming = incoming + received[row].astype(jnp.float32)
    residual = (given[1].astype(jnp.float32) - incoming).astype(jnp.bfloat16)
    found = jnp.dot(inverse[1], residual, preferred_element_type=jnp.float32)
    out[...] = found.astype(jnp.bfloat16)
    mine = half_first(found)
    kept[...] = packed(mine).astype(jnp.bfloat16)
    sent[...] = packed(turned(mine)).astype(jnp.bfloat16)


def sub_solve(received, given, inverse):
    _, width, sides = received.shape
    half = jax.ShapeDtypeStruct((width // 2, sides), jnp.bfloat16)
    return pl.pallas_call(
        sub_solve_kernel,
        out_shape=[jax.ShapeDtypeStruct((width, sides), jnp.bfloat16), half, half],
        in_specs=[vmem] * 3,
        out_specs=[vmem] * 3,
        compiler_params=params,
    )(received, given, inverse)


def half_solve_kernel(level, received, given, inverse, *refs):
    incoming = received[0].astype(jnp.float32)
    for row in range(1, received.shape[0]):
        incoming = incoming + received[row].astype(jnp.float32)
    right = half_first(given[level].astype(jnp.float32))
    residual = (right - unpacked(incoming)).astype(jnp.bfloat16)
    found = jnp.dot(inverse[level], residual, preferred_element_type=jnp.float32)
    found = packed(found).astype(jnp.bfloat16)
    if len(refs) == 1:
        refs[0][...] = found
    else:
        earlier, out = refs
        out[0] = earlier[...]
        out[1] = found


def half_solve(level, received, given, inverse, earlier):
    shape = received.shape[1:]
    operands = [received, given, inverse] + ([] if earlier is None else [earlier])
    return pl.pallas_call(
        functools.partial(half_solve_kernel, level),
        out_shape=jax.ShapeDtypeStruct(shape if earlier is None else (2,) + shape, jnp.bfloat16),
        in_specs=[vmem] * len(operands),
        out_specs=vmem,
        compiler_params=params,
    )(*operands)


def join_kernel(own, other, out):
    first_core = lax.axis_index("zgrid") == 0
    for level in range(own.shape[0]):
        mine, theirs = own[level].astype(jnp.float32), other[level].astype(jnp.float32)
        first = unpacked(jnp.where(first_core, mine, theirs))
        second = unpacked(jnp.where(first_core, theirs, mine))
        out[0, 0, level] = jnp.where(low_lanes(first), first, turned(second)).astype(jnp.bfloat16)


def join_halves(own, other):
    levels, half, sides = own.shape
    return pl.pallas_call(
        join_kernel,
        out_shape=jax.ShapeDtypeStruct((1, 1, levels, 2 * half, sides), jnp.bfloat16),
        in_specs=[vmem, vmem],
        out_specs=vmem,
        compiler_params=params,
    )(own, other)


def solve_block(inverse, residual):
    return jnp.dot(inverse, residual, preferred_element_type=jnp.float32).astype(jnp.bfloat16)


def exchange(send):
    order = exchange_order(lax.axis_size("prow"))
    return lax.all_to_all(send, "prow", 0, 0, tiled=True, axis_index_groups=[order])


def local(blocks, sources, targets, counts, given_sub, given_top, inverse_sub, inverse_top):
    row_count = lax.axis_size("prow")
    cols = lax.axis_size("pcol")
    levels, capacity = sources.shape[3:]
    block_set = blocks[0, 0, 0]
    right_sub = given_sub[0, 0, 0]
    factor_sub = inverse_sub[0, 0, 0]
    right_top = given_top[0, 0]
    factor_top = inverse_top[0, 0]

    level_zero = first_solve(right_sub, factor_sub)
    zero_own = sibling_values(level_zero, 0)
    block_own = in_hbm(block_set)
    block_sent, level_zero = lax.optimization_barrier((block_set, level_zero))
    plan, own_plan, staged = make_plan(
        row_count, cols,
        sources.reshape(levels, 1, capacity), targets.reshape(levels, 1, capacity),
        counts.reshape(levels), block_own,
    )
    both = [block_own, in_hbm(from_other_core(block_sent))]

    send = update(
        [(0, 0, 0)], [own_plan], both[:1], [zero_own], None, row_count, "whole", {(0, 0): staged}, None
    )
    send, zero_sent, plan_sent = lax.optimization_barrier((send, level_zero, plan))
    received = exchange(send)
    zero_other = sibling_values(zero_sent, 1)
    plans = [own_plan, from_other_core(plan_sent)]
    second, staged, plans[1] = update(
        [(1, 0, 0), (1, 1, 1)], plans, both, [zero_own, zero_other], None, row_count, "summed",
        {}, (0, 1), True,
    )
    received, second, staged = lax.optimization_barrier((received, second, staged))
    level_one, one_kept, one_sent = sub_solve(received, right_sub, factor_sub)
    one_own = sibling_values(one_kept, 0)
    one_other = sibling_values(one_sent, 1)

    resident = {(0, 1): staged}
    second, resident[(1, 1)] = update(
        [(3, 0, 0)], plans, both, [[one_kept] * cols], second, row_count, "summed", resident, (1, 1)
    )
    send = update(
        [(4, 0, 0), (3, 1, 1), (4, 1, 1)], plans, both, [one_own, one_other], second, row_count,
        "half", resident, None,
    )
    send, one_own, one_other = lax.optimization_barrier((send, one_own, one_other))
    received = exchange(send)
    third, staged = update(
        [(2, 0, 0), (2, 1, 1), (5, 0, 2), (5, 1, 3)], plans, both,
        [zero_own, zero_other, one_own, one_other], None, row_count, "summed", {}, (0, 2),
    )
    received, third, staged = lax.optimization_barrier((received, third, staged))
    level_two = half_solve(0, received, right_top, factor_top, None)
    two_own = sibling_values(level_two, 0)

    resident = {(0, 2): staged}
    third, resident[(1, 2)] = update(
        [(6, 0, 0), (6, 1, 0)], plans, both, [[level_two] * cols], third, row_count, "summed",
        resident, (1, 2),
    )
    send = update(
        [(7, 0, 0), (7, 1, 0)], plans, both, [two_own], third, row_count, "half", resident, None
    )
    send, level_zero, level_one = lax.optimization_barrier((send, level_zero, level_one))
    halves = half_solve(1, exchange(send), right_top, factor_top, level_two)
    solved_top = join_halves(halves, from_other_core(halves))
    solved_sub = jnp.stack([level_zero, level_one])[None, None, None]
    return (solved_sub, solved_top)


def solution(mesh):
    in_specs = (
        P("prow", "pcol", "zgrid", None, None, None, None),
        P("prow", "pcol", "zgrid", None, None),
        P("prow", "pcol", "zgrid", None, None),
        P("prow", "pcol", "zgrid", None),
        P("prow", "pcol", "zgrid", None, None, None),
        P("prow", "pcol", None, None, None),
        P("prow", "pcol", "zgrid", None, None, None),
        P("prow", "pcol", None, None, None),
    )
    out_specs = (P("prow", "pcol", "zgrid", None, None, None), P("prow", "pcol", None, None, None))
    return jax.shard_map(local, mesh=mesh, in_specs=in_specs, out_specs=out_specs, check_vma=False)
```

```python
import functools

import jax
import jax.numpy as jnp
from jax import lax
from jax.experimental import pallas as pl
from jax.experimental.pallas import tpu as pltpu
from jax.sharding import PartitionSpec as P

slot_group = 8
batch = 4
field = 10
field_mask = (1 << field) - 1
pairs = ((0, 1), (0, 2), (0, 3), (1, 2), (1, 2), (1, 3), (2, 3), (2, 3))
params = pltpu.CompilerParams(vmem_limit_bytes=24 * 1024 * 1024)
vmem = pl.BlockSpec(memory_space=pltpu.VMEM)
smem = pl.BlockSpec(memory_space=pltpu.SMEM)
hbm = pl.BlockSpec(memory_space=pltpu.HBM)
anywhere = pl.BlockSpec(memory_space=pl.ANY)


def sibling_values(value, layers):
    cols = lax.axis_size("pcol")
    depth = lax.axis_size("zgrid")
    found = []
    for k in reversed(range(cols)):
        if k == 0 and layers == 0:
            found.append(value)
            continue
        moves = []
        for c in range(cols):
            for z in range(depth):
                target = ((c - k) % cols) * depth + (z - layers) % depth
                moves.append((c * depth + z, target))
        found.append(lax.ppermute(value, ("pcol", "zgrid"), moves))
    return found[::-1]


def from_other_core(value):
    return lax.ppermute(value, "zgrid", [(0, 1), (1, 0)])


def in_hbm(value):
    return pltpu.with_memory_space_constraint(value, pltpu.HBM)


def plan_kernel(row_count, cols, sources_in, targets_in, counts_in, blocks, plan, kept, staged, *scratch):
    sources, targets, counts, semaphores = scratch
    loads = [
        pltpu.make_async_copy(sources_in, sources, semaphores.at[0]),
        pltpu.make_async_copy(targets_in, targets, semaphores.at[1]),
        pltpu.make_async_copy(counts_in, counts, semaphores.at[2]),
    ]
    for load in loads:
        load.start()
    stage = pltpu.make_async_copy(blocks.at[0], staged, semaphores.at[3])
    stage.start()
    for load in loads:
        load.wait()
    me = lax.axis_index("pcol")
    spare = row_count << field
    width = plan.shape[1]
    live = [counts[level] for level in range(3)]

    def one_slot(slot, found):
        found = list(found)
        for level in range(3):
            first_list = pairs.index((level, level + 1))
            steps = 3 - level
            lists = sum(pair[0] == level for pair in pairs)
            target = targets[level, 0, slot]
            higher = [(target >= (level + j) * row_count).astype(jnp.int32) for j in range(1, steps)]
            step = sum(higher, jnp.int32(0))
            row = target - (level + step) * row_count
            column = sources[level, 0, slot] - me
            column = jnp.where(column < 0, column + cols, column)
            kind = step
            if lists > steps:
                kind = step + ((step > 0) | (column > 0)).astype(jnp.int32)
            alive = slot < live[level]
            place = found[first_list + lists - 1]
            for j in range(lists - 1):
                place = jnp.where(kind == j, found[first_list + j], place)
            place = jnp.where(alive, place, width - 2)
            entry = (slot << (2 * field)) + (row << field) + column
            plan[first_list + kind, place] = entry
            kept[first_list + kind, place] = entry
            for j in range(lists):
                found[first_list + j] += ((kind == j) & alive).astype(jnp.int32)
        return tuple(found)

    found = lax.fori_loop(
        0, sources.shape[2], one_slot, (jnp.int32(0),) * len(pairs), unroll=2
    )
    for which in range(len(pairs)):
        plan[which, width - 1] = found[which]
        kept[which, width - 1] = found[which]
        for extra in range(slot_group):
            plan[which, found[which] + extra] = spare
            kept[which, found[which] + extra] = spare
    stage.wait()


def make_plan(row_count, cols, sources, targets, counts, blocks):
    width = -(-(sources.shape[-1] + slot_group + 2) // 128) * 128
    return pl.pallas_call(
        functools.partial(plan_kernel, row_count, cols),
        out_shape=[
            jax.ShapeDtypeStruct((len(pairs), width), jnp.int32),
            pltpu.SMEM((len(pairs), width), jnp.int32),
            pltpu.VMEM(blocks.shape[1:], blocks.dtype),
        ],
        in_specs=[hbm] * 4,
        out_specs=[smem, smem, vmem],
        scratch_shapes=[
            pltpu.SMEM(sources.shape, jnp.int32),
            pltpu.SMEM(targets.shape, jnp.int32),
            pltpu.SMEM(counts.shape, jnp.int32),
            pltpu.SemaphoreType.DMA((4,)),
        ],
        compiler_params=params,
    )(in_hbm(sources), in_hbm(targets), in_hbm(counts), blocks)


def low_lanes(value):
    return lax.broadcasted_iota(jnp.int32, value.shape, 1) < value.shape[1] // 2


def turned(value):
    return pltpu.roll(value, value.shape[1] // 2, 1)


def half_first(value):
    return jnp.where(lax.axis_index("zgrid") == 0, value, turned(value))


def packed(value):
    half = value.shape[0] // 2
    upper = value[:half]
    return jnp.where(low_lanes(upper), upper, turned(value[half:]))


def unpacked(value):
    return jnp.concatenate([value, turned(value)], axis=0)


def exchange_order(row_count):
    return [(row + row_count // 2) % row_count for row in range(row_count)]


def fetched_levels(lists, resident):
    needed = dict.fromkeys((layer, pairs[pair][0]) for pair, layer, _ in lists)
    return [key for key in needed if key not in resident]


def update_kernel(config, *refs):
    lists, layer_count, groups_of_solutions, cols, row_count, resident, stages, carries, keeps_plan, form = config
    refs = list(refs)
    plans_in = [refs.pop(0) for _ in range(layer_count)]
    blocks = [refs.pop(0) for _ in range(layer_count)]
    solutions = [refs.pop(0) for _ in range(groups_of_solutions * cols)]
    places = {key: refs.pop(0) for key in resident}
    total_in = refs.pop(0) if carries else None
    out = refs.pop(0)
    next_ref = refs.pop(0) if stages else None
    plans = list(plans_in)
    if keeps_plan:
        plans[1] = refs.pop(0)
    chosen, total, plan_semaphore, semaphores = refs[:4]
    fetched = fetched_levels(lists, resident + ((stages,) if stages else ()))

    plan_loads = []
    if keeps_plan:
        plan_loads.append(pltpu.make_async_copy(plans_in[1], plans[1], plan_semaphore))
    loads = {
        key: pltpu.make_async_copy(blocks[key[0]].at[key[1]], refs[4].at[k], semaphores.at[k])
        for k, key in enumerate(fetched)
    }
    for load in plan_loads + list(loads.values()):
        load.start()
    places.update({key: refs[4].at[k] for k, key in enumerate(fetched)})
    if stages:
        places[stages] = next_ref
        loads[stages] = pltpu.make_async_copy(
            blocks[stages[0]].at[stages[1]], next_ref, semaphores.at[len(fetched)]
        )
        loads[stages].start()

    for j, solution_ref in enumerate(solutions):
        if solution_ref.shape == chosen.shape[1:]:
            chosen[j] = solution_ref[...]
        else:
            chosen[j] = unpacked(solution_ref[...].astype(jnp.float32)).astype(jnp.bfloat16)
    if carries:
        total[:row_count] = total_in[...]
    else:
        total[...] = jnp.zeros_like(total)
    for load in plan_loads:
        load.wait()

    for pair, layer, j in lists:
        key = (layer, pairs[pair][0])
        if key in loads:
            loads.pop(key).wait()
        pieces = places[key]

        def one_group(g, unused):
            for first in range(0, slot_group, batch):
                entries = [plans[layer][pair, g * slot_group + first + s] for s in range(batch)]
                products = [
                    jnp.dot(
                        pieces[lax.shift_right_logical(entry, 2 * field)],
                        chosen[j * cols + (entry & field_mask)],
                        preferred_element_type=jnp.float32,
                    )
                    for entry in entries
                ]
                for entry, product in zip(entries, products):
                    total[lax.shift_right_logical(entry, field) & field_mask] += product
            return unused

        live = plans[layer][pair, plans[layer].shape[1] - 1]
        lax.fori_loop(0, (live + slot_group - 1) // slot_group, one_group, 0)

    if form == "summed":
        out[...] = total[:row_count]
    elif form == "turned":
        for row in range(row_count):
            out[row] = half_first(total[row])
    else:
        for k, row in enumerate(exchange_order(row_count)):
            value = half_first(total[row]) if form == "half" else total[row]
            out[k] = (value if form == "whole" else packed(value)).astype(jnp.bfloat16)
    for load in loads.values():
        load.wait()


def update(
    lists, plans, blocks, solution_groups, total_in, row_count, form, resident, stages, keeps_plan=False
):
    cols = len(solution_groups[0])
    width, sides = blocks[0].shape[-1], solution_groups[0][0].shape[-1]
    solutions = [part for group in solution_groups for part in group]
    operands = plans + blocks + solutions
    specs = [smem] * len(plans) + [hbm] * len(blocks) + [vmem] * len(solutions)
    for extra in list(resident.values()) + [total_in]:
        if extra is not None:
            operands.append(extra)
            specs.append(vmem)
    fetched = fetched_levels(lists, tuple(resident) + ((stages,) if stages else ()))
    shape = (row_count, width, sides)
    if form in ("half", "rest"):
        shape = (row_count, width // 2, sides)
    if form in ("summed", "turned"):
        outs = [jax.ShapeDtypeStruct(shape, jnp.float32)]
    else:
        outs = [pltpu.VMEM(shape, jnp.bfloat16)]
    if stages:
        outs.append(pltpu.VMEM(blocks[0].shape[1:], blocks[0].dtype))
    places = [vmem] * len(outs)
    if keeps_plan:
        specs[1] = anywhere
        outs.append(pltpu.SMEM(plans[1].shape, jnp.int32))
        places.append(smem)
    config = (
        lists, len(plans), len(solution_groups), cols, row_count, tuple(resident), stages,
        total_in is not None, keeps_plan, form,
    )
    scratch = [
        pltpu.VMEM((len(solutions), width, sides), jnp.bfloat16),
        pltpu.VMEM((row_count + 1, width, sides), jnp.float32),
        pltpu.SemaphoreType.DMA,
        pltpu.SemaphoreType.DMA((len(fetched) + 1,)),
    ]
    if fetched:
        scratch.append(pltpu.VMEM((len(fetched),) + blocks[0].shape[1:], jnp.bfloat16))
    found = pl.pallas_call(
        functools.partial(update_kernel, config),
        out_shape=outs,
        in_specs=specs,
        out_specs=places,
        scratch_shapes=scratch,
        compiler_params=params,
    )(*operands)
    return found if len(outs) > 1 else found[0]


def half_solve_kernel(level, received, given, inverse, *refs):
    incoming = received[0].astype(jnp.float32)
    for row in range(1, received.shape[0]):
        incoming = incoming + received[row].astype(jnp.float32)
    right = half_first(given[level].astype(jnp.float32))
    residual = (right - unpacked(incoming)).astype(jnp.bfloat16)
    found = jnp.dot(inverse[level], residual, preferred_element_type=jnp.float32)
    found = packed(found).astype(jnp.bfloat16)
    if len(refs) == 1:
        refs[0][...] = found
    else:
        earlier, out = refs
        out[0] = earlier[...]
        out[1] = found


def half_solve(level, received, given, inverse, earlier):
    shape = received.shape[1:]
    operands = [received, given, inverse] + ([] if earlier is None else [earlier])
    return pl.pallas_call(
        functools.partial(half_solve_kernel, level),
        out_shape=jax.ShapeDtypeStruct(shape if earlier is None else (2,) + shape, jnp.bfloat16),
        in_specs=[vmem] * len(operands),
        out_specs=vmem,
        compiler_params=params,
    )(*operands)


def join_kernel(own, other, out):
    first_core = lax.axis_index("zgrid") == 0
    for level in range(own.shape[0]):
        mine, theirs = own[level].astype(jnp.float32), other[level].astype(jnp.float32)
        first = unpacked(jnp.where(first_core, mine, theirs))
        second = unpacked(jnp.where(first_core, theirs, mine))
        out[0, 0, level] = jnp.where(low_lanes(first), first, turned(second)).astype(jnp.bfloat16)


def join_halves(own, other):
    levels, half, sides = own.shape
    return pl.pallas_call(
        join_kernel,
        out_shape=jax.ShapeDtypeStruct((1, 1, levels, 2 * half, sides), jnp.bfloat16),
        in_specs=[vmem, vmem],
        out_specs=vmem,
        compiler_params=params,
    )(own, other)


def solve_block(inverse, residual):
    return jnp.dot(inverse, residual, preferred_element_type=jnp.float32).astype(jnp.bfloat16)


def reduced_solve(received, given, inverse):
    incoming = jnp.sum(received.astype(jnp.float32), axis=0)
    residual = (given.astype(jnp.float32) - incoming).astype(jnp.bfloat16)
    return solve_block(inverse, residual)


def exchange(send):
    order = exchange_order(lax.axis_size("prow"))
    return lax.all_to_all(send, "prow", 0, 0, tiled=True, axis_index_groups=[order])


def local(blocks, sources, targets, counts, given_sub, given_top, inverse_sub, inverse_top):
    row_count = lax.axis_size("prow")
    cols = lax.axis_size("pcol")
    levels, capacity = sources.shape[3:]
    block_set = blocks[0, 0, 0]
    right_sub = given_sub[0, 0, 0]
    factor_sub = inverse_sub[0, 0, 0]
    right_top = given_top[0, 0]
    factor_top = inverse_top[0, 0]

    level_zero = solve_block(factor_sub[0], right_sub[0])
    zero_own = sibling_values(level_zero, 0)
    block_own = in_hbm(block_set)
    block_sent, level_zero = lax.optimization_barrier((block_set, level_zero))
    plan, own_plan, staged = make_plan(
        row_count, cols,
        sources.reshape(levels, 1, capacity), targets.reshape(levels, 1, capacity),
        counts.reshape(levels), block_own,
    )
    both = [block_own, in_hbm(from_other_core(block_sent))]

    send = update(
        [(0, 0, 0)], [own_plan], both[:1], [zero_own], None, row_count, "whole", {(0, 0): staged}, None
    )
    send, zero_sent, plan_sent = lax.optimization_barrier((send, level_zero, plan))
    received = exchange(send)
    zero_other = sibling_values(zero_sent, 1)
    plans = [own_plan, from_other_core(plan_sent)]
    second, staged, plans[1] = update(
        [(1, 0, 0), (1, 1, 1)], plans, both, [zero_own, zero_other], None, row_count, "summed",
        {}, (0, 1), True,
    )
    received, second, staged = lax.optimization_barrier((received, second, staged))
    level_one = reduced_solve(received, right_sub[1], factor_sub[1])
    one_own = sibling_values(level_one, 0)
    one_other = sibling_values(level_one, 1)

    resident = {(0, 1): staged}
    second, resident[(1, 1)] = update(
        [(3, 0, 0)], plans, both, [[level_one] * cols], second, row_count, "summed", resident, (1, 1)
    )
    send = update(
        [(4, 0, 0), (3, 1, 1), (4, 1, 1)], plans, both, [one_own, one_other], second, row_count,
        "half", resident, None,
    )
    send, one_own, one_other = lax.optimization_barrier((send, one_own, one_other))
    received = exchange(send)
    third, staged = update(
        [(2, 0, 0), (2, 1, 1), (5, 0, 2), (5, 1, 3)], plans, both,
        [zero_own, zero_other, one_own, one_other], None, row_count, "turned", {}, (0, 2),
    )
    received, third, staged = lax.optimization_barrier((received, third, staged))
    level_two = half_solve(0, received, right_top, factor_top, None)
    two_own = sibling_values(level_two, 0)

    resident = {(0, 2): staged}
    third, resident[(1, 2)] = update(
        [(6, 0, 0), (6, 1, 0)], plans, both, [[level_two] * cols], third, row_count, "summed",
        resident, (1, 2),
    )
    send = update(
        [(7, 0, 0), (7, 1, 0)], plans, both, [two_own], third, row_count, "rest", resident, None
    )
    send, level_zero, level_one = lax.optimization_barrier((send, level_zero, level_one))
    halves = half_solve(1, exchange(send), right_top, factor_top, level_two)
    solved_top = join_halves(halves, from_other_core(halves))
    solved_sub = jnp.stack([level_zero, level_one])[None, None, None]
    return (solved_sub, solved_top)


def solution(mesh):
    in_specs = (
        P("prow", "pcol", "zgrid", None, None, None, None),
        P("prow", "pcol", "zgrid", None, None),
        P("prow", "pcol", "zgrid", None, None),
        P("prow", "pcol", "zgrid", None),
        P("prow", "pcol", "zgrid", None, None, None),
        P("prow", "pcol", None, None, None),
        P("prow", "pcol", "zgrid", None, None, None),
        P("prow", "pcol", None, None, None),
    )
    out_specs = (P("prow", "pcol", "zgrid", None, None, None), P("prow", "pcol", None, None, None))
    return jax.shard_map(local, mesh=mesh, in_specs=in_specs, out_specs=out_specs, check_vma=False)
```

```python
import functools

import jax
import jax.numpy as jnp
from jax import lax
from jax.experimental import pallas as pl
from jax.experimental.pallas import tpu as pltpu
from jax.sharding import PartitionSpec as P

slot_group = 4
batch = 4
field = 10
field_mask = (1 << field) - 1
pairs = ((0, 1), (0, 2), (0, 3), (1, 2), (1, 2), (1, 3), (2, 3), (2, 3))
params = pltpu.CompilerParams(vmem_limit_bytes=24 * 1024 * 1024)
vmem = pl.BlockSpec(memory_space=pltpu.VMEM)
smem = pl.BlockSpec(memory_space=pltpu.SMEM)
hbm = pl.BlockSpec(memory_space=pltpu.HBM)
anywhere = pl.BlockSpec(memory_space=pl.ANY)


def sibling_values(value, layers):
    cols = lax.axis_size("pcol")
    depth = lax.axis_size("zgrid")
    found = []
    for k in reversed(range(cols)):
        if k == 0 and layers == 0:
            found.append(value)
            continue
        moves = []
        for c in range(cols):
            for z in range(depth):
                target = ((c - k) % cols) * depth + (z - layers) % depth
                moves.append((c * depth + z, target))
        found.append(lax.ppermute(value, ("pcol", "zgrid"), moves))
    return found[::-1]


def from_other_core(value):
    return lax.ppermute(value, "zgrid", [(0, 1), (1, 0)])


def in_hbm(value):
    return pltpu.with_memory_space_constraint(value, pltpu.HBM)


def plan_kernel(row_count, cols, sources_in, targets_in, counts_in, blocks, plan, kept, staged, *scratch):
    sources, targets, counts, semaphores = scratch
    loads = [
        pltpu.make_async_copy(sources_in, sources, semaphores.at[0]),
        pltpu.make_async_copy(targets_in, targets, semaphores.at[1]),
        pltpu.make_async_copy(counts_in, counts, semaphores.at[2]),
    ]
    for load in loads:
        load.start()
    stage = pltpu.make_async_copy(blocks.at[0], staged, semaphores.at[3])
    stage.start()
    for load in loads:
        load.wait()
    me = lax.axis_index("pcol")
    spare = row_count << field
    width = plan.shape[1]
    for level in range(3):
        first_list = pairs.index((level, level + 1))
        steps = 3 - level
        lists = sum(pair[0] == level for pair in pairs)

        def one_slot(slot, found):
            target = targets[level, 0, slot]
            higher = [(target >= (level + j) * row_count).astype(jnp.int32) for j in range(1, steps)]
            step = sum(higher, jnp.int32(0))
            row = target - (level + step) * row_count
            column = sources[level, 0, slot] - me
            column = jnp.where(column < 0, column + cols, column)
            kind = step
            if lists > steps:
                kind = step + ((step > 0) | (column > 0)).astype(jnp.int32)
            place = found[lists - 1]
            for j in range(lists - 1):
                place = jnp.where(kind == j, found[j], place)
            entry = (slot << (2 * field)) + (row << field) + column
            plan[first_list + kind, place] = entry
            kept[first_list + kind, place] = entry
            return tuple(found[j] + (kind == j).astype(jnp.int32) for j in range(lists))

        found = lax.fori_loop(0, counts[level], one_slot, (jnp.int32(0),) * lists)
        for j in range(lists):
            plan[first_list + j, width - 1] = found[j]
            kept[first_list + j, width - 1] = found[j]
            for extra in range(slot_group):
                plan[first_list + j, found[j] + extra] = spare
                kept[first_list + j, found[j] + extra] = spare
    stage.wait()


def make_plan(row_count, cols, sources, targets, counts, blocks):
    width = -(-(sources.shape[-1] + slot_group + 1) // 128) * 128
    return pl.pallas_call(
        functools.partial(plan_kernel, row_count, cols),
        out_shape=[
            jax.ShapeDtypeStruct((len(pairs), width), jnp.int32),
            pltpu.SMEM((len(pairs), width), jnp.int32),
            pltpu.VMEM(blocks.shape[1:], blocks.dtype),
        ],
        in_specs=[hbm] * 4,
        out_specs=[smem, smem, vmem],
        scratch_shapes=[
            pltpu.SMEM(sources.shape, jnp.int32),
            pltpu.SMEM(targets.shape, jnp.int32),
            pltpu.SMEM(counts.shape, jnp.int32),
            pltpu.SemaphoreType.DMA((4,)),
        ],
        compiler_params=params,
    )(in_hbm(sources), in_hbm(targets), in_hbm(counts), blocks)


def low_lanes(value):
    return lax.broadcasted_iota(jnp.int32, value.shape, 1) < value.shape[1] // 2


def turned(value):
    return pltpu.roll(value, value.shape[1] // 2, 1)


def half_first(value):
    return jnp.where(lax.axis_index("zgrid") == 0, value, turned(value))


def packed(value):
    half = value.shape[0] // 2
    upper = value[:half]
    return jnp.where(low_lanes(upper), upper, turned(value[half:]))


def unpacked(value):
    return jnp.concatenate([value, turned(value)], axis=0)


def exchange_order(row_count):
    return [(row + row_count // 2) % row_count for row in range(row_count)]


def fetched_levels(lists, resident):
    needed = dict.fromkeys((layer, pairs[pair][0]) for pair, layer, _ in lists)
    return [key for key in needed if key not in resident]


def update_kernel(config, *refs):
    lists, layer_count, groups_of_solutions, cols, row_count, resident, stages, carries, keeps_plan, form = config
    refs = list(refs)
    plans_in = [refs.pop(0) for _ in range(layer_count)]
    blocks = [refs.pop(0) for _ in range(layer_count)]
    solutions = [refs.pop(0) for _ in range(groups_of_solutions * cols)]
    places = {key: refs.pop(0) for key in resident}
    total_in = refs.pop(0) if carries else None
    out = refs.pop(0)
    next_ref = refs.pop(0) if stages else None
    plans = list(plans_in)
    if keeps_plan:
        plans[1] = refs.pop(0)
    chosen, total, plan_semaphore, semaphores = refs[:4]
    fetched = fetched_levels(lists, resident + ((stages,) if stages else ()))

    plan_loads = []
    if keeps_plan:
        plan_loads.append(pltpu.make_async_copy(plans_in[1], plans[1], plan_semaphore))
    loads = {
        key: pltpu.make_async_copy(blocks[key[0]].at[key[1]], refs[4].at[k], semaphores.at[k])
        for k, key in enumerate(fetched)
    }
    for load in plan_loads + list(loads.values()):
        load.start()
    places.update({key: refs[4].at[k] for k, key in enumerate(fetched)})
    if stages:
        places[stages] = next_ref
        loads[stages] = pltpu.make_async_copy(
            blocks[stages[0]].at[stages[1]], next_ref, semaphores.at[len(fetched)]
        )
        loads[stages].start()

    for j, solution_ref in enumerate(solutions):
        if form == "whole":
            chosen[j] = solution_ref[...]
        elif solution_ref.shape == chosen.shape[1:]:
            chosen[j] = half_first(solution_ref[...].astype(jnp.float32)).astype(jnp.bfloat16)
        else:
            chosen[j] = unpacked(solution_ref[...].astype(jnp.float32)).astype(jnp.bfloat16)
    if carries:
        total[:row_count] = total_in[...]
    else:
        total[...] = jnp.zeros_like(total)
    for load in plan_loads:
        load.wait()

    for pair, layer, j in lists:
        key = (layer, pairs[pair][0])
        if key in loads:
            loads.pop(key).wait()
        pieces = places[key]

        def one_group(g, unused):
            for first in range(0, slot_group, batch):
                entries = [plans[layer][pair, g * slot_group + first + s] for s in range(batch)]
                products = [
                    jnp.dot(
                        pieces[lax.shift_right_logical(entry, 2 * field)],
                        chosen[j * cols + (entry & field_mask)],
                        preferred_element_type=jnp.float32,
                    )
                    for entry in entries
                ]
                for entry, product in zip(entries, products):
                    total[lax.shift_right_logical(entry, field) & field_mask] += product
            return unused

        live = plans[layer][pair, plans[layer].shape[1] - 1]
        lax.fori_loop(0, (live + slot_group - 1) // slot_group, one_group, 0)

    if form == "summed":
        out[...] = total[:row_count]
    else:
        for k, row in enumerate(exchange_order(row_count)):
            value = total[row] if form == "whole" else packed(total[row])
            out[k] = value.astype(jnp.bfloat16)
    for load in loads.values():
        load.wait()


def update(
    lists, plans, blocks, solution_groups, total_in, row_count, form, resident, stages, keeps_plan=False
):
    cols = len(solution_groups[0])
    width, sides = blocks[0].shape[-1], solution_groups[0][0].shape[-1]
    solutions = [part for group in solution_groups for part in group]
    operands = plans + blocks + solutions
    specs = [smem] * len(plans) + [hbm] * len(blocks) + [vmem] * len(solutions)
    for extra in list(resident.values()) + [total_in]:
        if extra is not None:
            operands.append(extra)
            specs.append(vmem)
    fetched = fetched_levels(lists, tuple(resident) + ((stages,) if stages else ()))
    shape = (row_count, width, sides)
    if form == "half":
        shape = (row_count, width // 2, sides)
    if form == "summed":
        outs = [jax.ShapeDtypeStruct(shape, jnp.float32)]
    else:
        outs = [pltpu.VMEM(shape, jnp.bfloat16)]
    if stages:
        outs.append(pltpu.VMEM(blocks[0].shape[1:], blocks[0].dtype))
    places = [vmem] * len(outs)
    if keeps_plan:
        specs[1] = anywhere
        outs.append(pltpu.SMEM(plans[1].shape, jnp.int32))
        places.append(smem)
    config = (
        lists, len(plans), len(solution_groups), cols, row_count, tuple(resident), stages,
        total_in is not None, keeps_plan, form,
    )
    scratch = [
        pltpu.VMEM((len(solutions), width, sides), jnp.bfloat16),
        pltpu.VMEM((row_count + 1, width, sides), jnp.float32),
        pltpu.SemaphoreType.DMA,
        pltpu.SemaphoreType.DMA((len(fetched) + 1,)),
    ]
    if fetched:
        scratch.append(pltpu.VMEM((len(fetched),) + blocks[0].shape[1:], jnp.bfloat16))
    found = pl.pallas_call(
        functools.partial(update_kernel, config),
        out_shape=outs,
        in_specs=specs,
        out_specs=places,
        scratch_shapes=scratch,
        compiler_params=params,
    )(*operands)
    return found if len(outs) > 1 else found[0]


def sub_solve_kernel(received, given, inverse, out, kept, sent):
    incoming = received[0].astype(jnp.float32)
    for row in range(1, received.shape[0]):
        incoming = incoming + received[row].astype(jnp.float32)
    residual = (given[1].astype(jnp.float32) - incoming).astype(jnp.bfloat16)
    found = jnp.dot(inverse[1], residual, preferred_element_type=jnp.float32)
    out[...] = found.astype(jnp.bfloat16)
    mine = half_first(found)
    kept[...] = packed(mine).astype(jnp.bfloat16)
    sent[...] = packed(turned(mine)).astype(jnp.bfloat16)


def sub_solve(received, given, inverse):
    _, width, sides = received.shape
    half = jax.ShapeDtypeStruct((width // 2, sides), jnp.bfloat16)
    return pl.pallas_call(
        sub_solve_kernel,
        out_shape=[jax.ShapeDtypeStruct((width, sides), jnp.bfloat16), half, half],
        in_specs=[vmem] * 3,
        out_specs=[vmem] * 3,
        compiler_params=params,
    )(received, given, inverse)


def half_solve_kernel(level, received, given, inverse, *refs):
    incoming = received[0].astype(jnp.float32)
    for row in range(1, received.shape[0]):
        incoming = incoming + received[row].astype(jnp.float32)
    right = half_first(given[level].astype(jnp.float32))
    residual = (right - unpacked(incoming)).astype(jnp.bfloat16)
    found = jnp.dot(inverse[level], residual, preferred_element_type=jnp.float32)
    found = packed(found).astype(jnp.bfloat16)
    if len(refs) == 1:
        refs[0][...] = found
    else:
        earlier, out = refs
        out[0] = earlier[...]
        out[1] = found


def half_solve(level, received, given, inverse, earlier):
    shape = received.shape[1:]
    operands = [received, given, inverse] + ([] if earlier is None else [earlier])
    return pl.pallas_call(
        functools.partial(half_solve_kernel, level),
        out_shape=jax.ShapeDtypeStruct(shape if earlier is None else (2,) + shape, jnp.bfloat16),
        in_specs=[vmem] * len(operands),
        out_specs=vmem,
        compiler_params=params,
    )(*operands)


def join_kernel(own, other, out):
    first_core = lax.axis_index("zgrid") == 0
    for level in range(own.shape[0]):
        mine, theirs = own[level].astype(jnp.float32), other[level].astype(jnp.float32)
        first = unpacked(jnp.where(first_core, mine, theirs))
        second = unpacked(jnp.where(first_core, theirs, mine))
        out[0, 0, level] = jnp.where(low_lanes(first), first, turned(second)).astype(jnp.bfloat16)


def join_halves(own, other):
    levels, half, sides = own.shape
    return pl.pallas_call(
        join_kernel,
        out_shape=jax.ShapeDtypeStruct((1, 1, levels, 2 * half, sides), jnp.bfloat16),
        in_specs=[vmem, vmem],
        out_specs=vmem,
        compiler_params=params,
    )(own, other)


def solve_block(inverse, residual):
    return jnp.dot(inverse, residual, preferred_element_type=jnp.float32).astype(jnp.bfloat16)


def exchange(send):
    order = exchange_order(lax.axis_size("prow"))
    return lax.all_to_all(send, "prow", 0, 0, tiled=True, axis_index_groups=[order])


def local(blocks, sources, targets, counts, given_sub, given_top, inverse_sub, inverse_top):
    row_count = lax.axis_size("prow")
    cols = lax.axis_size("pcol")
    levels, capacity = sources.shape[3:]
    block_set = blocks[0, 0, 0]
    right_sub = given_sub[0, 0, 0]
    factor_sub = inverse_sub[0, 0, 0]
    right_top = given_top[0, 0]
    factor_top = inverse_top[0, 0]

    level_zero = solve_block(factor_sub[0], right_sub[0])
    zero_own = sibling_values(level_zero, 0)
    block_own = in_hbm(block_set)
    block_sent, level_zero = lax.optimization_barrier((block_set, level_zero))
    plan, own_plan, staged = make_plan(
        row_count, cols,
        sources.reshape(levels, 1, capacity), targets.reshape(levels, 1, capacity),
        counts.reshape(levels), block_own,
    )
    both = [block_own, in_hbm(from_other_core(block_sent))]

    send = update(
        [(0, 0, 0)], [own_plan], both[:1], [zero_own], None, row_count, "whole", {(0, 0): staged}, None
    )
    send, zero_sent, plan_sent = lax.optimization_barrier((send, level_zero, plan))
    received = exchange(send)
    zero_other = sibling_values(zero_sent, 1)
    plans = [own_plan, from_other_core(plan_sent)]
    second, staged, plans[1] = update(
        [(1, 0, 0), (1, 1, 1)], plans, both, [zero_own, zero_other], None, row_count, "summed",
        {}, (0, 1), True,
    )
    received, second, staged = lax.optimization_barrier((received, second, staged))
    level_one, one_kept, one_sent = sub_solve(received, right_sub, factor_sub)
    one_own = sibling_values(one_kept, 0)
    one_other = sibling_values(one_sent, 1)

    resident = {(0, 1): staged}
    second, resident[(1, 1)] = update(
        [(3, 0, 0)], plans, both, [[one_kept] * cols], second, row_count, "summed", resident, (1, 1)
    )
    send = update(
        [(4, 0, 0), (3, 1, 1), (4, 1, 1)], plans, both, [one_own, one_other], second, row_count,
        "half", resident, None,
    )
    send, one_own, one_other = lax.optimization_barrier((send, one_own, one_other))
    received = exchange(send)
    third, staged = update(
        [(2, 0, 0), (2, 1, 1), (5, 0, 2), (5, 1, 3)], plans, both,
        [zero_own, zero_other, one_own, one_other], None, row_count, "summed", {}, (0, 2),
    )
    received, third, staged = lax.optimization_barrier((received, third, staged))
    level_two = half_solve(0, received, right_top, factor_top, None)
    two_own = sibling_values(level_two, 0)

    resident = {(0, 2): staged}
    third, resident[(1, 2)] = update(
        [(6, 0, 0), (6, 1, 0)], plans, both, [[level_two] * cols], third, row_count, "summed",
        resident, (1, 2),
    )
    send = update(
        [(7, 0, 0), (7, 1, 0)], plans, both, [two_own], third, row_count, "half", resident, None
    )
    send, level_zero, level_one = lax.optimization_barrier((send, level_zero, level_one))
    halves = half_solve(1, exchange(send), right_top, factor_top, level_two)
    solved_top = join_halves(halves, from_other_core(halves))
    solved_sub = jnp.stack([level_zero, level_one])[None, None, None]
    return (solved_sub, solved_top)


def solution(mesh):
    in_specs = (
        P("prow", "pcol", "zgrid", None, None, None, None),
        P("prow", "pcol", "zgrid", None, None),
        P("prow", "pcol", "zgrid", None, None),
        P("prow", "pcol", "zgrid", None),
        P("prow", "pcol", "zgrid", None, None, None),
        P("prow", "pcol", None, None, None),
        P("prow", "pcol", "zgrid", None, None, None),
        P("prow", "pcol", None, None, None),
    )
    out_specs = (P("prow", "pcol", "zgrid", None, None, None), P("prow", "pcol", None, None, None))
    return jax.shard_map(local, mesh=mesh, in_specs=in_specs, out_specs=out_specs, check_vma=False)
```

```python
import functools

import jax
import jax.numpy as jnp
from jax import lax
from jax.experimental import pallas as pl
from jax.experimental.pallas import tpu as pltpu
from jax.sharding import PartitionSpec as P

slot_group = 8
batch = 8
field = 10
field_mask = (1 << field) - 1
pairs = ((0, 1), (0, 2), (0, 3), (1, 2), (1, 2), (1, 3), (2, 3), (2, 3))
params = pltpu.CompilerParams(vmem_limit_bytes=24 * 1024 * 1024)
vmem = pl.BlockSpec(memory_space=pltpu.VMEM)
smem = pl.BlockSpec(memory_space=pltpu.SMEM)
hbm = pl.BlockSpec(memory_space=pltpu.HBM)
anywhere = pl.BlockSpec(memory_space=pl.ANY)


def sibling_values(value, layers):
    cols = lax.axis_size("pcol")
    depth = lax.axis_size("zgrid")
    found = []
    for k in reversed(range(cols)):
        if k == 0 and layers == 0:
            found.append(value)
            continue
        moves = []
        for c in range(cols):
            for z in range(depth):
                target = ((c - k) % cols) * depth + (z - layers) % depth
                moves.append((c * depth + z, target))
        found.append(lax.ppermute(value, ("pcol", "zgrid"), moves))
    return found[::-1]


def from_other_core(value):
    return lax.ppermute(value, "zgrid", [(0, 1), (1, 0)])


def in_hbm(value):
    return pltpu.with_memory_space_constraint(value, pltpu.HBM)


def plan_kernel(row_count, cols, sources_in, targets_in, counts_in, blocks, plan, kept, staged, *scratch):
    sources, targets, counts, semaphores = scratch
    loads = [
        pltpu.make_async_copy(sources_in, sources, semaphores.at[0]),
        pltpu.make_async_copy(targets_in, targets, semaphores.at[1]),
        pltpu.make_async_copy(counts_in, counts, semaphores.at[2]),
    ]
    for load in loads:
        load.start()
    stage = pltpu.make_async_copy(blocks.at[0], staged, semaphores.at[3])
    stage.start()
    for load in loads:
        load.wait()
    me = lax.axis_index("pcol")
    spare = row_count << field
    width = plan.shape[1]
    for level in range(3):
        first_list = pairs.index((level, level + 1))
        steps = 3 - level
        lists = sum(pair[0] == level for pair in pairs)

        def one_slot(slot, found):
            target = targets[level, 0, slot]
            higher = [(target >= (level + j) * row_count).astype(jnp.int32) for j in range(1, steps)]
            step = sum(higher, jnp.int32(0))
            row = target - (level + step) * row_count
            column = sources[level, 0, slot] - me
            column = jnp.where(column < 0, column + cols, column)
            kind = step
            if lists > steps:
                kind = step + ((step > 0) | (column > 0)).astype(jnp.int32)
            place = found[lists - 1]
            for j in range(lists - 1):
                place = jnp.where(kind == j, found[j], place)
            entry = (slot << (2 * field)) + (row << field) + column
            plan[first_list + kind, place] = entry
            kept[first_list + kind, place] = entry
            return tuple(found[j] + (kind == j).astype(jnp.int32) for j in range(lists))

        found = lax.fori_loop(0, counts[level], one_slot, (jnp.int32(0),) * lists)
        for j in range(lists):
            plan[first_list + j, width - 1] = found[j]
            kept[first_list + j, width - 1] = found[j]
            for extra in range(slot_group):
                plan[first_list + j, found[j] + extra] = spare
                kept[first_list + j, found[j] + extra] = spare
    stage.wait()


def make_plan(row_count, cols, sources, targets, counts, blocks):
    width = -(-(sources.shape[-1] + slot_group + 1) // 128) * 128
    return pl.pallas_call(
        functools.partial(plan_kernel, row_count, cols),
        out_shape=[
            jax.ShapeDtypeStruct((len(pairs), width), jnp.int32),
            pltpu.SMEM((len(pairs), width), jnp.int32),
            pltpu.VMEM(blocks.shape[1:], blocks.dtype),
        ],
        in_specs=[hbm] * 4,
        out_specs=[smem, smem, vmem],
        scratch_shapes=[
            pltpu.SMEM(sources.shape, jnp.int32),
            pltpu.SMEM(targets.shape, jnp.int32),
            pltpu.SMEM(counts.shape, jnp.int32),
            pltpu.SemaphoreType.DMA((4,)),
        ],
        compiler_params=params,
    )(in_hbm(sources), in_hbm(targets), in_hbm(counts), blocks)


def low_lanes(value):
    return lax.broadcasted_iota(jnp.int32, value.shape, 1) < value.shape[1] // 2


def turned(value):
    return pltpu.roll(value, value.shape[1] // 2, 1)


def half_first(value):
    return jnp.where(lax.axis_index("zgrid") == 0, value, turned(value))


def packed(value):
    half = value.shape[0] // 2
    upper = value[:half]
    return jnp.where(low_lanes(upper), upper, turned(value[half:]))


def unpacked(value):
    return jnp.concatenate([value, turned(value)], axis=0)


def exchange_order(row_count):
    return [(row + row_count // 2) % row_count for row in range(row_count)]


def fetched_levels(lists, resident):
    needed = dict.fromkeys((layer, pairs[pair][0]) for pair, layer, _ in lists)
    return [key for key in needed if key not in resident]


def update_kernel(config, *refs):
    lists, layer_count, groups_of_solutions, cols, row_count, resident, stages, carries, keeps_plan, form = config
    refs = list(refs)
    plans_in = [refs.pop(0) for _ in range(layer_count)]
    blocks = [refs.pop(0) for _ in range(layer_count)]
    solutions = [refs.pop(0) for _ in range(groups_of_solutions * cols)]
    places = {key: refs.pop(0) for key in resident}
    total_in = refs.pop(0) if carries else None
    out = refs.pop(0)
    next_ref = refs.pop(0) if stages else None
    plans = list(plans_in)
    if keeps_plan:
        plans[1] = refs.pop(0)
    chosen, total, plan_semaphore, semaphores = refs[:4]
    fetched = fetched_levels(lists, resident + ((stages,) if stages else ()))

    plan_loads = []
    if keeps_plan:
        plan_loads.append(pltpu.make_async_copy(plans_in[1], plans[1], plan_semaphore))
    loads = {
        key: pltpu.make_async_copy(blocks[key[0]].at[key[1]], refs[4].at[k], semaphores.at[k])
        for k, key in enumerate(fetched)
    }
    for load in plan_loads + list(loads.values()):
        load.start()
    places.update({key: refs[4].at[k] for k, key in enumerate(fetched)})
    if stages:
        places[stages] = next_ref
        loads[stages] = pltpu.make_async_copy(
            blocks[stages[0]].at[stages[1]], next_ref, semaphores.at[len(fetched)]
        )
        loads[stages].start()

    for j, solution_ref in enumerate(solutions):
        if solution_ref.shape == chosen.shape[1:]:
            chosen[j] = solution_ref[...]
        else:
            chosen[j] = unpacked(solution_ref[...].astype(jnp.float32)).astype(jnp.bfloat16)
    if carries:
        total[:row_count] = total_in[...]
    else:
        total[...] = jnp.zeros_like(total)
    for load in plan_loads:
        load.wait()

    for pair, layer, j in lists:
        key = (layer, pairs[pair][0])
        if key in loads:
            loads.pop(key).wait()
        pieces = places[key]

        def one_group(g, unused):
            for first in range(0, slot_group, batch):
                entries = [plans[layer][pair, g * slot_group + first + s] for s in range(batch)]
                products = [
                    jnp.dot(
                        pieces[lax.shift_right_logical(entry, 2 * field)],
                        chosen[j * cols + (entry & field_mask)],
                        preferred_element_type=jnp.float32,
                    )
                    for entry in entries
                ]
                for entry, product in zip(entries, products):
                    total[lax.shift_right_logical(entry, field) & field_mask] += product
            return unused

        live = plans[layer][pair, plans[layer].shape[1] - 1]
        lax.fori_loop(0, (live + slot_group - 1) // slot_group, one_group, 0)

    if form == "summed":
        out[...] = total[:row_count]
    elif form == "turned":
        for row in range(row_count):
            out[row] = half_first(total[row])
    else:
        for k, row in enumerate(exchange_order(row_count)):
            value = half_first(total[row]) if form == "half" else total[row]
            out[k] = (value if form == "whole" else packed(value)).astype(jnp.bfloat16)
    for load in loads.values():
        load.wait()


def update(
    lists, plans, blocks, solution_groups, total_in, row_count, form, resident, stages, keeps_plan=False
):
    cols = len(solution_groups[0])
    width, sides = blocks[0].shape[-1], solution_groups[0][0].shape[-1]
    solutions = [part for group in solution_groups for part in group]
    operands = plans + blocks + solutions
    specs = [smem] * len(plans) + [hbm] * len(blocks) + [vmem] * len(solutions)
    for extra in list(resident.values()) + [total_in]:
        if extra is not None:
            operands.append(extra)
            specs.append(vmem)
    fetched = fetched_levels(lists, tuple(resident) + ((stages,) if stages else ()))
    shape = (row_count, width, sides)
    if form in ("half", "rest"):
        shape = (row_count, width // 2, sides)
    if form in ("summed", "turned"):
        outs = [jax.ShapeDtypeStruct(shape, jnp.float32)]
    else:
        outs = [pltpu.VMEM(shape, jnp.bfloat16)]
    if stages:
        outs.append(pltpu.VMEM(blocks[0].shape[1:], blocks[0].dtype))
    places = [vmem] * len(outs)
    if keeps_plan:
        specs[1] = anywhere
        outs.append(pltpu.SMEM(plans[1].shape, jnp.int32))
        places.append(smem)
    config = (
        lists, len(plans), len(solution_groups), cols, row_count, tuple(resident), stages,
        total_in is not None, keeps_plan, form,
    )
    scratch = [
        pltpu.VMEM((len(solutions), width, sides), jnp.bfloat16),
        pltpu.VMEM((row_count + 1, width, sides), jnp.float32),
        pltpu.SemaphoreType.DMA,
        pltpu.SemaphoreType.DMA((len(fetched) + 1,)),
    ]
    if fetched:
        scratch.append(pltpu.VMEM((len(fetched),) + blocks[0].shape[1:], jnp.bfloat16))
    found = pl.pallas_call(
        functools.partial(update_kernel, config),
        out_shape=outs,
        in_specs=specs,
        out_specs=places,
        scratch_shapes=scratch,
        compiler_params=params,
    )(*operands)
    return found if len(outs) > 1 else found[0]


def half_solve_kernel(level, received, given, inverse, *refs):
    incoming = received[0].astype(jnp.float32)
    for row in range(1, received.shape[0]):
        incoming = incoming + received[row].astype(jnp.float32)
    right = half_first(given[level].astype(jnp.float32))
    residual = (right - unpacked(incoming)).astype(jnp.bfloat16)
    found = jnp.dot(inverse[level], residual, preferred_element_type=jnp.float32)
    found = packed(found).astype(jnp.bfloat16)
    if len(refs) == 1:
        refs[0][...] = found
    else:
        earlier, out = refs
        out[0] = earlier[...]
        out[1] = found


def half_solve(level, received, given, inverse, earlier):
    shape = received.shape[1:]
    operands = [received, given, inverse] + ([] if earlier is None else [earlier])
    return pl.pallas_call(
        functools.partial(half_solve_kernel, level),
        out_shape=jax.ShapeDtypeStruct(shape if earlier is None else (2,) + shape, jnp.bfloat16),
        in_specs=[vmem] * len(operands),
        out_specs=vmem,
        compiler_params=params,
    )(*operands)


def join_kernel(own, other, out):
    first_core = lax.axis_index("zgrid") == 0
    for level in range(own.shape[0]):
        mine, theirs = own[level].astype(jnp.float32), other[level].astype(jnp.float32)
        first = unpacked(jnp.where(first_core, mine, theirs))
        second = unpacked(jnp.where(first_core, theirs, mine))
        out[0, 0, level] = jnp.where(low_lanes(first), first, turned(second)).astype(jnp.bfloat16)


def join_halves(own, other):
    levels, half, sides = own.shape
    return pl.pallas_call(
        join_kernel,
        out_shape=jax.ShapeDtypeStruct((1, 1, levels, 2 * half, sides), jnp.bfloat16),
        in_specs=[vmem, vmem],
        out_specs=vmem,
        compiler_params=params,
    )(own, other)


def solve_block(inverse, residual):
    return jnp.dot(inverse, residual, preferred_element_type=jnp.float32).astype(jnp.bfloat16)


def reduced_solve(received, given, inverse):
    incoming = jnp.sum(received.astype(jnp.float32), axis=0)
    residual = (given.astype(jnp.float32) - incoming).astype(jnp.bfloat16)
    return solve_block(inverse, residual)


def exchange(send):
    order = exchange_order(lax.axis_size("prow"))
    return lax.all_to_all(send, "prow", 0, 0, tiled=True, axis_index_groups=[order])


def local(blocks, sources, targets, counts, given_sub, given_top, inverse_sub, inverse_top):
    row_count = lax.axis_size("prow")
    cols = lax.axis_size("pcol")
    levels, capacity = sources.shape[3:]
    block_set = blocks[0, 0, 0]
    right_sub = given_sub[0, 0, 0]
    factor_sub = inverse_sub[0, 0, 0]
    right_top = given_top[0, 0]
    factor_top = inverse_top[0, 0]

    level_zero = solve_block(factor_sub[0], right_sub[0])
    zero_own = sibling_values(level_zero, 0)
    block_own = in_hbm(block_set)
    block_sent, level_zero = lax.optimization_barrier((block_set, level_zero))
    plan, own_plan, staged = make_plan(
        row_count, cols,
        sources.reshape(levels, 1, capacity), targets.reshape(levels, 1, capacity),
        counts.reshape(levels), block_own,
    )
    both = [block_own, in_hbm(from_other_core(block_sent))]

    send = update(
        [(0, 0, 0)], [own_plan], both[:1], [zero_own], None, row_count, "whole", {(0, 0): staged}, None
    )
    send, zero_sent, plan_sent = lax.optimization_barrier((send, level_zero, plan))
    received = exchange(send)
    zero_other = sibling_values(zero_sent, 1)
    plans = [own_plan, from_other_core(plan_sent)]
    second, staged, plans[1] = update(
        [(1, 0, 0), (1, 1, 1)], plans, both, [zero_own, zero_other], None, row_count, "summed",
        {}, (0, 1), True,
    )
    received, second, staged = lax.optimization_barrier((received, second, staged))
    level_one = reduced_solve(received, right_sub[1], factor_sub[1])
    one_own = sibling_values(level_one, 0)
    one_other = sibling_values(level_one, 1)

    resident = {(0, 1): staged}
    second, resident[(1, 1)] = update(
        [(3, 0, 0)], plans, both, [[level_one] * cols], second, row_count, "summed", resident, (1, 1)
    )
    send = update(
        [(4, 0, 0), (3, 1, 1), (4, 1, 1)], plans, both, [one_own, one_other], second, row_count,
        "half", resident, None,
    )
    send, one_own, one_other = lax.optimization_barrier((send, one_own, one_other))
    received = exchange(send)
    third, staged = update(
        [(2, 0, 0), (2, 1, 1), (5, 0, 2), (5, 1, 3)], plans, both,
        [zero_own, zero_other, one_own, one_other], None, row_count, "turned", {}, (0, 2),
    )
    received, third, staged = lax.optimization_barrier((received, third, staged))
    level_two = half_solve(0, received, right_top, factor_top, None)
    two_own = sibling_values(level_two, 0)

    resident = {(0, 2): staged}
    third, resident[(1, 2)] = update(
        [(6, 0, 0), (6, 1, 0)], plans, both, [[level_two] * cols], third, row_count, "summed",
        resident, (1, 2),
    )
    send = update(
        [(7, 0, 0), (7, 1, 0)], plans, both, [two_own], third, row_count, "rest", resident, None
    )
    send, level_zero, level_one = lax.optimization_barrier((send, level_zero, level_one))
    halves = half_solve(1, exchange(send), right_top, factor_top, level_two)
    solved_top = join_halves(halves, from_other_core(halves))
    solved_sub = jnp.stack([level_zero, level_one])[None, None, None]
    return (solved_sub, solved_top)


def solution(mesh):
    in_specs = (
        P("prow", "pcol", "zgrid", None, None, None, None),
        P("prow", "pcol", "zgrid", None, None),
        P("prow", "pcol", "zgrid", None, None),
        P("prow", "pcol", "zgrid", None),
        P("prow", "pcol", "zgrid", None, None, None),
        P("prow", "pcol", None, None, None),
        P("prow", "pcol", "zgrid", None, None, None),
        P("prow", "pcol", None, None, None),
    )
    out_specs = (P("prow", "pcol", "zgrid", None, None, None), P("prow", "pcol", None, None, None))
    return jax.shard_map(local, mesh=mesh, in_specs=in_specs, out_specs=out_specs, check_vma=False)
```
